32 devices in a mesh: polar: 4 (over x, core), azimuth: 8 (over z, y).
Axes of the slice: x: 2, y: 2, z: 4, core: 2. Of those that a mesh axis runs over, the one named last changes fastest.
Arguments:
- field: float32 [1, 128, 192, 384], P(None, 'polar', 'azimuth'), may hold values from -6 to 6
- filter_real: float32 [64, 384, 384], P('azimuth'), may hold values from -0.3125 to 0.3125
- filter_imag: float32 [64, 384, 384], P('azimuth'), may hold values from -0.3125 to 0.3125
- norm_gain: float32 [384], replicated, may hold values from 0.1 to 1.9
- w_in: bfloat16 [384, 768], replicated, may hold values from -0.3125 to 0.3125
- w_out: bfloat16 [768, 384], replicated, may hold values from -0.21875 to 0.21875
Outputs:
- mixed: float32 [1, 64, 96, 384], P(None, 'polar', 'azimuth')
The draws below stay inside these ranges and needn't reach their ends.
All inputs are finite; a program needn't handle non-finite values.
Results may differ from the reference program's by a relative error of at most 0.0035.
Values sent between devices are 32-bit elements; how exact they have to be, the bound alone decides.
No kernel may reach another device: no remote copies, remote signals or barrier semaphores. Data moves between devices by JAX's collectives and lax.ppermute only.
A program may use at most 128 MiB of HBM per device.

```python
import math
import jax
import jax.numpy as jnp
from jax import lax

C = 384
H = 768
B = 1
NLAT = 128
NLON = 192
NLATC = 64
NLONC = 96
LMAX = 64
MMAX = 48


def steps_of(own_key, extent, cuts, least, top_value):
    def one(dim, shards_of):
        heights = jax.random.uniform(jax.random.fold_in(jax.random.fold_in(own_key, 6), dim), (shards_of,), jnp.float32, least / len(cuts), top_value / len(cuts))
        return jnp.repeat(jnp.exp(heights), extent[dim] // shards_of).reshape((-1,) + (1,) * (len(extent) - dim - 1))

    level = one(*cuts[0])
    for cut in cuts[1:]:
        level = level * one(*cut)
    return level


def normal_values(stream_key, shape, scale, most, cuts=(), kind=jnp.bfloat16):
    entries = jax.random.normal(stream_key, shape, jnp.float32) * scale
    if len(cuts) > 0:
        entries = steps_of(stream_key, shape, cuts, -0.22, 0.18) * entries
    return jnp.clip(entries, min=-most, max=most).astype(kind)


def setup_inputs(seed: int = 0) -> dict:
    splits = jax.random.split(jax.random.key(seed), 7)
    field = normal_values(splits[0], (B, NLAT, NLON, C), 1.0, 6.0, ((1, 4), (2, 8)), jnp.float32)
    filter_real = normal_values(splits[1], (LMAX, C, C), C ** -0.5, 0.3125, ((0, 8),), jnp.float32)
    filter_imag = normal_values(splits[2], (LMAX, C, C), C ** -0.5, 0.3125, ((0, 8),), jnp.float32)
    norm_gain = jnp.clip(1.0 + 0.18 * jax.random.normal(splits[3], (C,), jnp.float32), 0.1, 1.9)
    w_in = normal_values(splits[4], (C, H), C ** -0.5, 0.3125)
    w_out = normal_values(splits[5], (H, C), H ** -0.5, 0.21875)
    return {"field": field, "filter_real": filter_real, "filter_imag": filter_imag, "norm_gain": norm_gain, "w_in": w_in, "w_out": w_out}


def legendre(modes, cosines, sines, degrees, mode_bound):
    mode_col = modes[:, None]
    counter = jnp.arange(1, mode_bound + 1, dtype=jnp.float32)
    ratios = jnp.log((2.0 * counter - 1.0) / (2.0 * counter))
    product_log = lax.optimization_barrier(jnp.sum(jnp.where(counter[None, :] <= mode_col, ratios[None, :], 0.0), axis=1, keepdims=True))
    log_diag = 0.5 * (jnp.log((2.0 * mode_col + 1.0) / (4.0 * math.pi)) + product_log) + mode_col * jnp.log(sines)[None, :]
    diagonal = jnp.exp(log_diag)
    nodes = cosines[None, :]

    def advance(state, degree):
        newest, older = state
        lower = jnp.where(degree > mode_col, degree * degree - mode_col * mode_col, 1.0)
        factor_a = jnp.sqrt((4.0 * degree * degree - 1.0) / lower)
        factor_b = jnp.sqrt(jnp.maximum((degree - 1.0) ** 2 - mode_col ** 2, 0.0) / jnp.maximum(4.0 * (degree - 1.0) ** 2 - 1.0, 1.0))
        recurred = factor_a * (nodes * newest - factor_b * older)
        second = jnp.sqrt(2.0 * mode_col + 3.0) * nodes * newest
        value = jnp.where(degree == mode_col, diagonal, jnp.where(degree == mode_col + 1.0, second, jnp.where(degree > mode_col + 1.0, recurred, 0.0)))
        return ((value, newest), value)
    zeros_state = jnp.zeros_like(diagonal)
    _, stacked = lax.scan(advance, (zeros_state, zeros_state), jnp.arange(degrees, dtype=jnp.float32))
    return jnp.transpose(stacked, (1, 0, 2))

def latitudes(count):
    theta = math.pi * (jnp.arange(count).astype(jnp.float32) + 0.5) / count
    return (jnp.cos(theta), jnp.sin(theta))

def trig_tables(points, mode_ids):
    phase = jnp.arange(points, dtype=jnp.int32)[:, None] * mode_ids[None, :] % points
    angle = 2.0 * math.pi / points * phase.astype(jnp.float32)
    return (jnp.cos(angle), jnp.sin(angle))

def reference(field, filter_real, filter_imag, norm_gain, w_in, w_out):
    high = lax.Precision.HIGHEST
    mode_ids = jnp.arange(MMAX, dtype=jnp.int32)
    modes = mode_ids.astype(jnp.float32)
    cos_fine, sin_fine = latitudes(NLAT)
    quadrature = math.pi / NLAT * sin_fine * (2.0 * math.pi / NLON)
    table_fine = legendre(modes, cos_fine, sin_fine, LMAX, MMAX) * quadrature[None, None, :]
    cos_coarse, sin_coarse = latitudes(NLATC)
    table_coarse = legendre(modes, cos_coarse, sin_coarse, LMAX, MMAX)
    fwd_cos, fwd_sin = trig_tables(NLON, mode_ids)
    inv_cos, inv_sin = trig_tables(NLONC, mode_ids)
    weights = jnp.where(mode_ids == 0, 1.0, 2.0).astype(jnp.float32)
    inv_cos = (inv_cos * weights[None, :]).T
    inv_sin = (-inv_sin * weights[None, :]).T

    def synthesis(spec_re, spec_im):
        grid_re = jnp.einsum('mli,lmc->imc', table_coarse, spec_re, precision=high)
        grid_im = jnp.einsum('mli,lmc->imc', table_coarse, spec_im, precision=high)
        return jnp.einsum('imc,mj->ijc', grid_re, inv_cos, precision=high) + jnp.einsum('imc,mj->ijc', grid_im, inv_sin, precision=high)

    def single(sample_field):
        four_re = jnp.einsum('ijc,jm->imc', sample_field, fwd_cos, precision=high)
        four_im = -jnp.einsum('ijc,jm->imc', sample_field, fwd_sin, precision=high)
        coef_re = jnp.einsum('mli,imc->lmc', table_fine, four_re, precision=high)
        coef_im = jnp.einsum('mli,imc->lmc', table_fine, four_im, precision=high)
        filt_re = jnp.einsum('lco,lmc->lmo', filter_real, coef_re, precision=high) - jnp.einsum('lco,lmc->lmo', filter_imag, coef_im, precision=high)
        filt_im = jnp.einsum('lco,lmc->lmo', filter_real, coef_im, precision=high) + jnp.einsum('lco,lmc->lmo', filter_imag, coef_re, precision=high)
        skip = synthesis(coef_re, coef_im)
        branch = synthesis(filt_re, filt_im)
        state = jax.nn.gelu(branch, approximate=False) + skip
        center = lax.optimization_barrier(jnp.mean(state, axis=-1, keepdims=True))
        spread = lax.optimization_barrier(jnp.mean((state - center) ** 2, axis=-1, keepdims=True))
        normed = ((state - center) * lax.rsqrt(spread + 1e-05) * norm_gain).astype(jnp.bfloat16)
        flat = normed.reshape(-1, normed.shape[-1])
        hidden = jax.nn.gelu(jnp.dot(flat, w_in, preferred_element_type=jnp.float32), approximate=False).astype(jnp.bfloat16)
        update = jnp.dot(hidden, w_out, preferred_element_type=jnp.float32)
        return state + update.reshape(state.shape)
    return lax.map(single, field)
```

```python
import math

import jax
import jax.numpy as jnp
import numpy as np
from jax import lax
from jax.sharding import PartitionSpec as P


def legendre(nodes, degrees, orders):
    cosines, sines = np.cos(nodes)[None, :], np.sin(nodes)[None, :]
    mode = np.arange(orders, dtype=np.float64)[:, None]
    counter = np.arange(1, orders + 1, dtype=np.float64)
    ratios = np.log((2.0 * counter - 1.0) / (2.0 * counter))
    product_log = np.concatenate([[0.0], np.cumsum(ratios)])[:orders, None]
    diagonal = np.exp(
        0.5 * (np.log((2.0 * mode + 1.0) / (4.0 * math.pi)) + product_log) + mode * np.log(sines)
    )
    newest, older = np.zeros_like(diagonal), np.zeros_like(diagonal)
    stacked = []
    for degree in range(degrees):
        lower = np.where(degree > mode, degree * degree - mode * mode, 1.0)
        factor_a = np.sqrt(max(4.0 * degree * degree - 1.0, 0.0) / lower)
        factor_b = np.sqrt(
            np.maximum((degree - 1.0) ** 2 - mode**2, 0.0) / max(4.0 * (degree - 1.0) ** 2 - 1.0, 1.0)
        )
        recurred = factor_a * (cosines * newest - factor_b * older)
        second = np.sqrt(2.0 * mode + 3.0) * cosines * newest
        value = np.where(
            degree == mode,
            diagonal,
            np.where(degree == mode + 1.0, second, np.where(degree > mode + 1.0, recurred, 0.0)),
        )
        stacked.append(value)
        newest, older = value, newest
    return np.stack(stacked, axis=1)


def colatitudes(count):
    return math.pi * (np.arange(count) + 0.5) / count


def fourier_table(points, mode_ids, halves, weights):
    angle = 2.0 * math.pi / points * (np.arange(points)[:, None] * mode_ids[None, :] % points)
    return np.where(
        halves[None, :] == 0, weights[None, :] * np.cos(angle), -weights[None, :] * np.sin(angle)
    )


def per_device(field, filter_real, filter_imag, norm_gain, w_in, w_out):
    high = lax.Precision.HIGHEST
    samples, lat_rows, lon_cols, channels = field.shape
    polar_count = lax.axis_size("polar")
    azimuth_count = lax.axis_size("azimuth")
    fine_lat = lat_rows * polar_count
    fine_lon = lon_cols * azimuth_count
    coarse_lat = fine_lat // 2
    coarse_lon = fine_lon // 2
    orders = coarse_lon // 2
    order_piece = orders // polar_count
    chan_slice = channels // azimuth_count
    columns_all = np.arange(2 * orders)
    halves = columns_all // order_piece % 2
    mode_ids = columns_all // (2 * order_piece) * order_piece + columns_all % order_piece
    twofold = np.where(mode_ids == 0, 1.0, 2.0)
    forward_table = jnp.asarray(
        fourier_table(fine_lon, mode_ids, halves, np.ones(2 * orders)), jnp.float32
    )
    inverse_table = jnp.asarray(fourier_table(coarse_lon, mode_ids, halves, twofold).T, jnp.float32)
    polar_index = lax.axis_index("polar")
    fine_nodes = colatitudes(fine_lat)
    quadrature = math.pi / fine_lat * np.sin(fine_nodes) * (2.0 * math.pi / fine_lon)
    all_fine = legendre(fine_nodes, coarse_lat, orders) * quadrature
    all_coarse = legendre(colatitudes(coarse_lat), coarse_lat, orders)
    own_orders = lambda table: lax.dynamic_slice_in_dim(
        jnp.asarray(table, jnp.float32), polar_index * order_piece, order_piece, 0
    )
    table_fine = own_orders(all_fine)
    table_coarse = own_orders(all_coarse)
    moved = lax.all_to_all(field, "azimuth", split_axis=3, concat_axis=2, tiled=True)
    spectrum = jnp.einsum("bijc,jk->bick", moved, forward_table, precision=high)
    by_order = lax.all_to_all(spectrum, "polar", split_axis=3, concat_axis=1, tiled=True)
    by_order = by_order.reshape(samples, fine_lat, chan_slice, 2, order_piece)
    coef = jnp.einsum("kli,bicpk->blcpk", table_fine, by_order, precision=high)
    degree_block = lax.all_to_all(coef, "azimuth", split_axis=1, concat_axis=2, tiled=True)
    block_re = degree_block[:, :, :, 0]
    block_im = degree_block[:, :, :, 1]
    out_re = jnp.einsum("lco,blck->blok", filter_real, block_re, precision=high) - jnp.einsum(
        "lco,blck->blok", filter_imag, block_im, precision=high
    )
    out_im = jnp.einsum("lco,blck->blok", filter_real, block_im, precision=high) + jnp.einsum(
        "lco,blck->blok", filter_imag, block_re, precision=high
    )
    mixed_spec = jnp.stack([out_re, out_im], axis=3)
    filtered = lax.all_to_all(mixed_spec, "azimuth", split_axis=2, concat_axis=1, tiled=True)
    both_fields = jnp.concatenate([coef, filtered], axis=2)
    grid_modes = jnp.einsum("kli,blcpk->bicpk", table_coarse, both_fields, precision=high)
    grid_modes = grid_modes.reshape(samples, coarse_lat, 2 * chan_slice, 2 * order_piece)
    row_block = lax.all_to_all(grid_modes, "polar", split_axis=1, concat_axis=3, tiled=True)
    values = jnp.einsum("bick,kj->bijc", row_block, inverse_table, precision=high)
    state_split = (
        jax.nn.gelu(values[..., chan_slice:], approximate=False) + values[..., :chan_slice]
    )
    state = lax.all_to_all(state_split, "azimuth", split_axis=2, concat_axis=3, tiled=True)
    center = jnp.mean(state, axis=-1, keepdims=True)
    spread = jnp.mean((state - center) ** 2, axis=-1, keepdims=True)
    normed = ((state - center) * lax.rsqrt(spread + 1e-05) * norm_gain).astype(jnp.bfloat16)
    flat = normed.reshape(-1, channels)
    hidden = jax.nn.gelu(
        jnp.dot(flat, w_in, preferred_element_type=jnp.float32), approximate=False
    ).astype(jnp.bfloat16)
    update = jnp.dot(hidden, w_out, preferred_element_type=jnp.float32)
    return state + update.reshape(state.shape)


def solution(mesh):
    in_specs = (
        P(None, "polar", "azimuth", None),
        P("azimuth", None, None),
        P("azimuth", None, None),
        P(),
        P(),
        P(),
    )
    out_specs = P(None, "polar", "azimuth", None)
    return jax.shard_map(
        per_device, mesh=mesh, in_specs=in_specs, out_specs=out_specs, check_vma=False
    )
```

```python
import functools
import math

import jax
import jax.numpy as jnp
import numpy as np
from jax import lax
from jax.experimental import pallas as pl
from jax.experimental.pallas import tpu as pltpu
from jax.sharding import PartitionSpec as P


def legendre(nodes, degrees, orders):
    cosines, sines = np.cos(nodes)[None, :], np.sin(nodes)[None, :]
    mode = np.arange(orders, dtype=np.float64)[:, None]
    counter = np.arange(1, orders + 1, dtype=np.float64)
    ratios = np.log((2.0 * counter - 1.0) / (2.0 * counter))
    product_log = np.concatenate([[0.0], np.cumsum(ratios)])[:orders, None]
    diagonal = np.exp(
        0.5 * (np.log((2.0 * mode + 1.0) / (4.0 * math.pi)) + product_log) + mode * np.log(sines)
    )
    newest, older = np.zeros_like(diagonal), np.zeros_like(diagonal)
    stacked = []
    for degree in range(degrees):
        lower = np.where(degree > mode, degree * degree - mode * mode, 1.0)
        factor_a = np.sqrt(max(4.0 * degree * degree - 1.0, 0.0) / lower)
        factor_b = np.sqrt(
            np.maximum((degree - 1.0) ** 2 - mode**2, 0.0) / max(4.0 * (degree - 1.0) ** 2 - 1.0, 1.0)
        )
        recurred = factor_a * (cosines * newest - factor_b * older)
        second = np.sqrt(2.0 * mode + 3.0) * cosines * newest
        value = np.where(
            degree == mode,
            diagonal,
            np.where(degree == mode + 1.0, second, np.where(degree > mode + 1.0, recurred, 0.0)),
        )
        stacked.append(value)
        newest, older = value, newest
    return np.stack(stacked, axis=1)


def colatitudes(count):
    return math.pi * (np.arange(count) + 0.5) / count


def fourier_table(points, mode_ids, halves, weights):
    angle = 2.0 * math.pi / points * (np.arange(points)[:, None] * mode_ids[None, :] % points)
    return np.where(
        halves[None, :] == 0, weights[None, :] * np.cos(angle), -weights[None, :] * np.sin(angle)
    )


def by_axes(field, filter_real, filter_imag, norm_gain, w_in, w_out):
    high = lax.Precision.HIGHEST
    samples, lat_rows, lon_cols, channels = field.shape
    polar_count = lax.axis_size("polar")
    azimuth_count = lax.axis_size("azimuth")
    fine_lat = lat_rows * polar_count
    fine_lon = lon_cols * azimuth_count
    coarse_lat = fine_lat // 2
    coarse_lon = fine_lon // 2
    orders = coarse_lon // 2
    order_piece = orders // polar_count
    chan_slice = channels // azimuth_count
    columns_all = np.arange(2 * orders)
    halves = columns_all // order_piece % 2
    mode_ids = columns_all // (2 * order_piece) * order_piece + columns_all % order_piece
    twofold = np.where(mode_ids == 0, 1.0, 2.0)
    forward_table = jnp.asarray(
        fourier_table(fine_lon, mode_ids, halves, np.ones(2 * orders)), jnp.float32
    )
    inverse_table = jnp.asarray(fourier_table(coarse_lon, mode_ids, halves, twofold).T, jnp.float32)
    polar_index = lax.axis_index("polar")
    fine_nodes = colatitudes(fine_lat)
    quadrature = math.pi / fine_lat * np.sin(fine_nodes) * (2.0 * math.pi / fine_lon)
    all_fine = legendre(fine_nodes, coarse_lat, orders) * quadrature
    all_coarse = legendre(colatitudes(coarse_lat), coarse_lat, orders)
    own_orders = lambda table: lax.dynamic_slice_in_dim(
        jnp.asarray(table, jnp.float32), polar_index * order_piece, order_piece, 0
    )
    table_fine = own_orders(all_fine)
    table_coarse = own_orders(all_coarse)
    moved = lax.all_to_all(field, "azimuth", split_axis=3, concat_axis=2, tiled=True)
    spectrum = jnp.einsum("bijc,jk->bick", moved, forward_table, precision=high)
    by_order = lax.all_to_all(spectrum, "polar", split_axis=3, concat_axis=1, tiled=True)
    by_order = by_order.reshape(samples, fine_lat, chan_slice, 2, order_piece)
    coef = jnp.einsum("kli,bicpk->blcpk", table_fine, by_order, precision=high)
    degree_block = lax.all_to_all(coef, "azimuth", split_axis=1, concat_axis=2, tiled=True)
    block_re = degree_block[:, :, :, 0]
    block_im = degree_block[:, :, :, 1]
    out_re = jnp.einsum("lco,blck->blok", filter_real, block_re, precision=high) - jnp.einsum(
        "lco,blck->blok", filter_imag, block_im, precision=high
    )
    out_im = jnp.einsum("lco,blck->blok", filter_real, block_im, precision=high) + jnp.einsum(
        "lco,blck->blok", filter_imag, block_re, precision=high
    )
    mixed_spec = jnp.stack([out_re, out_im], axis=3)
    filtered = lax.all_to_all(mixed_spec, "azimuth", split_axis=2, concat_axis=1, tiled=True)
    both_fields = jnp.concatenate([coef, filtered], axis=2)
    grid_modes = jnp.einsum("kli,blcpk->bicpk", table_coarse, both_fields, precision=high)
    grid_modes = grid_modes.reshape(samples, coarse_lat, 2 * chan_slice, 2 * order_piece)
    row_block = lax.all_to_all(grid_modes, "polar", split_axis=1, concat_axis=3, tiled=True)
    values = jnp.einsum("bick,kj->bijc", row_block, inverse_table, precision=high)
    state_split = (
        jax.nn.gelu(values[..., chan_slice:], approximate=False) + values[..., :chan_slice]
    )
    state = lax.all_to_all(state_split, "azimuth", split_axis=2, concat_axis=3, tiled=True)
    center = jnp.mean(state, axis=-1, keepdims=True)
    spread = jnp.mean((state - center) ** 2, axis=-1, keepdims=True)
    normed = ((state - center) * lax.rsqrt(spread + 1e-05) * norm_gain).astype(jnp.bfloat16)
    flat = normed.reshape(-1, channels)
    hidden = jax.nn.gelu(
        jnp.dot(flat, w_in, preferred_element_type=jnp.float32), approximate=False
    ).astype(jnp.bfloat16)
    update = jnp.dot(hidden, w_out, preferred_element_type=jnp.float32)
    return state + update.reshape(state.shape)


LANES = 128
BOTH = ("polar", "azimuth")
MIB = 1024 * 1024


def split_bf16(table):
    high = table.astype(jnp.bfloat16)
    return high, (table - high.astype(jnp.float32)).astype(jnp.bfloat16)


def split_constant(table):
    table = np.asarray(table, np.float32)
    high = table.astype(jnp.bfloat16)
    return jnp.asarray(high), jnp.asarray((table - high.astype(np.float32)).astype(jnp.bfloat16))


def dot(left, right):
    return jnp.dot(left, right, preferred_element_type=jnp.float32)


def dot3(left, right_high, right_low):
    rows = left.shape[0]
    left_high, left_low = split_bf16(left)
    both = dot(jnp.concatenate([left_high, left_low], axis=0), right_high)
    return both[:rows] + both[rows:] + dot(left_high, right_low)


def swap(blocks, bits):
    lane = lax.broadcasted_iota(jnp.int32, blocks[0].shape, len(blocks[0].shape) - 1)
    axis = len(blocks[0].shape) - 1
    blocks = list(blocks)
    for order, bit in enumerate(bits):
        step = 1 << bit
        keep = (lane & step) == 0
        for index in range(len(blocks)):
            if index >> order & 1:
                continue
            first, second = blocks[index], blocks[index | 1 << order]
            blocks[index] = jnp.where(keep, first, pltpu.roll(second, step, axis))
            blocks[index | 1 << order] = jnp.where(
                keep, pltpu.roll(first, LANES - step, axis), second
            )
    return blocks


OWNER_BITS = (0, 1, 2, 3, 6)
QUAD_BITS = (4, 5)
LOW_BITS = (0, 1, 2, 3, 4)


def gelu(values):
    return 0.5 * values * (1.0 + lax.erf(values * math.sqrt(0.5)))


def scatter_kernel(field, sent):
    devices, rows, channels = sent.shape
    for tile in range(channels // LANES):
        lanes = pl.ds(tile * LANES, LANES)
        blocks = swap([field[0, lat, :, lanes] for lat in range(devices)], OWNER_BITS)
        for device in range(devices):
            sent[device, :, lanes] = blocks[device]


def analysis_kernel(
    polar_count, got, four_high, four_low, leg_high, leg_low, coef, sent, rows, high_buf, low_buf, sems
):
    copies = [
        pltpu.make_async_copy(leg_high, high_buf, sems.at[0]),
        pltpu.make_async_copy(leg_low, low_buf, sems.at[1]),
    ]
    for copy in copies:
        copy.start()
    devices, lon_cols, width = got.shape
    azimuth_count = devices // polar_count
    modes = four_high.shape[0]
    orders = modes // 2
    four = jnp.concatenate([four_high[...], four_low[...]], axis=0)
    tiles = width // LANES
    for tile in range(tiles):
        spectra = []
        for polar in range(polar_count):
            block = got[pl.ds(polar * azimuth_count, azimuth_count), :, pl.ds(tile * LANES, LANES)]
            block = block.reshape(azimuth_count * lon_cols, LANES)
            block_high, block_low = split_bf16(block)
            both = dot(four, block_high)
            spectra.append(both[:modes] + both[modes:] + dot(four[:modes], block_low))
        for quad, spectrum in enumerate(swap(spectra, QUAD_BITS)):
            rows[pl.ds((tile * polar_count + quad) * modes, modes), :] = spectrum
    for copy in copies:
        copy.wait()
    pairs = orders // 2
    count = 2 * tiles * polar_count
    for pair in range(pairs):
        first = rows[pl.ds(pair, count, stride=orders), :]
        second = rows[pl.ds(pairs + pair, count, stride=orders), :]
        coef[pair] = dot3(jnp.concatenate([first, second], axis=1), high_buf[pair], low_buf[pair])
    pack_by_degree(coef, sent)


def pack_by_degree(coef, sent):
    devices, count, _ = sent.shape
    pairs = coef.shape[0]
    for row in range(0, count, 8):
        part = pl.ds(row, 8)
        zero = jnp.zeros((8, LANES), jnp.float32)
        blocks = swap(
            [coef[pair, part, :] if pair < pairs else zero for pair in range(devices)], LOW_BITS
        )
        for device in range(devices):
            sent[device, part, :] = blocks[device]


def filter_kernel(first_degree, got, real, imag, sent, real_buf, imag_buf, turned, sems):
    degrees, channels, _ = real_buf.shape
    start = first_degree[0]
    copies = []
    for degree in range(degrees):
        pair = [
            pltpu.make_async_copy(real.at[start + degree], real_buf.at[degree], sems.at[0, degree]),
            pltpu.make_async_copy(imag.at[start + degree], imag_buf.at[degree], sems.at[1, degree]),
        ]
        for copy in pair:
            copy.start()
        copies.append(pair)
    devices, count, _ = sent.shape
    tiles = channels // LANES
    groups = [
        (tile, top, quad) for tile in range(tiles) for top in range(2) for quad in range(4)
    ]
    spectra = []
    for half in range(2):
        parts = [
            got[pl.ds(top * 16 * count + 2 * (4 * tile + quad) + half, 16, stride=count), :]
            for tile, top, quad in groups
        ]
        spectra.append(jnp.concatenate(parts, axis=0).T)
    pad = LANES // (2 * degrees)
    results = [[None] * (2 * degrees) for _ in range(2)]
    for degree in range(degrees):
        for copy in copies[degree]:
            copy.wait()
        own = jnp.concatenate(
            [
                spectra[half][(order * degrees + degree) * pad : (order * degrees + degree + 1) * pad]
                for half in range(2)
                for order in range(2)
            ],
            axis=0,
        )
        by_real = dot3(own, *split_bf16(real_buf[degree]))
        by_imag = dot3(own, *split_bf16(imag_buf[degree]))
        size = 2 * pad
        out_re = by_real[:size] - by_imag[size:]
        out_im = by_real[size:] + by_imag[:size]
        for order in range(2):
            results[0][order * degrees + degree] = out_re[order * pad : (order + 1) * pad]
            results[1][order * degrees + degree] = out_im[order * pad : (order + 1) * pad]
    for half in range(2):
        across = jnp.concatenate(results[half], axis=0).T
        for place, (tile, top, quad) in enumerate(groups):
            turned[pl.ds(((top * tiles * 4 + 4 * tile + quad) * 2 + half) * 16, 16), :] = across[
                place * 16 : (place + 1) * 16
            ]
    for device in range(devices):
        sent[device] = turned[pl.ds(device // 16 * 16 * count + device % 16, count, stride=16), :]


def synthesis_kernel(
    polar_count, got, coef, four_high, four_low, leg_high, leg_low, sent, back, modes_buf,
    high_buf, low_buf, sems
):
    copies = [
        pltpu.make_async_copy(leg_high, high_buf, sems.at[0]),
        pltpu.make_async_copy(leg_low, low_buf, sems.at[1]),
    ]
    for copy in copies:
        copy.start()
    devices, count, _ = got.shape
    azimuth_count = devices // polar_count
    pairs = coef.shape[0]
    orders = 2 * pairs
    for row in range(0, count, 8):
        part = pl.ds(row, 8)
        blocks = swap([got[device, part, :] for device in range(devices)], LOW_BITS)
        for pair in range(pairs):
            back[pair, part, :] = blocks[pair]
    for copy in copies:
        copy.wait()
    keep = (lax.broadcasted_iota(jnp.int32, (count, LANES), 1) & 64) == 0
    for pair in range(pairs):
        both = jnp.concatenate([coef[pair], back[pair]], axis=0)
        values = dot3(both, high_buf[pair], low_buf[pair])
        for order in range(2):
            lanes = slice(order * LANES, (order + 1) * LANES)
            modes_buf[pl.ds((order * pairs + pair) * count, count), :] = jnp.where(
                keep, values[:count, lanes], values[count:, lanes]
            )
    four = jnp.concatenate([four_high[...], four_low[...]], axis=0)
    points = four_high.shape[0]
    half = points // 2
    keep = (lax.broadcasted_iota(jnp.int32, (half, LANES), 1) & 64) == 0
    for tile in range(count // 8):
        states = []
        for quad in range(4):
            row = 2 * (4 * tile + quad)
            modes = jnp.concatenate(
                [modes_buf[pl.ds(row + part, orders, stride=count), :] for part in range(2)], axis=0
            )
            modes_high, modes_low = split_bf16(modes)
            both = dot(four, modes_high)
            values = both[:points] + both[points:] + dot(four[:points], modes_low)
            first, second = values[:half], values[half:]
            skip = jnp.where(keep, first, pltpu.roll(second, 64, 1))
            branch = jnp.where(keep, pltpu.roll(first, 64, 1), second)
            states.append(gelu(branch) + skip)
        for polar, state in enumerate(swap(states, QUAD_BITS)):
            for azimuth in range(azimuth_count):
                sent[polar * azimuth_count + azimuth, pl.ds(8 * tile, 8), :] = state[
                    8 * azimuth : 8 * azimuth + 8
                ]


def mlp_kernel(got, gain, w_in, w_out, mixed, state):
    devices, count, _ = got.shape
    tiles = count // 8
    for tile in range(tiles):
        blocks = swap([got[device, pl.ds(8 * tile, 8), :] for device in range(devices)], OWNER_BITS)
        for device in range(devices):
            state[pl.ds(8 * device, 8), pl.ds(tile * LANES, LANES)] = blocks[device]
    value = state[...]
    center = jnp.mean(value, axis=-1, keepdims=True)
    spread = jnp.mean((value - center) ** 2, axis=-1, keepdims=True)
    normed = ((value - center) * lax.rsqrt(spread + 1e-05) * gain[...]).astype(jnp.bfloat16)
    hidden = gelu(dot(normed, w_in[...])).astype(jnp.bfloat16)
    state[...] = value + dot(hidden, w_out[...])
    _, lat_rows, lon_cols, _ = mixed.shape
    part = lon_cols // 2
    for top in range(2):
        for lat in range(lat_rows):
            row = 8 * (top * lat_rows + lat)
            mixed[0, lat, pl.ds(top * part, part), :] = state[pl.ds(row, part), :]


def joint_fits(field, filter_real, polar_count, azimuth_count):
    samples, lat_rows, lon_cols, channels = field.shape
    devices = polar_count * azimuth_count
    orders = lon_cols * azimuth_count // 4
    return (
        samples == 1
        and devices == 32
        and polar_count == 4
        and lat_rows == 32
        and lon_cols % 8 == 0
        and lon_cols // 4 <= 8
        and channels % LANES == 0
        and filter_real.shape[0] == 2 * polar_count
        and orders % 16 == 0
        and orders // 2 <= 32
    )


def jointly(field, filter_real, filter_imag, norm_gain, w_in, w_out):
    _, lat_rows, lon_cols, channels = field.shape
    polar_count = lax.axis_size("polar")
    azimuth_count = lax.axis_size("azimuth")
    devices = polar_count * azimuth_count
    fine_lat, fine_lon = lat_rows * polar_count, lon_cols * azimuth_count
    coarse_lat, coarse_lon = fine_lat // 2, fine_lon // 2
    orders = coarse_lon // 2
    pairs = orders // 2
    tiles = channels // LANES
    count = 2 * channels // devices
    degrees_here = coarse_lat // devices
    lat_out, lon_out = coarse_lat // polar_count, coarse_lon // azimuth_count

    mode_ids = np.tile(np.arange(orders), 2)
    halves = np.repeat(np.arange(2), orders)
    forward = fourier_table(fine_lon, mode_ids, halves, np.ones(2 * orders)).T
    twofold = np.where(mode_ids == 0, 1.0, 2.0)
    inverse = fourier_table(coarse_lon, mode_ids, halves, twofold)
    backward = np.zeros((2, azimuth_count, 8, 2 * orders))
    backward[:, :, : lon_out // 2] = inverse.reshape(
        azimuth_count, 2, lon_out // 2, 2 * orders
    ).transpose(1, 0, 2, 3)
    backward = backward.reshape(-1, 2 * orders)

    fine_nodes = colatitudes(fine_lat)
    quadrature = math.pi / fine_lat * np.sin(fine_nodes) * (2.0 * math.pi / fine_lon)
    fine = legendre(fine_nodes, coarse_lat, orders) * quadrature
    coarse = legendre(colatitudes(coarse_lat), coarse_lat, orders)
    owner = np.arange(devices)
    degree = (
        owner % azimuth_count * (coarse_lat // azimuth_count) + owner // azimuth_count * degrees_here
    )
    degree = (degree[None, :] + np.arange(degrees_here)[:, None]).reshape(-1)
    lane = np.arange(LANES)
    lat_fine = (lane >> 4 & 3) * lat_rows + (lane >> 6) * 16 + (lane & 15)
    lat_coarse = (lane >> 4 & 3) * lat_out + (lane & 15)
    fine = fine[:, degree][:, :, lat_fine].transpose(0, 2, 1)
    coarse = coarse[:, degree][:, :, lat_coarse]
    size = degree.shape[0]
    analyse = np.zeros((pairs, 2, LANES, 2, size))
    synthesise = np.zeros((pairs, 2, size, 2, LANES))
    for order in range(2):
        analyse[:, order, :, order, :] = fine[order * pairs : (order + 1) * pairs]
        synthesise[:, order, :, order, :] = coarse[order * pairs : (order + 1) * pairs]
    analyse = analyse.reshape(pairs, 2 * LANES, 2 * size)
    synthesise = synthesise.reshape(pairs, 2 * size, 2 * LANES)

    vmem = pl.BlockSpec(memory_space=pltpu.VMEM)
    anywhere = pl.BlockSpec(memory_space=pl.ANY)
    block = jax.ShapeDtypeStruct((devices, count, LANES), jnp.float32)
    exchange = functools.partial(
        lax.all_to_all, axis_name=BOTH, split_axis=0, concat_axis=0, tiled=True
    )

    sent = pl.pallas_call(
        scatter_kernel,
        grid=(lon_cols // 8,),
        in_specs=[pl.BlockSpec((1, lat_rows, 8, channels), lambda step: (0, 0, step, 0))],
        out_specs=pl.BlockSpec((devices, 8, channels), lambda step: (0, step, 0)),
        out_shape=jax.ShapeDtypeStruct((devices, lon_cols, channels), jnp.float32),
        compiler_params=pltpu.CompilerParams(vmem_limit_bytes=8 * MIB),
        name="scatter_channels",
    )(field)
    got = exchange(sent)
    table_buf = pltpu.VMEM(analyse.shape, jnp.bfloat16)
    coef, sent = pl.pallas_call(
        functools.partial(analysis_kernel, polar_count),
        in_specs=[vmem, vmem, vmem, anywhere, anywhere],
        out_specs=[vmem, vmem],
        out_shape=[jax.ShapeDtypeStruct((pairs, count, LANES), jnp.float32), block],
        scratch_shapes=[
            pltpu.VMEM((count * orders, LANES), jnp.float32),
            table_buf,
            table_buf,
            pltpu.SemaphoreType.DMA((2,)),
        ],
        compiler_params=pltpu.CompilerParams(vmem_limit_bytes=16 * MIB),
        name="analysis",
    )(got, *split_constant(forward), *split_constant(analyse))
    got = exchange(sent)
    first_degree = (lax.axis_index("polar") * degrees_here).astype(jnp.int32).reshape(1)
    sent = pl.pallas_call(
        filter_kernel,
        in_specs=[pl.BlockSpec(memory_space=pltpu.SMEM), vmem, anywhere, anywhere],
        out_specs=vmem,
        out_shape=block,
        scratch_shapes=[
            pltpu.VMEM((degrees_here, channels, channels), jnp.float32),
            pltpu.VMEM((degrees_here, channels, channels), jnp.float32),
            pltpu.VMEM((2 * channels, LANES), jnp.float32),
            pltpu.SemaphoreType.DMA((2, degrees_here)),
        ],
        compiler_params=pltpu.CompilerParams(vmem_limit_bytes=16 * MIB),
        name="channel_filter",
    )(first_degree, got.reshape(devices * count, LANES), filter_real, filter_imag)
    got = exchange(sent)
    table_buf = pltpu.VMEM(synthesise.shape, jnp.bfloat16)
    sent = pl.pallas_call(
        functools.partial(synthesis_kernel, polar_count),
        in_specs=[vmem, vmem, vmem, vmem, anywhere, anywhere],
        out_specs=vmem,
        out_shape=block,
        scratch_shapes=[
            pltpu.VMEM((pairs, count, LANES), jnp.float32),
            pltpu.VMEM((orders * count, LANES), jnp.float32),
            table_buf,
            table_buf,
            pltpu.SemaphoreType.DMA((2,)),
        ],
        compiler_params=pltpu.CompilerParams(vmem_limit_bytes=16 * MIB),
        name="synthesis",
    )(got, coef, *split_constant(backward), *split_constant(synthesise))
    got = exchange(sent)
    return pl.pallas_call(
        mlp_kernel,
        in_specs=[vmem] * 4,
        out_specs=vmem,
        out_shape=jax.ShapeDtypeStruct((1, lat_out, lon_out, channels), jnp.float32),
        scratch_shapes=[pltpu.VMEM((8 * devices, channels), jnp.float32)],
        compiler_params=pltpu.CompilerParams(vmem_limit_bytes=16 * MIB),
        name="mlp",
    )(got, norm_gain.reshape(1, channels), w_in, w_out)


def per_device(field, filter_real, filter_imag, norm_gain, w_in, w_out):
    polar_count, azimuth_count = lax.axis_size("polar"), lax.axis_size("azimuth")
    plan = jointly if joint_fits(field, filter_real, polar_count, azimuth_count) else by_axes
    return plan(field, filter_real, filter_imag, norm_gain, w_in, w_out)


def solution(mesh):
    in_specs = (
        P(None, "polar", "azimuth", None),
        P("azimuth", None, None),
        P("azimuth", None, None),
        P(),
        P(),
        P(),
    )
    out_specs = P(None, "polar", "azimuth", None)
    return jax.shard_map(
        per_device, mesh=mesh, in_specs=in_specs, out_specs=out_specs, check_vma=False
    )
```

```python
import functools
import math

import jax
import jax.numpy as jnp
import numpy as np
from jax import lax
from jax.experimental import pallas as pl
from jax.experimental.pallas import tpu as pltpu
from jax.sharding import PartitionSpec as P


def legendre(nodes, degrees, orders):
    cosines, sines = np.cos(nodes)[None, :], np.sin(nodes)[None, :]
    mode = np.arange(orders, dtype=np.float64)[:, None]
    counter = np.arange(1, orders + 1, dtype=np.float64)
    ratios = np.log((2.0 * counter - 1.0) / (2.0 * counter))
    product_log = np.concatenate([[0.0], np.cumsum(ratios)])[:orders, None]
    diagonal = np.exp(
        0.5 * (np.log((2.0 * mode + 1.0) / (4.0 * math.pi)) + product_log) + mode * np.log(sines)
    )
    newest, older = np.zeros_like(diagonal), np.zeros_like(diagonal)
    stacked = []
    for degree in range(degrees):
        lower = np.where(degree > mode, degree * degree - mode * mode, 1.0)
        factor_a = np.sqrt(max(4.0 * degree * degree - 1.0, 0.0) / lower)
        factor_b = np.sqrt(
            np.maximum((degree - 1.0) ** 2 - mode**2, 0.0) / max(4.0 * (degree - 1.0) ** 2 - 1.0, 1.0)
        )
        recurred = factor_a * (cosines * newest - factor_b * older)
        second = np.sqrt(2.0 * mode + 3.0) * cosines * newest
        value = np.where(
            degree == mode,
            diagonal,
            np.where(degree == mode + 1.0, second, np.where(degree > mode + 1.0, recurred, 0.0)),
        )
        stacked.append(value)
        newest, older = value, newest
    return np.stack(stacked, axis=1)


def colatitudes(count):
    return math.pi * (np.arange(count) + 0.5) / count


def fourier_table(points, mode_ids, halves, weights):
    angle = 2.0 * math.pi / points * (np.arange(points)[:, None] * mode_ids[None, :] % points)
    return np.where(
        halves[None, :] == 0, weights[None, :] * np.cos(angle), -weights[None, :] * np.sin(angle)
    )


def by_axes(field, filter_real, filter_imag, norm_gain, w_in, w_out):
    high = lax.Precision.HIGHEST
    samples, lat_rows, lon_cols, channels = field.shape
    polar_count = lax.axis_size("polar")
    azimuth_count = lax.axis_size("azimuth")
    fine_lat = lat_rows * polar_count
    fine_lon = lon_cols * azimuth_count
    coarse_lat = fine_lat // 2
    coarse_lon = fine_lon // 2
    orders = coarse_lon // 2
    order_piece = orders // polar_count
    chan_slice = channels // azimuth_count
    columns_all = np.arange(2 * orders)
    halves = columns_all // order_piece % 2
    mode_ids = columns_all // (2 * order_piece) * order_piece + columns_all % order_piece
    twofold = np.where(mode_ids == 0, 1.0, 2.0)
    forward_table = jnp.asarray(
        fourier_table(fine_lon, mode_ids, halves, np.ones(2 * orders)), jnp.float32
    )
    inverse_table = jnp.asarray(fourier_table(coarse_lon, mode_ids, halves, twofold).T, jnp.float32)
    polar_index = lax.axis_index("polar")
    fine_nodes = colatitudes(fine_lat)
    quadrature = math.pi / fine_lat * np.sin(fine_nodes) * (2.0 * math.pi / fine_lon)
    all_fine = legendre(fine_nodes, coarse_lat, orders) * quadrature
    all_coarse = legendre(colatitudes(coarse_lat), coarse_lat, orders)
    own_orders = lambda table: lax.dynamic_slice_in_dim(
        jnp.asarray(table, jnp.float32), polar_index * order_piece, order_piece, 0
    )
    table_fine = own_orders(all_fine)
    table_coarse = own_orders(all_coarse)
    moved = lax.all_to_all(field, "azimuth", split_axis=3, concat_axis=2, tiled=True)
    spectrum = jnp.einsum("bijc,jk->bick", moved, forward_table, precision=high)
    by_order = lax.all_to_all(spectrum, "polar", split_axis=3, concat_axis=1, tiled=True)
    by_order = by_order.reshape(samples, fine_lat, chan_slice, 2, order_piece)
    coef = jnp.einsum("kli,bicpk->blcpk", table_fine, by_order, precision=high)
    degree_block = lax.all_to_all(coef, "azimuth", split_axis=1, concat_axis=2, tiled=True)
    block_re = degree_block[:, :, :, 0]
    block_im = degree_block[:, :, :, 1]
    out_re = jnp.einsum("lco,blck->blok", filter_real, block_re, precision=high) - jnp.einsum(
        "lco,blck->blok", filter_imag, block_im, precision=high
    )
    out_im = jnp.einsum("lco,blck->blok", filter_real, block_im, precision=high) + jnp.einsum(
        "lco,blck->blok", filter_imag, block_re, precision=high
    )
    mixed_spec = jnp.stack([out_re, out_im], axis=3)
    filtered = lax.all_to_all(mixed_spec, "azimuth", split_axis=2, concat_axis=1, tiled=True)
    both_fields = jnp.concatenate([coef, filtered], axis=2)
    grid_modes = jnp.einsum("kli,blcpk->bicpk", table_coarse, both_fields, precision=high)
    grid_modes = grid_modes.reshape(samples, coarse_lat, 2 * chan_slice, 2 * order_piece)
    row_block = lax.all_to_all(grid_modes, "polar", split_axis=1, concat_axis=3, tiled=True)
    values = jnp.einsum("bick,kj->bijc", row_block, inverse_table, precision=high)
    state_split = (
        jax.nn.gelu(values[..., chan_slice:], approximate=False) + values[..., :chan_slice]
    )
    state = lax.all_to_all(state_split, "azimuth", split_axis=2, concat_axis=3, tiled=True)
    center = jnp.mean(state, axis=-1, keepdims=True)
    spread = jnp.mean((state - center) ** 2, axis=-1, keepdims=True)
    normed = ((state - center) * lax.rsqrt(spread + 1e-05) * norm_gain).astype(jnp.bfloat16)
    flat = normed.reshape(-1, channels)
    hidden = jax.nn.gelu(
        jnp.dot(flat, w_in, preferred_element_type=jnp.float32), approximate=False
    ).astype(jnp.bfloat16)
    update = jnp.dot(hidden, w_out, preferred_element_type=jnp.float32)
    return state + update.reshape(state.shape)


LANES = 128
BOTH = ("polar", "azimuth")
MIB = 1024 * 1024


def split_bf16(table):
    high = table.astype(jnp.bfloat16)
    return high, (table - high.astype(jnp.float32)).astype(jnp.bfloat16)


def split_constant(table):
    table = np.asarray(table, np.float32)
    high = table.astype(jnp.bfloat16)
    return jnp.asarray(high), jnp.asarray((table - high.astype(np.float32)).astype(jnp.bfloat16))


def dot(left, right):
    return jnp.dot(left, right, preferred_element_type=jnp.float32)


def dot3(left, right_high, right_low):
    rows = left.shape[0]
    left_high, left_low = split_bf16(left)
    both = dot(jnp.concatenate([left_high, left_low], axis=0), right_high)
    return both[:rows] + both[rows:] + dot(left_high, right_low)


def swap(blocks, bits):
    lane = lax.broadcasted_iota(jnp.int32, blocks[0].shape, len(blocks[0].shape) - 1)
    axis = len(blocks[0].shape) - 1
    blocks = list(blocks)
    for order, bit in enumerate(bits):
        step = 1 << bit
        keep = (lane & step) == 0
        for index in range(len(blocks)):
            if index >> order & 1:
                continue
            first, second = blocks[index], blocks[index | 1 << order]
            blocks[index] = jnp.where(keep, first, pltpu.roll(second, step, axis))
            blocks[index | 1 << order] = jnp.where(
                keep, pltpu.roll(first, LANES - step, axis), second
            )
    return blocks


OWNER_BITS = (0, 1, 2, 3, 6)
QUAD_BITS = (4, 5)
LOW_BITS = (0, 1, 2, 3, 4)


def gelu(values):
    return 0.5 * values * (1.0 + lax.erf(values * math.sqrt(0.5)))


def scatter_kernel(field, sent, buf, sems):
    devices, rows, channels = sent.shape
    copies = []
    for part in range(rows // 8):
        copy = pltpu.make_async_copy(
            field.at[0, :, pl.ds(8 * part, 8), :], buf.at[part], sems.at[part]
        )
        copy.start()
        copies.append(copy)
    for part, copy in enumerate(copies):
        copy.wait()
        for tile in range(channels // LANES):
            lanes = pl.ds(tile * LANES, LANES)
            blocks = swap([buf[part, lat, :, lanes] for lat in range(devices)], OWNER_BITS)
            for device in range(devices):
                sent[device, pl.ds(8 * part, 8), lanes] = blocks[device]


def analysis_kernel(
    polar_count, got, four_high, four_low, leg_high, leg_low, coef, sent, rows
):
    devices, lon_cols, width = got.shape
    azimuth_count = devices // polar_count
    modes = four_high.shape[0]
    orders = modes // 2
    four = jnp.concatenate([four_high[...], four_low[...]], axis=0)
    tiles = width // LANES
    for tile in range(tiles):
        spectra = []
        for polar in range(polar_count):
            block = got[pl.ds(polar * azimuth_count, azimuth_count), :, pl.ds(tile * LANES, LANES)]
            block = block.reshape(azimuth_count * lon_cols, LANES)
            block_high, block_low = split_bf16(block)
            both = dot(four, block_high)
            spectra.append(both[:modes] + both[modes:] + dot(four[:modes], block_low))
        for quad, spectrum in enumerate(swap(spectra, QUAD_BITS)):
            rows[pl.ds((tile * polar_count + quad) * modes, modes), :] = spectrum
    count = 2 * tiles * polar_count
    extra = orders - devices
    for order in range(devices):
        first = rows[pl.ds(order, count, stride=orders), :]
        second = rows[pl.ds(devices + order % extra, count, stride=orders), :]
        coef[order] = dot3(jnp.concatenate([first, second], axis=1), leg_high[order], leg_low[order])
    pack_by_degree(coef, sent)


def pack_by_degree(coef, sent):
    devices, count, _ = coef.shape
    dense, tail = count * 3 // 4, count // 4
    used = LANES * 3 // 4
    for row in range(0, count, 8):
        blocks = swap([coef[order, pl.ds(row, 8), :] for order in range(devices)], LOW_BITS)
        head = min(max(dense - row, 0), 8)
        for device in range(devices):
            start = device * dense
            if head:
                sent[pl.ds(start + row, head), pl.ds(0, used)] = blocks[device][:head, :used]
            if head < 8:
                skip = max(row - dense, 0)
                for part in range(3):
                    moved = pltpu.roll(blocks[device], used - 32 * part, 1)
                    sent[pl.ds(start + tail * part + skip, 8 - head), pl.ds(used, LANES - used)] = moved[
                        head:, used:
                    ]


def filter_kernel(first_degree, got, real, imag, sent, real_buf, imag_buf, turned, sems):
    degrees, channels, _ = real_buf.shape
    start = first_degree[0]
    copies = []
    for degree in range(degrees):
        pair = [
            pltpu.make_async_copy(real.at[start + degree], real_buf.at[degree], sems.at[0, degree]),
            pltpu.make_async_copy(imag.at[start + degree], imag_buf.at[degree], sems.at[1, degree]),
        ]
        for copy in pair:
            copy.start()
        copies.append(pair)
    tiles = channels // LANES
    count = 8 * tiles
    dense, tail = count * 3 // 4, count // 4
    devices = sent.shape[0] // dense
    groups = [
        (tile, top, quad) for tile in range(tiles) for top in range(2) for quad in range(4)
    ]
    quarter = lax.broadcasted_iota(jnp.int32, (16, LANES), 1) // 32
    spectra = []
    for half in range(2):
        parts = []
        for tile, top, quad in groups:
            row = 2 * (4 * tile + quad) + half
            load = lambda start: got[pl.ds(top * 16 * dense + start, 16, stride=dense), :]
            if row < dense:
                parts.append(load(row))
                continue
            folded = [
                pltpu.roll(load(tail * part + row - dense), 32 * (part + 1), 1) for part in range(3)
            ]
            parts.append(
                jnp.where(quarter == 0, folded[0], jnp.where(quarter == 1, folded[1], folded[2]))
            )
        spectra.append(jnp.concatenate(parts, axis=0).T)
    results = [[None] * 4 for _ in range(2)]
    for degree in range(degrees):
        for copy in copies[degree]:
            copy.wait()
        places = [(32 * degree, 32), (64 + 16 * degree, 16)]
        own = jnp.concatenate(
            [spectra[half][start : start + size] for half in range(2) for start, size in places],
            axis=0,
        )
        by_real = dot3(own, *split_bf16(real_buf[degree]))
        by_imag = dot3(own, *split_bf16(imag_buf[degree]))
        size = 48
        outs = (by_real[:size] - by_imag[size:], by_real[size:] + by_imag[:size])
        for half in range(2):
            results[half][degree] = outs[half][:32]
            results[half][2 + degree] = outs[half][32:]
    across = []
    for half in range(2):
        padding = jnp.zeros((32, channels), jnp.float32)
        across.append(jnp.concatenate(results[half] + [padding], axis=0).T)
    for top in range(2):
        rows = []
        for row in range(count):
            tile, quad, half = row // 8, row // 2 % 4, row % 2
            start = ((tile * 2 + top) * 4 + quad) * 16
            rows.append(across[half][start : start + 16])
        for row in range(dense):
            part = row // tail
            folded = pltpu.roll(rows[dense + row % tail], 96 - 32 * part, 1)
            turned[pl.ds((top * dense + row) * 16, 16), :] = jnp.where(
                quarter < 3, rows[row], folded
            )
    for device in range(devices):
        sent[pl.ds(device * dense, dense), :] = turned[
            pl.ds(device // 16 * 16 * dense + device % 16, dense, stride=16), :
        ]


def synthesis_kernel(
    polar_count, got, coef, four_high, four_low, leg_high, leg_low, sent, tails, back, modes_buf
):
    devices, count, _ = coef.shape
    dense, tail = count * 3 // 4, count // 4
    azimuth_count = devices // polar_count
    orders = four_high.shape[1] // 2
    extra = orders - devices
    quarter = lax.broadcasted_iota(jnp.int32, (tail, LANES), 1) // 32
    for device in range(devices):
        folded = [
            pltpu.roll(got[pl.ds(device * dense + tail * part, tail), :], 32 * (part + 1), 1)
            for part in range(3)
        ]
        tails[device, pl.ds(8 - tail, tail), :] = jnp.where(
            quarter == 0, folded[0], jnp.where(quarter == 1, folded[1], folded[2])
        )
        tails[device, pl.ds(0, 8 - tail), :] = got[
            pl.ds(device * dense + count - 8, 8 - tail), :
        ]
    for row in range(0, count, 8):
        if row + 8 < count:
            blocks = [got[pl.ds(device * dense + row, 8), :] for device in range(devices)]
        else:
            blocks = [tails[device] for device in range(devices)]
        blocks = swap(blocks, LOW_BITS)
        for order in range(devices):
            back[order, pl.ds(row, 8), :] = blocks[order]
    keep = (lax.broadcasted_iota(jnp.int32, (count, LANES), 1) & 64) == 0
    for order in range(devices):
        both = jnp.concatenate([coef[order], back[order]], axis=0)
        values = dot3(both, leg_high[order], leg_low[order])
        merged = [
            jnp.where(
                keep,
                values[:count, part * LANES : (part + 1) * LANES],
                values[count:, part * LANES : (part + 1) * LANES],
            )
            for part in range(2)
        ]
        modes_buf[pl.ds(order * count, count), :] = merged[0]
        later = devices + order % extra
        if order < extra:
            modes_buf[pl.ds(later * count, count), :] = merged[1]
        else:
            modes_buf[pl.ds(later * count, count), :] += merged[1]
    four = jnp.concatenate([four_high[...], four_low[...]], axis=0)
    points = four_high.shape[0]
    half = points // 2
    keep = (lax.broadcasted_iota(jnp.int32, (half, LANES), 1) & 64) == 0
    for tile in range(count // 8):
        states = []
        for quad in range(4):
            row = 2 * (4 * tile + quad)
            modes = jnp.concatenate(
                [modes_buf[pl.ds(row + part, orders, stride=count), :] for part in range(2)], axis=0
            )
            modes_high, modes_low = split_bf16(modes)
            both = dot(four, modes_high)
            values = both[:points] + both[points:] + dot(four[:points], modes_low)
            first, second = values[:half], values[half:]
            skip = jnp.where(keep, first, pltpu.roll(second, 64, 1))
            branch = jnp.where(keep, pltpu.roll(first, 64, 1), second)
            states.append(gelu(branch) + skip)
        for polar, state in enumerate(swap(states, QUAD_BITS)):
            for azimuth in range(azimuth_count):
                device = polar * azimuth_count + azimuth
                sent[pl.ds(device * dense + tail * tile, tail), :] = state[
                    tail * azimuth : tail * (azimuth + 1)
                ]


def mlp_kernel(got, gain, w_in, w_out, mixed, state, result, sem):
    channels = state.shape[1]
    _, lat_rows, lon_cols, _ = mixed.shape
    part = lon_cols // 2
    tiles = channels // LANES
    devices = got.shape[0] // (tiles * part)
    for tile in range(tiles):
        blocks = swap(
            [
                got[pl.ds((device * tiles + tile) * part, part), :]
                for device in range(devices)
            ],
            OWNER_BITS,
        )
        for device in range(devices):
            state[pl.ds(part * device, part), pl.ds(tile * LANES, LANES)] = blocks[device]
    value = state[...]
    center = jnp.mean(value, axis=-1, keepdims=True)
    spread = jnp.mean((value - center) ** 2, axis=-1, keepdims=True)
    normed = ((value - center) * lax.rsqrt(spread + 1e-05) * gain[...]).astype(jnp.bfloat16)
    hidden = gelu(dot(normed, w_in[...])).astype(jnp.bfloat16)
    state[...] = value + dot(hidden, w_out[...])
    for top in range(2):
        for lat in range(lat_rows):
            row = part * (top * lat_rows + lat)
            result[0, lat, pl.ds(top * part, part), :] = state[pl.ds(row, part), :]
    copy = pltpu.make_async_copy(result, mixed, sem)
    copy.start()
    copy.wait()


def joint_fits(field, filter_real, polar_count, azimuth_count):
    samples, lat_rows, lon_cols, channels = field.shape
    devices = polar_count * azimuth_count
    orders = lon_cols * azimuth_count // 4
    return (
        samples == 1
        and devices == 32
        and polar_count == 4
        and lat_rows == 32
        and lon_cols == 24
        and channels == 3 * LANES
        and filter_real.shape[0] == 2 * polar_count
        and 2 * orders == 3 * devices
    )


def jointly(field, filter_real, filter_imag, norm_gain, w_in, w_out):
    _, lat_rows, lon_cols, channels = field.shape
    polar_count = lax.axis_size("polar")
    azimuth_count = lax.axis_size("azimuth")
    devices = polar_count * azimuth_count
    fine_lat, fine_lon = lat_rows * polar_count, lon_cols * azimuth_count
    coarse_lat, coarse_lon = fine_lat // 2, fine_lon // 2
    orders = coarse_lon // 2
    extra = orders - devices
    count = 2 * channels // devices
    degrees_here = coarse_lat // devices
    lat_out, lon_out = coarse_lat // polar_count, coarse_lon // azimuth_count

    mode_ids = np.tile(np.arange(orders), 2)
    halves = np.repeat(np.arange(2), orders)
    forward = fourier_table(fine_lon, mode_ids, halves, np.ones(2 * orders)).T
    twofold = np.where(mode_ids == 0, 1.0, 2.0)
    inverse = fourier_table(coarse_lon, mode_ids, halves, twofold)
    backward = inverse.reshape(azimuth_count, 2, lon_out // 2, 2 * orders)
    backward = backward.transpose(1, 0, 2, 3).reshape(-1, 2 * orders)

    fine_nodes = colatitudes(fine_lat)
    quadrature = math.pi / fine_lat * np.sin(fine_nodes) * (2.0 * math.pi / fine_lon)
    fine = legendre(fine_nodes, coarse_lat, orders) * quadrature
    coarse = legendre(colatitudes(coarse_lat), coarse_lat, orders)
    owner = np.arange(devices)
    degree = (
        owner % azimuth_count * (coarse_lat // azimuth_count) + owner // azimuth_count * degrees_here
    )
    degree = (degree[None, :] + np.arange(degrees_here)[:, None]).reshape(-1)
    lane = np.arange(LANES)
    lat_fine = (lane >> 4 & 3) * lat_rows + (lane >> 6) * 16 + (lane & 15)
    lat_coarse = (lane >> 4 & 3) * lat_out + (lane & 15)
    fine = fine[:, degree][:, :, lat_fine].transpose(0, 2, 1)
    coarse = coarse[:, degree][:, :, lat_coarse]
    analyse = np.zeros((devices, 2, LANES, 4, devices))
    synthesise = np.zeros((devices, 4, devices, 2, LANES))
    for order in range(devices):
        later, which = devices + order % extra, order // extra
        own = slice(which * devices, (which + 1) * devices)
        analyse[order, 0, :, :2] = fine[order].reshape(LANES, 2, devices)
        analyse[order, 1, :, 2] = fine[later][:, own]
        synthesise[order, :2, :, 0] = coarse[order].reshape(2, devices, LANES)
        synthesise[order, 2, :, 1] = coarse[later][own]
    analyse = analyse.reshape(devices, 2 * LANES, LANES)
    synthesise = synthesise.reshape(devices, LANES, 2 * LANES)

    vmem = pl.BlockSpec(memory_space=pltpu.VMEM)
    hbm = pl.BlockSpec(memory_space=pltpu.HBM)
    dense = count * 3 // 4
    block = pltpu.VMEM((devices * dense, LANES), jnp.float32)

    def exchange(blocks):
        split = blocks.reshape((devices, -1, 2, LANES)) if blocks.ndim == 2 else blocks
        moved = lax.all_to_all(split, BOTH, split_axis=0, concat_axis=0, tiled=True)
        return moved.reshape(blocks.shape)

    def near(*arrays):
        return [pltpu.with_memory_space_constraint(array, pltpu.VMEM) for array in arrays]

    def far(*arrays):
        return [pltpu.with_memory_space_constraint(array, pltpu.HBM) for array in arrays]

    sent = pl.pallas_call(
        scatter_kernel,
        in_specs=[hbm],
        out_specs=vmem,
        out_shape=pltpu.VMEM((devices, lon_cols, channels), jnp.float32),
        scratch_shapes=[
            pltpu.VMEM((lon_cols // 8, lat_rows, 8, channels), jnp.float32),
            pltpu.SemaphoreType.DMA((lon_cols // 8,)),
        ],
        compiler_params=pltpu.CompilerParams(vmem_limit_bytes=8 * MIB),
        name="scatter_channels",
    )(*far(field))
    got = exchange(sent)
    coef, sent = pl.pallas_call(
        functools.partial(analysis_kernel, polar_count),
        in_specs=[vmem] * 5,
        out_specs=[vmem, vmem],
        out_shape=[pltpu.VMEM((devices, count, LANES), jnp.float32), block],
        scratch_shapes=[pltpu.VMEM((count * orders, LANES), jnp.float32)],
        compiler_params=pltpu.CompilerParams(vmem_limit_bytes=8 * MIB),
        name="analysis",
    )(*near(got, *split_constant(forward), *split_constant(analyse)))
    got = exchange(sent)
    first_degree = (lax.axis_index("polar") * degrees_here).astype(jnp.int32).reshape(1)
    sent = pl.pallas_call(
        filter_kernel,
        in_specs=[pl.BlockSpec(memory_space=pltpu.SMEM), vmem, hbm, hbm],
        out_specs=vmem,
        out_shape=block,
        scratch_shapes=[
            pltpu.VMEM((degrees_here, channels, channels), jnp.float32),
            pltpu.VMEM((degrees_here, channels, channels), jnp.float32),
            pltpu.VMEM((devices * dense, LANES), jnp.float32),
            pltpu.SemaphoreType.DMA((2, degrees_here)),
        ],
        compiler_params=pltpu.CompilerParams(vmem_limit_bytes=8 * MIB),
        name="channel_filter",
    )(first_degree, *near(got), *far(filter_real, filter_imag))
    got = exchange(sent)
    sent = pl.pallas_call(
        functools.partial(synthesis_kernel, polar_count),
        in_specs=[vmem] * 6,
        out_specs=vmem,
        out_shape=block,
        scratch_shapes=[
            pltpu.VMEM((devices, 8, LANES), jnp.float32),
            pltpu.VMEM((devices, count, LANES), jnp.float32),
            pltpu.VMEM((orders * count, LANES), jnp.float32),
        ],
        compiler_params=pltpu.CompilerParams(vmem_limit_bytes=8 * MIB),
        name="synthesis",
    )(*near(got, coef, *split_constant(backward), *split_constant(synthesise)))
    got = exchange(sent)
    result = (1, lat_out, lon_out, channels)
    return pl.pallas_call(
        mlp_kernel,
        in_specs=[vmem] * 4,
        out_specs=pl.BlockSpec(memory_space=pl.ANY),
        out_shape=jax.ShapeDtypeStruct(result, jnp.float32),
        scratch_shapes=[
            pltpu.VMEM((lat_out * lon_out, channels), jnp.float32),
            pltpu.VMEM(result, jnp.float32),
            pltpu.SemaphoreType.DMA,
        ],
        compiler_params=pltpu.CompilerParams(vmem_limit_bytes=8 * MIB),
        name="mlp",
    )(*near(got, norm_gain.reshape(1, channels), w_in, w_out))


def per_device(field, filter_real, filter_imag, norm_gain, w_in, w_out):
    polar_count, azimuth_count = lax.axis_size("polar"), lax.axis_size("azimuth")
    plan = jointly if joint_fits(field, filter_real, polar_count, azimuth_count) else by_axes
    return plan(field, filter_real, filter_imag, norm_gain, w_in, w_out)


def solution(mesh):
    in_specs = (
        P(None, "polar", "azimuth", None),
        P("azimuth", None, None),
        P("azimuth", None, None),
        P(),
        P(),
        P(),
    )
    out_specs = P(None, "polar", "azimuth", None)
    return jax.shard_map(
        per_device, mesh=mesh, in_specs=in_specs, out_specs=out_specs, check_vma=False
    )
```

```python
import functools
import math

import jax
import jax.numpy as jnp
import numpy as np
from jax import lax
from jax.experimental import pallas as pl
from jax.experimental.pallas import tpu as pltpu
from jax.sharding import PartitionSpec as P


def legendre(nodes, degrees, orders):
    cosines, sines = np.cos(nodes)[None, :], np.sin(nodes)[None, :]
    mode = np.arange(orders, dtype=np.float64)[:, None]
    counter = np.arange(1, orders + 1, dtype=np.float64)
    ratios = np.log((2.0 * counter - 1.0) / (2.0 * counter))
    product_log = np.concatenate([[0.0], np.cumsum(ratios)])[:orders, None]
    diagonal = np.exp(
        0.5 * (np.log((2.0 * mode + 1.0) / (4.0 * math.pi)) + product_log) + mode * np.log(sines)
    )
    newest, older = np.zeros_like(diagonal), np.zeros_like(diagonal)
    stacked = []
    for degree in range(degrees):
        lower = np.where(degree > mode, degree * degree - mode * mode, 1.0)
        factor_a = np.sqrt(max(4.0 * degree * degree - 1.0, 0.0) / lower)
        factor_b = np.sqrt(
            np.maximum((degree - 1.0) ** 2 - mode**2, 0.0) / max(4.0 * (degree - 1.0) ** 2 - 1.0, 1.0)
        )
        recurred = factor_a * (cosines * newest - factor_b * older)
        second = np.sqrt(2.0 * mode + 3.0) * cosines * newest
        value = np.where(
            degree == mode,
            diagonal,
            np.where(degree == mode + 1.0, second, np.where(degree > mode + 1.0, recurred, 0.0)),
        )
        stacked.append(value)
        newest, older = value, newest
    return np.stack(stacked, axis=1)


def colatitudes(count):
    return math.pi * (np.arange(count) + 0.5) / count


def fourier_table(points, mode_ids, halves, weights):
    angle = 2.0 * math.pi / points * (np.arange(points)[:, None] * mode_ids[None, :] % points)
    return np.where(
        halves[None, :] == 0, weights[None, :] * np.cos(angle), -weights[None, :] * np.sin(angle)
    )


def by_axes(field, filter_real, filter_imag, norm_gain, w_in, w_out):
    high = lax.Precision.HIGHEST
    samples, lat_rows, lon_cols, channels = field.shape
    polar_count = lax.axis_size("polar")
    azimuth_count = lax.axis_size("azimuth")
    fine_lat = lat_rows * polar_count
    fine_lon = lon_cols * azimuth_count
    coarse_lat = fine_lat // 2
    coarse_lon = fine_lon // 2
    orders = coarse_lon // 2
    order_piece = orders // polar_count
    chan_slice = channels // azimuth_count
    columns_all = np.arange(2 * orders)
    halves = columns_all // order_piece % 2
    mode_ids = columns_all // (2 * order_piece) * order_piece + columns_all % order_piece
    twofold = np.where(mode_ids == 0, 1.0, 2.0)
    forward_table = jnp.asarray(
        fourier_table(fine_lon, mode_ids, halves, np.ones(2 * orders)), jnp.float32
    )
    inverse_table = jnp.asarray(fourier_table(coarse_lon, mode_ids, halves, twofold).T, jnp.float32)
    polar_index = lax.axis_index("polar")
    fine_nodes = colatitudes(fine_lat)
    quadrature = math.pi / fine_lat * np.sin(fine_nodes) * (2.0 * math.pi / fine_lon)
    all_fine = legendre(fine_nodes, coarse_lat, orders) * quadrature
    all_coarse = legendre(colatitudes(coarse_lat), coarse_lat, orders)
    own_orders = lambda table: lax.dynamic_slice_in_dim(
        jnp.asarray(table, jnp.float32), polar_index * order_piece, order_piece, 0
    )
    table_fine = own_orders(all_fine)
    table_coarse = own_orders(all_coarse)
    moved = lax.all_to_all(field, "azimuth", split_axis=3, concat_axis=2, tiled=True)
    spectrum = jnp.einsum("bijc,jk->bick", moved, forward_table, precision=high)
    by_order = lax.all_to_all(spectrum, "polar", split_axis=3, concat_axis=1, tiled=True)
    by_order = by_order.reshape(samples, fine_lat, chan_slice, 2, order_piece)
    coef = jnp.einsum("kli,bicpk->blcpk", table_fine, by_order, precision=high)
    degree_block = lax.all_to_all(coef, "azimuth", split_axis=1, concat_axis=2, tiled=True)
    block_re = degree_block[:, :, :, 0]
    block_im = degree_block[:, :, :, 1]
    out_re = jnp.einsum("lco,blck->blok", filter_real, block_re, precision=high) - jnp.einsum(
        "lco,blck->blok", filter_imag, block_im, precision=high
    )
    out_im = jnp.einsum("lco,blck->blok", filter_real, block_im, precision=high) + jnp.einsum(
        "lco,blck->blok", filter_imag, block_re, precision=high
    )
    mixed_spec = jnp.stack([out_re, out_im], axis=3)
    filtered = lax.all_to_all(mixed_spec, "azimuth", split_axis=2, concat_axis=1, tiled=True)
    both_fields = jnp.concatenate([coef, filtered], axis=2)
    grid_modes = jnp.einsum("kli,blcpk->bicpk", table_coarse, both_fields, precision=high)
    grid_modes = grid_modes.reshape(samples, coarse_lat, 2 * chan_slice, 2 * order_piece)
    row_block = lax.all_to_all(grid_modes, "polar", split_axis=1, concat_axis=3, tiled=True)
    values = jnp.einsum("bick,kj->bijc", row_block, inverse_table, precision=high)
    state_split = (
        jax.nn.gelu(values[..., chan_slice:], approximate=False) + values[..., :chan_slice]
    )
    state = lax.all_to_all(state_split, "azimuth", split_axis=2, concat_axis=3, tiled=True)
    center = jnp.mean(state, axis=-1, keepdims=True)
    spread = jnp.mean((state - center) ** 2, axis=-1, keepdims=True)
    normed = ((state - center) * lax.rsqrt(spread + 1e-05) * norm_gain).astype(jnp.bfloat16)
    flat = normed.reshape(-1, channels)
    hidden = jax.nn.gelu(
        jnp.dot(flat, w_in, preferred_element_type=jnp.float32), approximate=False
    ).astype(jnp.bfloat16)
    update = jnp.dot(hidden, w_out, preferred_element_type=jnp.float32)
    return state + update.reshape(state.shape)


LANES = 128
BOTH = ("polar", "azimuth")
MIB = 1024 * 1024


def split_bf16(table):
    high = table.astype(jnp.bfloat16)
    return high, (table - high.astype(jnp.float32)).astype(jnp.bfloat16)


def split_constant(table):
    table = np.asarray(table, np.float32)
    high = table.astype(jnp.bfloat16)
    return jnp.asarray(high), jnp.asarray((table - high.astype(np.float32)).astype(jnp.bfloat16))


def dot(left, right):
    return jnp.dot(left, right, preferred_element_type=jnp.float32)


def dot3(left, right_high, right_low):
    rows = left.shape[0]
    left_high, left_low = split_bf16(left)
    both = dot(jnp.concatenate([left_high, left_low], axis=0), right_high)
    return both[:rows] + both[rows:] + dot(left_high, right_low)


def swap(blocks, step):
    count = len(blocks)
    axis = len(blocks[0].shape) - 1
    turn = lambda block, fields: (
        pltpu.roll(block, fields * step % LANES, axis) if fields * step % LANES else block
    )
    place = lax.broadcasted_iota(jnp.int32, blocks[0].shape, axis) // step
    turned = [turn(blocks[-index % count], -index % count) for index in range(count)]
    shift = 1
    while shift < count:
        take = (place & shift) != 0
        turned = [
            jnp.where(take, turned[(index - shift) % count], turned[index]) for index in range(count)
        ]
        shift *= 2
    return [turn(block, -index) for index, block in enumerate(turned)]


QUAD = 4
FIELD = LANES // QUAD


def gelu(values):
    return 0.5 * values * (1.0 + lax.erf(values * math.sqrt(0.5)))


def scatter_kernel(field, real, imag, sent, own_filter, buf, sems, filter_sems):
    devices, rows, channels = sent.shape
    parts = [(row, tile) for row in range(rows // 8) for tile in range(channels // LANES)]
    copies = []
    for index, (row, tile) in enumerate(parts):
        copy = pltpu.make_async_copy(
            field.at[0, :, pl.ds(8 * row, 8), pl.ds(tile * LANES, LANES)],
            buf.at[index],
            sems.at[index],
        )
        copy.start()
        copies.append(copy)
    degrees = own_filter.shape[1]
    start = lax.axis_index("polar") * degrees
    filter_copies = [
        pltpu.make_async_copy(
            part.at[pl.ds(start, degrees)], own_filter.at[index], filter_sems.at[index]
        )
        for index, part in enumerate((real, imag))
    ]
    for copy in filter_copies:
        copy.start()
    for index, (row, tile) in enumerate(parts):
        copies[index].wait()
        blocks = swap([buf[index, lat] for lat in range(devices)], 1)
        for device in range(devices):
            sent[device, pl.ds(8 * row, 8), pl.ds(tile * LANES, LANES)] = blocks[device]
    for copy in filter_copies:
        copy.wait()


def analysis_kernel(
    polar_count, got, four_high, four_low, leg_high, leg_low, coef, sent, rows
):
    devices, lon_cols, width = got.shape
    azimuth_count = devices // polar_count
    modes = four_high.shape[0]
    orders = modes // 2
    four = jnp.concatenate([four_high[...], four_low[...]], axis=0)
    tiles = width // LANES
    wide = []
    for polar in range(polar_count):
        block = got[pl.ds(polar * azimuth_count, azimuth_count)]
        block_high, block_low = split_bf16(block.reshape(azimuth_count * lon_cols, width))
        both = dot(four, block_high)
        wide.append(both[:modes] + both[modes:] + dot(four[:modes], block_low))
    for tile in range(tiles):
        spectra = [spectrum[:, tile * LANES : (tile + 1) * LANES] for spectrum in wide]
        for quad, spectrum in enumerate(swap(spectra, FIELD)):
            rows[pl.ds((tile * polar_count + quad) * modes, modes), :] = spectrum
    count = 2 * tiles * polar_count
    extra = orders - devices
    for order in range(devices):
        first = rows[pl.ds(order, count, stride=orders), :]
        second = rows[pl.ds(devices + order % extra, count, stride=orders), :]
        coef[order] = dot3(jnp.concatenate([first, second], axis=1), leg_high[order], leg_low[order])
    pack_by_degree(coef, sent)


def pack_by_degree(coef, sent):
    devices, count, _ = coef.shape
    dense, tail = count * 3 // 4, count // 4
    used = LANES * 3 // 4
    for row in range(0, count, 8):
        blocks = swap([coef[order, pl.ds(row, 8), :] for order in range(devices)], 1)
        head = min(max(dense - row, 0), 8)
        for device in range(devices):
            start = device * dense
            if head:
                sent[pl.ds(start + row, head), pl.ds(0, used)] = blocks[device][:head, :used]
            if head < 8:
                skip = max(row - dense, 0)
                for part in range(3):
                    moved = pltpu.roll(blocks[device], used - 32 * part, 1)
                    sent[pl.ds(start + tail * part + skip, 8 - head), pl.ds(used, LANES - used)] = moved[
                        head:, used:
                    ]


def filter_kernel(got, own_filter, sent, turned):
    _, degrees, channels, _ = own_filter.shape
    tiles = channels // LANES
    count = 8 * tiles
    dense, tail = count * 3 // 4, count // 4
    devices = sent.shape[0] // dense
    quarter = lax.broadcasted_iota(jnp.int32, (devices, LANES), 1) // 32
    spectra = []
    for half in range(2):
        parts = []
        for own in range(count // 2):
            row = 2 * own + half
            load = lambda start: got[pl.ds(start, devices, stride=dense), :]
            if row < dense:
                parts.append(load(row))
                continue
            folded = [
                pltpu.roll(load(tail * part + row - dense), 32 * (part + 1), 1) for part in range(3)
            ]
            parts.append(
                jnp.where(quarter == 0, folded[0], jnp.where(quarter == 1, folded[1], folded[2]))
            )
        spectra.append(jnp.concatenate(parts, axis=0).T)
    results = [[None] * 4 for _ in range(2)]
    for degree in range(degrees):
        places = [(32 * degree, 32), (64 + 16 * degree, 16)]
        own = jnp.concatenate(
            [spectra[half][start : start + size] for half in range(2) for start, size in places],
            axis=0,
        )
        by_real, by_imag = (dot3(own, *split_bf16(own_filter[part, degree])) for part in range(2))
        size = 48
        outs = (by_real[:size] - by_imag[size:], by_real[size:] + by_imag[:size])
        for half in range(2):
            results[half][degree] = outs[half][:32]
            results[half][2 + degree] = outs[half][32:]
    across = []
    for half in range(2):
        padding = jnp.zeros((32, channels), jnp.float32)
        across.append(jnp.concatenate(results[half] + [padding], axis=0).T)
    rows = [
        across[row % 2][row // 2 * devices : (row // 2 + 1) * devices] for row in range(count)
    ]
    for row in range(dense):
        part = row // tail
        folded = pltpu.roll(rows[dense + row % tail], 96 - 32 * part, 1)
        turned[pl.ds(row * devices, devices), :] = jnp.where(quarter < 3, rows[row], folded)
    for device in range(devices):
        sent[pl.ds(device * dense, dense), :] = turned[pl.ds(device, dense, stride=devices), :]


def synthesis_kernel(
    polar_count, got, coef, four_high, four_low, leg_high, leg_low, sent, tails, back, modes_buf
):
    devices, count, _ = coef.shape
    dense, tail = count * 3 // 4, count // 4
    azimuth_count = devices // polar_count
    orders = four_high.shape[1] // 2
    extra = orders - devices
    quarter = lax.broadcasted_iota(jnp.int32, (tail, LANES), 1) // 32
    for device in range(devices):
        folded = [
            pltpu.roll(got[pl.ds(device * dense + tail * part, tail), :], 32 * (part + 1), 1)
            for part in range(3)
        ]
        tails[device, pl.ds(8 - tail, tail), :] = jnp.where(
            quarter == 0, folded[0], jnp.where(quarter == 1, folded[1], folded[2])
        )
        tails[device, pl.ds(0, 8 - tail), :] = got[
            pl.ds(device * dense + count - 8, 8 - tail), :
        ]
    for row in range(0, count, 8):
        if row + 8 < count:
            blocks = [got[pl.ds(device * dense + row, 8), :] for device in range(devices)]
        else:
            blocks = [tails[device] for device in range(devices)]
        blocks = swap(blocks, 1)
        for order in range(devices):
            back[order, pl.ds(row, 8), :] = blocks[order]
    keep = (lax.broadcasted_iota(jnp.int32, (count, LANES), 1) & 16) == 0
    for order in range(devices):
        both = jnp.concatenate([coef[order], back[order]], axis=0)
        values = dot3(both, leg_high[order], leg_low[order])
        merged = [
            jnp.where(
                keep,
                values[:count, part * LANES : (part + 1) * LANES],
                values[count:, part * LANES : (part + 1) * LANES],
            )
            for part in range(2)
        ]
        modes_buf[pl.ds(order * count, count), :] = merged[0]
        later = devices + order % extra
        if order < extra:
            modes_buf[pl.ds(later * count, count), :] = merged[1]
        else:
            modes_buf[pl.ds(later * count, count), :] += merged[1]
    four = jnp.concatenate([four_high[...], four_low[...]], axis=0)
    points = four_high.shape[0]
    half = points // 2
    keep = (lax.broadcasted_iota(jnp.int32, (half, LANES), 1) & 16) == 0
    for tile in range(count // 8):
        states = []
        for quad in range(4):
            row = 2 * (4 * tile + quad)
            modes = jnp.concatenate(
                [modes_buf[pl.ds(row + part, orders, stride=count), :] for part in range(2)], axis=0
            )
            modes_high, modes_low = split_bf16(modes)
            both = dot(four, modes_high)
            values = both[:points] + both[points:] + dot(four[:points], modes_low)
            first, second = values[:half], values[half:]
            skip = jnp.where(keep, first, pltpu.roll(second, 16, 1))
            branch = jnp.where(keep, pltpu.roll(first, LANES - 16, 1), second)
            states.append(gelu(branch) + skip)
        for polar, state in enumerate(swap(states, FIELD)):
            for azimuth in range(azimuth_count):
                device = polar * azimuth_count + azimuth
                sent[pl.ds(device * dense + tail * tile, tail), :] = state[
                    tail * azimuth : tail * (azimuth + 1)
                ]


def mlp_kernel(got, gain, w_in, w_out, mixed, state):
    tiles = state.shape[0]
    _, lon_cols, lat_rows, _ = mixed.shape
    part = lon_cols // 2
    devices = got.shape[0] // (tiles * part)
    for tile in range(tiles):
        blocks = swap(
            [
                got[pl.ds((device * tiles + tile) * part, part), :]
                for device in range(devices)
            ],
            1,
        )
        for device in range(devices):
            state[tile, pl.ds(part * device, part), :] = blocks[device]
    value = jnp.concatenate([state[tile] for tile in range(tiles)], axis=1)
    center = jnp.mean(value, axis=-1, keepdims=True)
    spread = jnp.mean((value - center) ** 2, axis=-1, keepdims=True)
    normed = ((value - center) * lax.rsqrt(spread + 1e-05) * gain[...][None, :]).astype(jnp.bfloat16)
    hidden = gelu(dot(normed, w_in[...])).astype(jnp.bfloat16)
    value = value + dot(hidden, w_out[...])
    for tile in range(tiles):
        state[tile] = value[:, tile * LANES : (tile + 1) * LANES]
    for top in range(2):
        for lon in range(part):
            for tile in range(tiles):
                lanes = pl.ds(tile * LANES, LANES)
                mixed[0, top * part + lon, :, lanes] = state[
                    tile, pl.ds(top * part * lat_rows + lon, lat_rows, stride=part), :
                ]


def joint_fits(field, filter_real, polar_count, azimuth_count):
    samples, lat_rows, lon_cols, channels = field.shape
    devices = polar_count * azimuth_count
    orders = lon_cols * azimuth_count // 4
    return (
        samples == 1
        and devices == 32
        and polar_count == 4
        and lat_rows == 32
        and lon_cols == 24
        and channels == 3 * LANES
        and filter_real.shape[0] == 2 * polar_count
        and 2 * orders == 3 * devices
    )


def jointly(field, filter_real, filter_imag, norm_gain, w_in, w_out):
    _, lat_rows, lon_cols, channels = field.shape
    polar_count = lax.axis_size("polar")
    azimuth_count = lax.axis_size("azimuth")
    devices = polar_count * azimuth_count
    fine_lat, fine_lon = lat_rows * polar_count, lon_cols * azimuth_count
    coarse_lat, coarse_lon = fine_lat // 2, fine_lon // 2
    orders = coarse_lon // 2
    extra = orders - devices
    count = 2 * channels // devices
    degrees_here = coarse_lat // devices
    lat_out, lon_out = coarse_lat // polar_count, coarse_lon // azimuth_count

    mode_ids = np.tile(np.arange(orders), 2)
    halves = np.repeat(np.arange(2), orders)
    forward = fourier_table(fine_lon, mode_ids, halves, np.ones(2 * orders)).T
    twofold = np.where(mode_ids == 0, 1.0, 2.0)
    inverse = fourier_table(coarse_lon, mode_ids, halves, twofold)
    backward = inverse.reshape(azimuth_count, 2, lon_out // 2, 2 * orders)
    backward = backward.transpose(1, 0, 2, 3).reshape(-1, 2 * orders)

    fine_nodes = colatitudes(fine_lat)
    quadrature = math.pi / fine_lat * np.sin(fine_nodes) * (2.0 * math.pi / fine_lon)
    fine = legendre(fine_nodes, coarse_lat, orders) * quadrature
    coarse = legendre(colatitudes(coarse_lat), coarse_lat, orders)
    owner = np.arange(devices)
    degree = (
        owner % azimuth_count * (coarse_lat // azimuth_count) + owner // azimuth_count * degrees_here
    )
    degree = (degree[None, :] + np.arange(degrees_here)[:, None]).reshape(-1)
    lane = np.arange(LANES)
    lat_fine = lane
    lat_coarse = lane // 32 * lat_out + lane % 16
    fine = fine[:, degree][:, :, lat_fine].transpose(0, 2, 1)
    coarse = coarse[:, degree][:, :, lat_coarse]
    analyse = np.zeros((devices, 2, LANES, 4, devices))
    synthesise = np.zeros((devices, 4, devices, 2, LANES))
    for order in range(devices):
        later, which = devices + order % extra, order // extra
        own = slice(which * devices, (which + 1) * devices)
        analyse[order, 0, :, :2] = fine[order].reshape(LANES, 2, devices)
        analyse[order, 1, :, 2] = fine[later][:, own]
        synthesise[order, :2, :, 0] = coarse[order].reshape(2, devices, LANES)
        synthesise[order, 2, :, 1] = coarse[later][own]
    analyse = analyse.reshape(devices, 2 * LANES, LANES)
    synthesise = synthesise.reshape(devices, LANES, 2 * LANES)

    vmem = pl.BlockSpec(memory_space=pltpu.VMEM)
    hbm = pl.BlockSpec(memory_space=pltpu.HBM)
    dense = count * 3 // 4
    block = pltpu.VMEM((devices * dense, LANES), jnp.float32)

    def exchange(blocks):
        split = blocks.reshape((devices, -1, 2, LANES)) if blocks.ndim == 2 else blocks
        moved = lax.all_to_all(split, BOTH, split_axis=0, concat_axis=0, tiled=True)
        return moved.reshape(blocks.shape)

    def near(*arrays):
        return [pltpu.with_memory_space_constraint(array, pltpu.VMEM) for array in arrays]

    def far(*arrays):
        return [pltpu.with_memory_space_constraint(array, pltpu.HBM) for array in arrays]

    parts = lon_cols // 8 * (channels // LANES)
    sent, own_filter = pl.pallas_call(
        scatter_kernel,
        in_specs=[hbm] * 3,
        out_specs=[vmem] * 2,
        out_shape=[
            pltpu.VMEM((devices, lon_cols, channels), jnp.float32),
            pltpu.VMEM((2, degrees_here, channels, channels), jnp.float32),
        ],
        scratch_shapes=[
            pltpu.VMEM((parts, lat_rows, 8, LANES), jnp.float32),
            pltpu.SemaphoreType.DMA((parts,)),
            pltpu.SemaphoreType.DMA((2,)),
        ],
        compiler_params=pltpu.CompilerParams(vmem_limit_bytes=8 * MIB),
        name="scatter_channels",
    )(*far(field, filter_real, filter_imag))
    got = exchange(sent)
    coef, sent = pl.pallas_call(
        functools.partial(analysis_kernel, polar_count),
        in_specs=[vmem] * 5,
        out_specs=[vmem] * 2,
        out_shape=[pltpu.VMEM((devices, count, LANES), jnp.float32), block],
        scratch_shapes=[pltpu.VMEM((count * orders, LANES), jnp.float32)],
        compiler_params=pltpu.CompilerParams(vmem_limit_bytes=8 * MIB),
        name="analysis",
    )(*near(got, *split_constant(forward), *split_constant(analyse)))
    got = exchange(sent)
    sent = pl.pallas_call(
        filter_kernel,
        in_specs=[vmem] * 2,
        out_specs=vmem,
        out_shape=block,
        scratch_shapes=[pltpu.VMEM((devices * dense, LANES), jnp.float32)],
        compiler_params=pltpu.CompilerParams(vmem_limit_bytes=8 * MIB),
        name="channel_filter",
    )(*near(got, own_filter))
    got = exchange(sent)
    sent = pl.pallas_call(
        functools.partial(synthesis_kernel, polar_count),
        in_specs=[vmem] * 6,
        out_specs=vmem,
        out_shape=block,
        scratch_shapes=[
            pltpu.VMEM((devices, 8, LANES), jnp.float32),
            pltpu.VMEM((devices, count, LANES), jnp.float32),
            pltpu.VMEM((orders * count, LANES), jnp.float32),
        ],
        compiler_params=pltpu.CompilerParams(vmem_limit_bytes=8 * MIB),
        name="synthesis",
    )(*near(got, coef, *split_constant(backward), *split_constant(synthesise)))
    got = exchange(sent)
    mixed = pl.pallas_call(
        mlp_kernel,
        in_specs=[vmem] * 4,
        out_specs=vmem,
        out_shape=jax.ShapeDtypeStruct((1, lon_out, lat_out, channels), jnp.float32),
        scratch_shapes=[pltpu.VMEM((channels // LANES, lat_out * lon_out, LANES), jnp.float32)],
        compiler_params=pltpu.CompilerParams(vmem_limit_bytes=8 * MIB),
        name="mlp",
    )(*near(got, norm_gain, w_in, w_out))
    return mixed.transpose(0, 2, 1, 3)


def per_device(field, filter_real, filter_imag, norm_gain, w_in, w_out):
    polar_count, azimuth_count = lax.axis_size("polar"), lax.axis_size("azimuth")
    plan = jointly if joint_fits(field, filter_real, polar_count, azimuth_count) else by_axes
    return plan(field, filter_real, filter_imag, norm_gain, w_in, w_out)


def solution(mesh):
    in_specs = (
        P(None, "polar", "azimuth", None),
        P("azimuth", None, None),
        P("azimuth", None, None),
        P(),
        P(),
        P(),
    )
    out_specs = P(None, "polar", "azimuth", None)
    return jax.shard_map(
        per_device, mesh=mesh, in_specs=in_specs, out_specs=out_specs, check_vma=False
    )
```

```python
import functools
import math

import jax
import jax.numpy as jnp
import numpy as np
from jax import lax
from jax.experimental import pallas as pl
from jax.experimental.pallas import tpu as pltpu
from jax.sharding import PartitionSpec as P


def legendre(nodes, degrees, orders):
    cosines, sines = np.cos(nodes)[None, :], np.sin(nodes)[None, :]
    mode = np.arange(orders, dtype=np.float64)[:, None]
    counter = np.arange(1, orders + 1, dtype=np.float64)
    ratios = np.log((2.0 * counter - 1.0) / (2.0 * counter))
    product_log = np.concatenate([[0.0], np.cumsum(ratios)])[:orders, None]
    diagonal = np.exp(
        0.5 * (np.log((2.0 * mode + 1.0) / (4.0 * math.pi)) + product_log) + mode * np.log(sines)
    )
    newest, older = np.zeros_like(diagonal), np.zeros_like(diagonal)
    stacked = []
    for degree in range(degrees):
        lower = np.where(degree > mode, degree * degree - mode * mode, 1.0)
        factor_a = np.sqrt(max(4.0 * degree * degree - 1.0, 0.0) / lower)
        factor_b = np.sqrt(
            np.maximum((degree - 1.0) ** 2 - mode**2, 0.0) / max(4.0 * (degree - 1.0) ** 2 - 1.0, 1.0)
        )
        recurred = factor_a * (cosines * newest - factor_b * older)
        second = np.sqrt(2.0 * mode + 3.0) * cosines * newest
        value = np.where(
            degree == mode,
            diagonal,
            np.where(degree == mode + 1.0, second, np.where(degree > mode + 1.0, recurred, 0.0)),
        )
        stacked.append(value)
        newest, older = value, newest
    return np.stack(stacked, axis=1)


def colatitudes(count):
    return math.pi * (np.arange(count) + 0.5) / count


def fourier_table(points, mode_ids, halves, weights):
    angle = 2.0 * math.pi / points * (np.arange(points)[:, None] * mode_ids[None, :] % points)
    return np.where(
        halves[None, :] == 0, weights[None, :] * np.cos(angle), -weights[None, :] * np.sin(angle)
    )


def by_axes(field, filter_real, filter_imag, norm_gain, w_in, w_out):
    high = lax.Precision.HIGHEST
    samples, lat_rows, lon_cols, channels = field.shape
    polar_count = lax.axis_size("polar")
    azimuth_count = lax.axis_size("azimuth")
    fine_lat = lat_rows * polar_count
    fine_lon = lon_cols * azimuth_count
    coarse_lat = fine_lat // 2
    coarse_lon = fine_lon // 2
    orders = coarse_lon // 2
    order_piece = orders // polar_count
    chan_slice = channels // azimuth_count
    columns_all = np.arange(2 * orders)
    halves = columns_all // order_piece % 2
    mode_ids = columns_all // (2 * order_piece) * order_piece + columns_all % order_piece
    twofold = np.where(mode_ids == 0, 1.0, 2.0)
    forward_table = jnp.asarray(
        fourier_table(fine_lon, mode_ids, halves, np.ones(2 * orders)), jnp.float32
    )
    inverse_table = jnp.asarray(fourier_table(coarse_lon, mode_ids, halves, twofold).T, jnp.float32)
    polar_index = lax.axis_index("polar")
    fine_nodes = colatitudes(fine_lat)
    quadrature = math.pi / fine_lat * np.sin(fine_nodes) * (2.0 * math.pi / fine_lon)
    all_fine = legendre(fine_nodes, coarse_lat, orders) * quadrature
    all_coarse = legendre(colatitudes(coarse_lat), coarse_lat, orders)
    own_orders = lambda table: lax.dynamic_slice_in_dim(
        jnp.asarray(table, jnp.float32), polar_index * order_piece, order_piece, 0
    )
    table_fine = own_orders(all_fine)
    table_coarse = own_orders(all_coarse)
    moved = lax.all_to_all(field, "azimuth", split_axis=3, concat_axis=2, tiled=True)
    spectrum = jnp.einsum("bijc,jk->bick", moved, forward_table, precision=high)
    by_order = lax.all_to_all(spectrum, "polar", split_axis=3, concat_axis=1, tiled=True)
    by_order = by_order.reshape(samples, fine_lat, chan_slice, 2, order_piece)
    coef = jnp.einsum("kli,bicpk->blcpk", table_fine, by_order, precision=high)
    degree_block = lax.all_to_all(coef, "azimuth", split_axis=1, concat_axis=2, tiled=True)
    block_re = degree_block[:, :, :, 0]
    block_im = degree_block[:, :, :, 1]
    out_re = jnp.einsum("lco,blck->blok", filter_real, block_re, precision=high) - jnp.einsum(
        "lco,blck->blok", filter_imag, block_im, precision=high
    )
    out_im = jnp.einsum("lco,blck->blok", filter_real, block_im, precision=high) + jnp.einsum(
        "lco,blck->blok", filter_imag, block_re, precision=high
    )
    mixed_spec = jnp.stack([out_re, out_im], axis=3)
    filtered = lax.all_to_all(mixed_spec, "azimuth", split_axis=2, concat_axis=1, tiled=True)
    both_fields = jnp.concatenate([coef, filtered], axis=2)
    grid_modes = jnp.einsum("kli,blcpk->bicpk", table_coarse, both_fields, precision=high)
    grid_modes = grid_modes.reshape(samples, coarse_lat, 2 * chan_slice, 2 * order_piece)
    row_block = lax.all_to_all(grid_modes, "polar", split_axis=1, concat_axis=3, tiled=True)
    values = jnp.einsum("bick,kj->bijc", row_block, inverse_table, precision=high)
    state_split = (
        jax.nn.gelu(values[..., chan_slice:], approximate=False) + values[..., :chan_slice]
    )
    state = lax.all_to_all(state_split, "azimuth", split_axis=2, concat_axis=3, tiled=True)
    center = jnp.mean(state, axis=-1, keepdims=True)
    spread = jnp.mean((state - center) ** 2, axis=-1, keepdims=True)
    normed = ((state - center) * lax.rsqrt(spread + 1e-05) * norm_gain).astype(jnp.bfloat16)
    flat = normed.reshape(-1, channels)
    hidden = jax.nn.gelu(
        jnp.dot(flat, w_in, preferred_element_type=jnp.float32), approximate=False
    ).astype(jnp.bfloat16)
    update = jnp.dot(hidden, w_out, preferred_element_type=jnp.float32)
    return state + update.reshape(state.shape)


LANES = 128
BOTH = ("polar", "azimuth")
MIB = 1024 * 1024


def split_bf16(table):
    high = table.astype(jnp.bfloat16)
    return high, (table - high.astype(jnp.float32)).astype(jnp.bfloat16)


def split_constant(table):
    table = np.asarray(table, np.float32)
    high = table.astype(jnp.bfloat16)
    return jnp.asarray(high), jnp.asarray((table - high.astype(np.float32)).astype(jnp.bfloat16))


def dot(left, right):
    return jnp.dot(left, right, preferred_element_type=jnp.float32)


def dot3(left, right_high, right_low):
    rows = left.shape[0]
    left_high, left_low = split_bf16(left)
    both = dot(jnp.concatenate([left_high, left_low], axis=0), right_high)
    return both[:rows] + both[rows:] + dot(left_high, right_low)


def swap(blocks, step):
    count = len(blocks)
    axis = len(blocks[0].shape) - 1
    turn = lambda block, fields: (
        pltpu.roll(block, fields * step % LANES, axis) if fields * step % LANES else block
    )
    place = lax.broadcasted_iota(jnp.int32, blocks[0].shape, axis) // step
    turned = [turn(blocks[-index % count], -index % count) for index in range(count)]
    shift = 1
    while shift < count:
        take = (place & shift) != 0
        turned = [
            jnp.where(take, turned[(index - shift) % count], turned[index]) for index in range(count)
        ]
        shift *= 2
    return [turn(block, -index) for index, block in enumerate(turned)]


QUAD = 4
FIELD = LANES // QUAD


def gelu(values):
    return 0.5 * values * (1.0 + lax.erf(values * math.sqrt(0.5)))


def scatter_kernel(field, real, imag, sent, own_filter, buf, sems, filter_sems):
    devices, rows, channels = sent.shape
    parts = [(row, tile) for row in range(rows // 8) for tile in range(channels // LANES)]
    copies = []
    for index, (row, tile) in enumerate(parts):
        copy = pltpu.make_async_copy(
            field.at[0, :, pl.ds(8 * row, 8), pl.ds(tile * LANES, LANES)],
            buf.at[index],
            sems.at[index],
        )
        copy.start()
        copies.append(copy)
    degrees = own_filter.shape[1]
    start = lax.axis_index("polar") * degrees
    filter_copies = [
        pltpu.make_async_copy(
            part.at[pl.ds(start, degrees)], own_filter.at[index], filter_sems.at[index]
        )
        for index, part in enumerate((real, imag))
    ]
    for copy in filter_copies:
        copy.start()
    for index, (row, tile) in enumerate(parts):
        copies[index].wait()
        blocks = swap([buf[index, lat] for lat in range(devices)], 1)
        for device in range(devices):
            sent[device, pl.ds(8 * row, 8), pl.ds(tile * LANES, LANES)] = blocks[device]
    for copy in filter_copies:
        copy.wait()


def analysis_kernel(
    polar_count, got, four_high, four_low, leg_high, leg_low, coef, sent, rows
):
    devices, lon_cols, width = got.shape
    azimuth_count = devices // polar_count
    modes = four_high.shape[0]
    orders = modes // 2
    four = jnp.concatenate([four_high[...], four_low[...]], axis=0)
    tiles = width // LANES
    wide = []
    for polar in range(polar_count):
        block = got[pl.ds(polar * azimuth_count, azimuth_count)]
        block_high, block_low = split_bf16(block.reshape(azimuth_count * lon_cols, width))
        both = dot(four, block_high)
        wide.append(both[:modes] + both[modes:] + dot(four[:modes], block_low))
    for tile in range(tiles):
        spectra = [spectrum[:, tile * LANES : (tile + 1) * LANES] for spectrum in wide]
        for quad, spectrum in enumerate(swap(spectra, FIELD)):
            rows[pl.ds((tile * polar_count + quad) * modes, modes), :] = spectrum
    count = 2 * tiles * polar_count
    extra = orders - devices
    first_half = lax.broadcasted_iota(jnp.int32, (count, LANES), 1) < LANES // 2
    for order in range(extra):
        own = [
            rows[pl.ds(row, count, stride=orders), :]
            for row in (order, order + extra, devices + order)
        ]
        values = dot3(jnp.concatenate(own, axis=0), leg_high[order], leg_low[order])
        for part in range(2):
            lanes = slice(part * LANES, (part + 1) * LANES)
            coef[order + part * extra] = jnp.where(
                first_half,
                values[part * count : (part + 1) * count, lanes],
                values[2 * count :, lanes],
            )
    pack_by_degree(coef, sent)


def pack_by_degree(coef, sent):
    devices, count, _ = coef.shape
    dense, tail = count * 3 // 4, count // 4
    used = LANES * 3 // 4
    for row in range(0, count, 8):
        blocks = swap([coef[order, pl.ds(row, 8), :] for order in range(devices)], 1)
        head = min(max(dense - row, 0), 8)
        for device in range(devices):
            start = device * dense
            if head:
                sent[pl.ds(start + row, head), pl.ds(0, used)] = blocks[device][:head, :used]
            if head < 8:
                skip = max(row - dense, 0)
                for part in range(3):
                    moved = pltpu.roll(blocks[device], used - 32 * part, 1)
                    sent[pl.ds(start + tail * part + skip, 8 - head), pl.ds(used, LANES - used)] = moved[
                        head:, used:
                    ]


def filter_kernel(got, own_filter, sent, turned):
    _, degrees, channels, _ = own_filter.shape
    tiles = channels // LANES
    count = 8 * tiles
    dense, tail = count * 3 // 4, count // 4
    devices = sent.shape[0] // dense
    quarter = lax.broadcasted_iota(jnp.int32, (devices, LANES), 1) // 32
    spectra = []
    for half in range(2):
        parts = []
        for own in range(count // 2):
            row = 2 * own + half
            load = lambda start: got[pl.ds(start, devices, stride=dense), :]
            if row < dense:
                parts.append(load(row))
                continue
            folded = [
                pltpu.roll(load(tail * part + row - dense), 32 * (part + 1), 1) for part in range(3)
            ]
            parts.append(
                jnp.where(quarter == 0, folded[0], jnp.where(quarter == 1, folded[1], folded[2]))
            )
        spectra.append(jnp.concatenate(parts, axis=0).T)
    results = [[None] * 4 for _ in range(2)]
    for degree in range(degrees):
        places = [(32 * degree, 32), (64 + 16 * degree, 16)]
        own = jnp.concatenate(
            [spectra[half][start : start + size] for half in range(2) for start, size in places],
            axis=0,
        )
        parts = [split_bf16(own_filter[part, degree]) for part in range(2)]
        both = dot3(own, *(jnp.concatenate(pair, axis=1) for pair in zip(*parts)))
        by_real, by_imag = both[:, :channels], both[:, channels:]
        size = 48
        outs = (by_real[:size] - by_imag[size:], by_real[size:] + by_imag[:size])
        for half in range(2):
            results[half][degree] = outs[half][:32]
            results[half][2 + degree] = outs[half][32:]
    across = []
    for half in range(2):
        padding = jnp.zeros((32, channels), jnp.float32)
        across.append(jnp.concatenate(results[half] + [padding], axis=0).T)
    rows = [
        across[row % 2][row // 2 * devices : (row // 2 + 1) * devices] for row in range(count)
    ]
    for row in range(dense):
        part = row // tail
        folded = pltpu.roll(rows[dense + row % tail], 96 - 32 * part, 1)
        turned[pl.ds(row * devices, devices), :] = jnp.where(quarter < 3, rows[row], folded)
    for device in range(devices):
        sent[pl.ds(device * dense, dense), :] = turned[pl.ds(device, dense, stride=devices), :]


def synthesis_kernel(
    polar_count, got, coef, four_high, four_low, leg_high, leg_low, sent, tails, back, modes_buf
):
    devices, count, _ = coef.shape
    dense, tail = count * 3 // 4, count // 4
    azimuth_count = devices // polar_count
    orders = four_high.shape[1] // 2
    extra = orders - devices
    quarter = lax.broadcasted_iota(jnp.int32, (tail, LANES), 1) // 32
    for device in range(devices):
        folded = [
            pltpu.roll(got[pl.ds(device * dense + tail * part, tail), :], 32 * (part + 1), 1)
            for part in range(3)
        ]
        tails[device, pl.ds(8 - tail, tail), :] = jnp.where(
            quarter == 0, folded[0], jnp.where(quarter == 1, folded[1], folded[2])
        )
        tails[device, pl.ds(0, 8 - tail), :] = got[
            pl.ds(device * dense + count - 8, 8 - tail), :
        ]
    for row in range(0, count, 8):
        if row + 8 < count:
            blocks = [got[pl.ds(device * dense + row, 8), :] for device in range(devices)]
        else:
            blocks = [tails[device] for device in range(devices)]
        blocks = swap(blocks, 1)
        for order in range(devices):
            back[order, pl.ds(row, 8), :] = blocks[order]
    keep = (lax.broadcasted_iota(jnp.int32, (count, LANES), 1) & 16) == 0
    for order in range(devices):
        both = jnp.concatenate([coef[order], back[order]], axis=0)
        values = dot3(both, leg_high[order], leg_low[order])
        merged = [
            jnp.where(
                keep,
                values[:count, part * LANES : (part + 1) * LANES],
                values[count:, part * LANES : (part + 1) * LANES],
            )
            for part in range(2)
        ]
        modes_buf[pl.ds(order * count, count), :] = merged[0]
        later = devices + order % extra
        if order < extra:
            modes_buf[pl.ds(later * count, count), :] = merged[1]
        else:
            modes_buf[pl.ds(later * count, count), :] += merged[1]
    four = jnp.concatenate([four_high[...], four_low[...]], axis=0)
    points = four_high.shape[0]
    half = points // 2
    keep = (lax.broadcasted_iota(jnp.int32, (half, LANES), 1) & 16) == 0
    for tile in range(count // 8):
        states = []
        for quad in range(4):
            row = 2 * (4 * tile + quad)
            modes = jnp.concatenate(
                [modes_buf[pl.ds(row + part, orders, stride=count), :] for part in range(2)], axis=0
            )
            modes_high, modes_low = split_bf16(modes)
            both = dot(four, modes_high)
            values = both[:points] + both[points:] + dot(four[:points], modes_low)
            first, second = values[:half], values[half:]
            skip = jnp.where(keep, first, pltpu.roll(second, 16, 1))
            branch = jnp.where(keep, pltpu.roll(first, LANES - 16, 1), second)
            states.append(gelu(branch) + skip)
        for polar, state in enumerate(swap(states, FIELD)):
            for azimuth in range(azimuth_count):
                device = polar * azimuth_count + azimuth
                sent[pl.ds(device * dense + tail * tile, tail), :] = state[
                    tail * azimuth : tail * (azimuth + 1)
                ]


def mlp_kernel(got, gain, w_in, w_out, mixed, state, result, sems):
    tiles = state.shape[0]
    _, lon_cols, lat_rows, _ = mixed.shape
    part = lon_cols // 2
    devices = got.shape[0] // (tiles * part)
    for tile in range(tiles):
        blocks = swap(
            [
                got[pl.ds((device * tiles + tile) * part, part), :]
                for device in range(devices)
            ],
            1,
        )
        for device in range(devices):
            state[tile, pl.ds(part * device, part), :] = blocks[device]
    copies = []
    for top in range(2):
        cells = pl.ds(top * part * lat_rows, part * lat_rows)
        value = jnp.concatenate([state[tile, cells, :] for tile in range(tiles)], axis=1)
        center = jnp.mean(value, axis=-1, keepdims=True)
        spread = jnp.mean((value - center) ** 2, axis=-1, keepdims=True)
        normed = (value - center) * lax.rsqrt(spread + 1e-05) * gain[...][None, :]
        hidden = gelu(dot(normed.astype(jnp.bfloat16), w_in[...])).astype(jnp.bfloat16)
        value = value + dot(hidden, w_out[...])
        for tile in range(tiles):
            state[tile, cells, :] = value[:, tile * LANES : (tile + 1) * LANES]
            for lon in range(part):
                result[top * part + lon, :, pl.ds(tile * LANES, LANES)] = state[
                    tile, pl.ds(top * part * lat_rows + lon, lat_rows, stride=part), :
                ]
        lons = pl.ds(top * part, part)
        copies.append(pltpu.make_async_copy(result.at[lons], mixed.at[0, lons], sems.at[top]))
        copies[-1].start()
    for copy in copies:
        copy.wait()


def joint_fits(field, filter_real, polar_count, azimuth_count):
    samples, lat_rows, lon_cols, channels = field.shape
    devices = polar_count * azimuth_count
    orders = lon_cols * azimuth_count // 4
    return (
        samples == 1
        and devices == 32
        and polar_count == 4
        and lat_rows == 32
        and lon_cols == 24
        and channels == 3 * LANES
        and filter_real.shape[0] == 2 * polar_count
        and 2 * orders == 3 * devices
    )


def jointly(field, filter_real, filter_imag, norm_gain, w_in, w_out):
    _, lat_rows, lon_cols, channels = field.shape
    polar_count = lax.axis_size("polar")
    azimuth_count = lax.axis_size("azimuth")
    devices = polar_count * azimuth_count
    fine_lat, fine_lon = lat_rows * polar_count, lon_cols * azimuth_count
    coarse_lat, coarse_lon = fine_lat // 2, fine_lon // 2
    orders = coarse_lon // 2
    extra = orders - devices
    count = 2 * channels // devices
    degrees_here = coarse_lat // devices
    lat_out, lon_out = coarse_lat // polar_count, coarse_lon // azimuth_count

    mode_ids = np.tile(np.arange(orders), 2)
    halves = np.repeat(np.arange(2), orders)
    forward = fourier_table(fine_lon, mode_ids, halves, np.ones(2 * orders)).T
    twofold = np.where(mode_ids == 0, 1.0, 2.0)
    inverse = fourier_table(coarse_lon, mode_ids, halves, twofold)
    backward = inverse.reshape(azimuth_count, 2, lon_out // 2, 2 * orders)
    backward = backward.transpose(1, 0, 2, 3).reshape(-1, 2 * orders)

    fine_nodes = colatitudes(fine_lat)
    quadrature = math.pi / fine_lat * np.sin(fine_nodes) * (2.0 * math.pi / fine_lon)
    fine = legendre(fine_nodes, coarse_lat, orders) * quadrature
    coarse = legendre(colatitudes(coarse_lat), coarse_lat, orders)
    owner = np.arange(devices)
    degree = (
        owner % azimuth_count * (coarse_lat // azimuth_count) + owner // azimuth_count * degrees_here
    )
    degree = (degree[None, :] + np.arange(degrees_here)[:, None]).reshape(-1)
    lane = np.arange(LANES)
    lat_fine = lane
    lat_coarse = lane // 32 * lat_out + lane % 16
    fine = fine[:, degree][:, :, lat_fine].transpose(0, 2, 1)
    coarse = coarse[:, degree][:, :, lat_coarse]
    analyse = np.zeros((extra, LANES, 2, 4, devices))
    synthesise = np.zeros((devices, 4, devices, 2, LANES))
    for order in range(devices):
        later, which = devices + order % extra, order // extra
        own = slice(which * devices, (which + 1) * devices)
        analyse[order % extra, :, which, :2] = fine[order].reshape(LANES, 2, devices)
        analyse[order % extra, :, which, 2] = fine[later][:, own]
        synthesise[order, :2, :, 0] = coarse[order].reshape(2, devices, LANES)
        synthesise[order, 2, :, 1] = coarse[later][own]
    analyse = analyse.reshape(extra, LANES, 2 * LANES)
    synthesise = synthesise.reshape(devices, LANES, 2 * LANES)

    vmem = pl.BlockSpec(memory_space=pltpu.VMEM)
    hbm = pl.BlockSpec(memory_space=pltpu.HBM)
    dense = count * 3 // 4
    block = pltpu.VMEM((devices * dense, LANES), jnp.float32)

    def exchange(blocks):
        split = blocks.reshape((devices, -1, 2, LANES)) if blocks.ndim == 2 else blocks
        moved = lax.all_to_all(split, BOTH, split_axis=0, concat_axis=0, tiled=True)
        return moved.reshape(blocks.shape)

    def near(*arrays):
        return [pltpu.with_memory_space_constraint(array, pltpu.VMEM) for array in arrays]

    def far(*arrays):
        return [pltpu.with_memory_space_constraint(array, pltpu.HBM) for array in arrays]

    parts = lon_cols // 8 * (channels // LANES)
    sent, own_filter = pl.pallas_call(
        scatter_kernel,
        in_specs=[hbm] * 3,
        out_specs=[vmem] * 2,
        out_shape=[
            pltpu.VMEM((devices, lon_cols, channels), jnp.float32),
            pltpu.VMEM((2, degrees_here, channels, channels), jnp.float32),
        ],
        scratch_shapes=[
            pltpu.VMEM((parts, lat_rows, 8, LANES), jnp.float32),
            pltpu.SemaphoreType.DMA((parts,)),
            pltpu.SemaphoreType.DMA((2,)),
        ],
        compiler_params=pltpu.CompilerParams(vmem_limit_bytes=8 * MIB),
        name="scatter_channels",
    )(*far(field, filter_real, filter_imag))
    got = exchange(sent)
    coef, sent = pl.pallas_call(
        functools.partial(analysis_kernel, polar_count),
        in_specs=[vmem] * 5,
        out_specs=[vmem] * 2,
        out_shape=[pltpu.VMEM((devices, count, LANES), jnp.float32), block],
        scratch_shapes=[pltpu.VMEM((count * orders, LANES), jnp.float32)],
        compiler_params=pltpu.CompilerParams(vmem_limit_bytes=8 * MIB),
        name="analysis",
    )(*near(got, *split_constant(forward), *split_constant(analyse)))
    got = exchange(sent)
    sent = pl.pallas_call(
        filter_kernel,
        in_specs=[vmem] * 2,
        out_specs=vmem,
        out_shape=block,
        scratch_shapes=[pltpu.VMEM((devices * dense, LANES), jnp.float32)],
        compiler_params=pltpu.CompilerParams(vmem_limit_bytes=8 * MIB),
        name="channel_filter",
    )(*near(got, own_filter))
    got = exchange(sent)
    sent = pl.pallas_call(
        functools.partial(synthesis_kernel, polar_count),
        in_specs=[vmem] * 6,
        out_specs=vmem,
        out_shape=block,
        scratch_shapes=[
            pltpu.VMEM((devices, 8, LANES), jnp.float32),
            pltpu.VMEM((devices, count, LANES), jnp.float32),
            pltpu.VMEM((orders * count, LANES), jnp.float32),
        ],
        compiler_params=pltpu.CompilerParams(vmem_limit_bytes=8 * MIB),
        name="synthesis",
    )(*near(got, coef, *split_constant(backward), *split_constant(synthesise)))
    got = exchange(sent)
    mixed = pl.pallas_call(
        mlp_kernel,
        in_specs=[vmem] * 4,
        out_specs=pl.BlockSpec(memory_space=pl.ANY),
        out_shape=jax.ShapeDtypeStruct((1, lon_out, lat_out, channels), jnp.float32),
        scratch_shapes=[
            pltpu.VMEM((channels // LANES, lat_out * lon_out, LANES), jnp.float32),
            pltpu.VMEM((lon_out, lat_out, channels), jnp.float32),
            pltpu.SemaphoreType.DMA((2,)),
        ],
        compiler_params=pltpu.CompilerParams(vmem_limit_bytes=8 * MIB),
        name="mlp",
    )(*near(got, norm_gain, w_in, w_out))
    return mixed.transpose(0, 2, 1, 3)


def per_device(field, filter_real, filter_imag, norm_gain, w_in, w_out):
    polar_count, azimuth_count = lax.axis_size("polar"), lax.axis_size("azimuth")
    plan = jointly if joint_fits(field, filter_real, polar_count, azimuth_count) else by_axes
    return plan(field, filter_real, filter_imag, norm_gain, w_in, w_out)


def solution(mesh):
    in_specs = (
        P(None, "polar", "azimuth", None),
        P("azimuth", None, None),
        P("azimuth", None, None),
        P(),
        P(),
        P(),
    )
    out_specs = P(None, "polar", "azimuth", None)
    return jax.shard_map(
        per_device, mesh=mesh, in_specs=in_specs, out_specs=out_specs, check_vma=False
    )
```

```python
import functools
import math

import jax
import jax.numpy as jnp
import numpy as np
from jax import lax
from jax.experimental import pallas as pl
from jax.experimental.pallas import tpu as pltpu
from jax.sharding import PartitionSpec as P


def legendre(nodes, degrees, orders):
    cosines, sines = np.cos(nodes)[None, :], np.sin(nodes)[None, :]
    mode = np.arange(orders, dtype=np.float64)[:, None]
    counter = np.arange(1, orders + 1, dtype=np.float64)
    ratios = np.log((2.0 * counter - 1.0) / (2.0 * counter))
    product_log = np.concatenate([[0.0], np.cumsum(ratios)])[:orders, None]
    diagonal = np.exp(
        0.5 * (np.log((2.0 * mode + 1.0) / (4.0 * math.pi)) + product_log) + mode * np.log(sines)
    )
    newest, older = np.zeros_like(diagonal), np.zeros_like(diagonal)
    stacked = []
    for degree in range(degrees):
        lower = np.where(degree > mode, degree * degree - mode * mode, 1.0)
        factor_a = np.sqrt(max(4.0 * degree * degree - 1.0, 0.0) / lower)
        factor_b = np.sqrt(
            np.maximum((degree - 1.0) ** 2 - mode**2, 0.0) / max(4.0 * (degree - 1.0) ** 2 - 1.0, 1.0)
        )
        recurred = factor_a * (cosines * newest - factor_b * older)
        second = np.sqrt(2.0 * mode + 3.0) * cosines * newest
        value = np.where(
            degree == mode,
            diagonal,
            np.where(degree == mode + 1.0, second, np.where(degree > mode + 1.0, recurred, 0.0)),
        )
        stacked.append(value)
        newest, older = value, newest
    return np.stack(stacked, axis=1)


def colatitudes(count):
    return math.pi * (np.arange(count) + 0.5) / count


def fourier_table(points, mode_ids, halves, weights):
    angle = 2.0 * math.pi / points * (np.arange(points)[:, None] * mode_ids[None, :] % points)
    return np.where(
        halves[None, :] == 0, weights[None, :] * np.cos(angle), -weights[None, :] * np.sin(angle)
    )


def by_axes(field, filter_real, filter_imag, norm_gain, w_in, w_out):
    high = lax.Precision.HIGHEST
    samples, lat_rows, lon_cols, channels = field.shape
    polar_count = lax.axis_size("polar")
    azimuth_count = lax.axis_size("azimuth")
    fine_lat = lat_rows * polar_count
    fine_lon = lon_cols * azimuth_count
    coarse_lat = fine_lat // 2
    coarse_lon = fine_lon // 2
    orders = coarse_lon // 2
    order_piece = orders // polar_count
    chan_slice = channels // azimuth_count
    columns_all = np.arange(2 * orders)
    halves = columns_all // order_piece % 2
    mode_ids = columns_all // (2 * order_piece) * order_piece + columns_all % order_piece
    twofold = np.where(mode_ids == 0, 1.0, 2.0)
    forward_table = jnp.asarray(
        fourier_table(fine_lon, mode_ids, halves, np.ones(2 * orders)), jnp.float32
    )
    inverse_table = jnp.asarray(fourier_table(coarse_lon, mode_ids, halves, twofold).T, jnp.float32)
    polar_index = lax.axis_index("polar")
    fine_nodes = colatitudes(fine_lat)
    quadrature = math.pi / fine_lat * np.sin(fine_nodes) * (2.0 * math.pi / fine_lon)
    all_fine = legendre(fine_nodes, coarse_lat, orders) * quadrature
    all_coarse = legendre(colatitudes(coarse_lat), coarse_lat, orders)
    own_orders = lambda table: lax.dynamic_slice_in_dim(
        jnp.asarray(table, jnp.float32), polar_index * order_piece, order_piece, 0
    )
    table_fine = own_orders(all_fine)
    table_coarse = own_orders(all_coarse)
    moved = lax.all_to_all(field, "azimuth", split_axis=3, concat_axis=2, tiled=True)
    spectrum = jnp.einsum("bijc,jk->bick", moved, forward_table, precision=high)
    by_order = lax.all_to_all(spectrum, "polar", split_axis=3, concat_axis=1, tiled=True)
    by_order = by_order.reshape(samples, fine_lat, chan_slice, 2, order_piece)
    coef = jnp.einsum("kli,bicpk->blcpk", table_fine, by_order, precision=high)
    degree_block = lax.all_to_all(coef, "azimuth", split_axis=1, concat_axis=2, tiled=True)
    block_re = degree_block[:, :, :, 0]
    block_im = degree_block[:, :, :, 1]
    out_re = jnp.einsum("lco,blck->blok", filter_real, block_re, precision=high) - jnp.einsum(
        "lco,blck->blok", filter_imag, block_im, precision=high
    )
    out_im = jnp.einsum("lco,blck->blok", filter_real, block_im, precision=high) + jnp.einsum(
        "lco,blck->blok", filter_imag, block_re, precision=high
    )
    mixed_spec = jnp.stack([out_re, out_im], axis=3)
    filtered = lax.all_to_all(mixed_spec, "azimuth", split_axis=2, concat_axis=1, tiled=True)
    both_fields = jnp.concatenate([coef, filtered], axis=2)
    grid_modes = jnp.einsum("kli,blcpk->bicpk", table_coarse, both_fields, precision=high)
    grid_modes = grid_modes.reshape(samples, coarse_lat, 2 * chan_slice, 2 * order_piece)
    row_block = lax.all_to_all(grid_modes, "polar", split_axis=1, concat_axis=3, tiled=True)
    values = jnp.einsum("bick,kj->bijc", row_block, inverse_table, precision=high)
    state_split = (
        jax.nn.gelu(values[..., chan_slice:], approximate=False) + values[..., :chan_slice]
    )
    state = lax.all_to_all(state_split, "azimuth", split_axis=2, concat_axis=3, tiled=True)
    center = jnp.mean(state, axis=-1, keepdims=True)
    spread = jnp.mean((state - center) ** 2, axis=-1, keepdims=True)
    normed = ((state - center) * lax.rsqrt(spread + 1e-05) * norm_gain).astype(jnp.bfloat16)
    flat = normed.reshape(-1, channels)
    hidden = jax.nn.gelu(
        jnp.dot(flat, w_in, preferred_element_type=jnp.float32), approximate=False
    ).astype(jnp.bfloat16)
    update = jnp.dot(hidden, w_out, preferred_element_type=jnp.float32)
    return state + update.reshape(state.shape)


LANES = 128
BOTH = ("polar", "azimuth")
MIB = 1024 * 1024


def split_bf16(table):
    high = table.astype(jnp.bfloat16)
    return high, (table - high.astype(jnp.float32)).astype(jnp.bfloat16)


def split_constant(table):
    table = np.asarray(table, np.float32)
    high = table.astype(jnp.bfloat16)
    return jnp.asarray(high), jnp.asarray((table - high.astype(np.float32)).astype(jnp.bfloat16))


def dot(left, right):
    return jnp.dot(left, right, preferred_element_type=jnp.float32)


def dot3(left, right_high, right_low):
    rows = left.shape[0]
    left_high, left_low = split_bf16(left)
    both = dot(jnp.concatenate([left_high, left_low], axis=0), right_high)
    return both[:rows] + both[rows:] + dot(left_high, right_low)


def swap(blocks, step, before=0, after=0, begin=True, finish=True):
    count = len(blocks)
    axis = len(blocks[0].shape) - 1

    def turn(block, fields, lanes, wanted):
        amount = (fields * step * wanted + lanes) % LANES
        return block if isinstance(amount, int) and amount == 0 else pltpu.roll(block, amount, axis)

    place = lax.broadcasted_iota(jnp.int32, blocks[0].shape, axis) // step
    turned = [turn(blocks[-index % count], -index % count, before, begin) for index in range(count)]
    shift = 1
    while shift < count:
        take = (place & shift) != 0
        turned = [
            jnp.where(take, turned[(index - shift) % count], turned[index]) for index in range(count)
        ]
        shift *= 2
    return [turn(block, -index, after, finish) for index, block in enumerate(turned)]


def own_index(azimuth_count):
    return lax.axis_index("polar") * azimuth_count + lax.axis_index("azimuth")


QUAD = 4
FIELD = LANES // QUAD


def gelu(values):
    return 0.5 * values * (1.0 + lax.erf(values * math.sqrt(0.5)))


def scatter_kernel(field, real, imag, sent, own_filter, buf, sems, filter_sems):
    devices, rows, channels = sent.shape
    copies = []
    for row in range(rows // 8):
        copy = pltpu.make_async_copy(
            field.at[0, :, pl.ds(8 * row, 8), :], buf.at[row], sems.at[row]
        )
        copy.start()
        copies.append(copy)
    degrees = own_filter.shape[1]
    start = lax.axis_index("polar") * degrees
    filter_copies = [
        pltpu.make_async_copy(
            part.at[pl.ds(start, degrees)], own_filter.at[index], filter_sems.at[index]
        )
        for index, part in enumerate((real, imag))
    ]
    for copy in filter_copies:
        copy.start()
    for row, copy in enumerate(copies):
        copy.wait()
        for tile in range(channels // LANES):
            lanes = pl.ds(tile * LANES, LANES)
            blocks = swap([buf[row, lat, :, lanes] for lat in range(devices)], 1, finish=False)
            for device in range(devices):
                sent[device, pl.ds(8 * row, 8), lanes] = blocks[device]
    for copy in filter_copies:
        copy.wait()


def analysis_kernel(
    polar_count, got, four_high, four_low, leg_high, leg_low, coef, sent, rows
):
    devices, lon_cols, width = got.shape
    azimuth_count = devices // polar_count
    modes = four_high.shape[0]
    orders = modes // 2
    four = jnp.concatenate([four_high[...], four_low[...]], axis=0)
    tiles = width // LANES
    own_turn = LANES - own_index(azimuth_count)
    wide = []
    for polar in range(polar_count):
        block = got[pl.ds(polar * azimuth_count, azimuth_count)]
        block_high, block_low = split_bf16(block.reshape(azimuth_count * lon_cols, width))
        both = dot(four, block_high)
        wide.append(both[:modes] + both[modes:] + dot(four[:modes], block_low))
    for tile in range(tiles):
        spectra = [spectrum[:, tile * LANES : (tile + 1) * LANES] for spectrum in wide]
        for quad, spectrum in enumerate(swap(spectra, FIELD, before=own_turn)):
            rows[pl.ds((tile * polar_count + quad) * modes, modes), :] = spectrum
    count = 2 * tiles * polar_count
    extra = orders - devices
    lane = lax.broadcasted_iota(jnp.int32, (count, LANES), 1)
    for order in range(extra):
        own = [
            rows[pl.ds(row, count, stride=orders), :]
            for row in (order, order + extra, devices + order)
        ]
        values = dot3(jnp.concatenate(own, axis=0), leg_high[order], leg_low[order])
        for part in range(2):
            lanes = slice(part * LANES, (part + 1) * LANES)
            index = order + part * extra
            coef[index] = jnp.where(
                ((lane - index) & (LANES - 1)) < LANES // 2,
                values[part * count : (part + 1) * count, lanes],
                values[2 * count :, lanes],
            )
    pack_by_degree(coef, sent)


def pack_by_degree(coef, sent):
    devices, count, _ = coef.shape
    dense, tail = count * 3 // 4, count // 4
    used = LANES * 3 // 4
    for row in range(0, count, 8):
        blocks = swap([coef[order, pl.ds(row, 8), :] for order in range(devices)], 1, begin=False)
        head = min(max(dense - row, 0), 8)
        for device in range(devices):
            start = device * dense
            if head:
                sent[pl.ds(start + row, head), pl.ds(0, used)] = blocks[device][:head, :used]
            if head < 8:
                skip = max(row - dense, 0)
                for part in range(3):
                    moved = pltpu.roll(blocks[device], used - 32 * part, 1)
                    sent[pl.ds(start + tail * part + skip, 8 - head), pl.ds(used, LANES - used)] = moved[
                        head:, used:
                    ]


def filter_kernel(got, own_filter, sent, turned):
    _, degrees, channels, _ = own_filter.shape
    tiles = channels // LANES
    count = 8 * tiles
    dense, tail = count * 3 // 4, count // 4
    devices = sent.shape[0] // dense
    quarter = lax.broadcasted_iota(jnp.int32, (devices, LANES), 1) // 32
    spectra = []
    for half in range(2):
        parts = []
        for own in range(count // 2):
            row = 2 * own + half
            load = lambda start: got[pl.ds(start, devices, stride=dense), :]
            if row < dense:
                parts.append(load(row))
                continue
            folded = [
                pltpu.roll(load(tail * part + row - dense), 32 * (part + 1), 1) for part in range(3)
            ]
            parts.append(
                jnp.where(quarter == 0, folded[0], jnp.where(quarter == 1, folded[1], folded[2]))
            )
        spectra.append(jnp.concatenate(parts, axis=0).T)
    results = [[None] * 4 for _ in range(2)]
    for degree in range(degrees):
        places = [(32 * degree, 32), (64 + 16 * degree, 16)]
        own = jnp.concatenate(
            [spectra[half][start : start + size] for half in range(2) for start, size in places],
            axis=0,
        )
        parts = [split_bf16(own_filter[part, degree]) for part in range(2)]
        both = dot3(own, *(jnp.concatenate(pair, axis=1) for pair in zip(*parts)))
        by_real, by_imag = both[:, :channels], both[:, channels:]
        size = 48
        outs = (by_real[:size] - by_imag[size:], by_real[size:] + by_imag[:size])
        for half in range(2):
            results[half][degree] = outs[half][:32]
            results[half][2 + degree] = outs[half][32:]
    across = []
    for half in range(2):
        padding = jnp.zeros((32, channels), jnp.float32)
        across.append(jnp.concatenate(results[half] + [padding], axis=0).T)
    rows = [
        across[row % 2][row // 2 * devices : (row // 2 + 1) * devices] for row in range(count)
    ]
    for row in range(dense):
        part = row // tail
        folded = pltpu.roll(rows[dense + row % tail], 96 - 32 * part, 1)
        turned[pl.ds(row * devices, devices), :] = jnp.where(quarter < 3, rows[row], folded)
    for device in range(devices):
        sent[pl.ds(device * dense, dense), :] = turned[pl.ds(device, dense, stride=devices), :]


def synthesis_kernel(
    polar_count, got, coef, four_high, four_low, leg_high, leg_low, sent, tails, back, modes_buf
):
    devices, count, _ = coef.shape
    dense, tail = count * 3 // 4, count // 4
    azimuth_count = devices // polar_count
    orders = four_high.shape[1] // 2
    extra = orders - devices
    quarter = lax.broadcasted_iota(jnp.int32, (tail, LANES), 1) // 32
    for device in range(devices):
        folded = [
            pltpu.roll(got[pl.ds(device * dense + tail * part, tail), :], 32 * (part + 1), 1)
            for part in range(3)
        ]
        tails[device, pl.ds(8 - tail, tail), :] = jnp.where(
            quarter == 0, folded[0], jnp.where(quarter == 1, folded[1], folded[2])
        )
        tails[device, pl.ds(0, 8 - tail), :] = got[
            pl.ds(device * dense + count - 8, 8 - tail), :
        ]
    for row in range(0, count, 8):
        if row + 8 < count:
            blocks = [got[pl.ds(device * dense + row, 8), :] for device in range(devices)]
        else:
            blocks = [tails[device] for device in range(devices)]
        blocks = swap(blocks, 1, finish=False)
        for order in range(devices):
            back[order, pl.ds(row, 8), :] = blocks[order]
    keep = (lax.broadcasted_iota(jnp.int32, (count, LANES), 1) & 16) == 0
    for order in range(devices):
        both = jnp.concatenate([coef[order], back[order]], axis=0)
        values = dot3(both, leg_high[order], leg_low[order])
        merged = [
            jnp.where(
                keep,
                values[:count, part * LANES : (part + 1) * LANES],
                values[count:, part * LANES : (part + 1) * LANES],
            )
            for part in range(2)
        ]
        modes_buf[pl.ds(order * count, count), :] = merged[0]
        later = devices + order % extra
        if order < extra:
            modes_buf[pl.ds(later * count, count), :] = merged[1]
        else:
            modes_buf[pl.ds(later * count, count), :] += merged[1]
    four = jnp.concatenate([four_high[...], four_low[...]], axis=0)
    points = four_high.shape[0]
    half = points // 2
    keep = (lax.broadcasted_iota(jnp.int32, (half, LANES), 1) & 16) == 0
    for tile in range(count // 8):
        states = []
        for quad in range(4):
            row = 2 * (4 * tile + quad)
            modes = jnp.concatenate(
                [modes_buf[pl.ds(row + part, orders, stride=count), :] for part in range(2)], axis=0
            )
            modes_high, modes_low = split_bf16(modes)
            both = dot(four, modes_high)
            values = both[:points] + both[points:] + dot(four[:points], modes_low)
            first, second = values[:half], values[half:]
            skip = jnp.where(keep, first, pltpu.roll(second, 16, 1))
            branch = jnp.where(keep, pltpu.roll(first, LANES - 16, 1), second)
            states.append(gelu(branch) + skip)
        for polar, state in enumerate(swap(states, FIELD, after=own_index(azimuth_count))):
            for azimuth in range(azimuth_count):
                device = polar * azimuth_count + azimuth
                sent[pl.ds(device * dense + tail * tile, tail), :] = state[
                    tail * azimuth : tail * (azimuth + 1)
                ]


def mlp_kernel(got, gain, w_in, w_out, mixed, state, result, sems):
    tiles = state.shape[0]
    _, lon_cols, lat_rows, _ = mixed.shape
    part = lon_cols // 2
    devices = got.shape[0] // (tiles * part)
    for tile in range(tiles):
        blocks = swap(
            [
                got[pl.ds((device * tiles + tile) * part, part), :]
                for device in range(devices)
            ],
            1,
            begin=False,
        )
        for device in range(devices):
            state[tile, pl.ds(part * device, part), :] = blocks[device]
    value = jnp.concatenate([state[tile] for tile in range(tiles)], axis=1)
    center = jnp.mean(value, axis=-1, keepdims=True)
    spread = jnp.mean((value - center) ** 2, axis=-1, keepdims=True)
    normed = (value - center) * lax.rsqrt(spread + 1e-05) * gain[...][None, :]
    hidden = gelu(dot(normed.astype(jnp.bfloat16), w_in[...])).astype(jnp.bfloat16)
    size = part * lat_rows
    copies = []
    for top in range(2):
        cells = slice(top * size, (top + 1) * size)
        update = value[cells] + dot(hidden[cells], w_out[...])
        for tile in range(tiles):
            state[tile, cells, :] = update[:, tile * LANES : (tile + 1) * LANES]
            for lon in range(part):
                result[top * part + lon, :, pl.ds(tile * LANES, LANES)] = state[
                    tile, pl.ds(top * size + lon, lat_rows, stride=part), :
                ]
        lons = pl.ds(top * part, part)
        copies.append(pltpu.make_async_copy(result.at[lons], mixed.at[0, lons], sems.at[top]))
        copies[-1].start()
    for copy in copies:
        copy.wait()


def joint_fits(field, filter_real, polar_count, azimuth_count):
    samples, lat_rows, lon_cols, channels = field.shape
    devices = polar_count * azimuth_count
    orders = lon_cols * azimuth_count // 4
    return (
        samples == 1
        and devices == 32
        and polar_count == 4
        and lat_rows == 32
        and lon_cols == 24
        and channels == 3 * LANES
        and filter_real.shape[0] == 2 * polar_count
        and 2 * orders == 3 * devices
    )


def jointly(field, filter_real, filter_imag, norm_gain, w_in, w_out):
    _, lat_rows, lon_cols, channels = field.shape
    polar_count = lax.axis_size("polar")
    azimuth_count = lax.axis_size("azimuth")
    devices = polar_count * azimuth_count
    fine_lat, fine_lon = lat_rows * polar_count, lon_cols * azimuth_count
    coarse_lat, coarse_lon = fine_lat // 2, fine_lon // 2
    orders = coarse_lon // 2
    extra = orders - devices
    count = 2 * channels // devices
    degrees_here = coarse_lat // devices
    lat_out, lon_out = coarse_lat // polar_count, coarse_lon // azimuth_count

    mode_ids = np.tile(np.arange(orders), 2)
    halves = np.repeat(np.arange(2), orders)
    forward = fourier_table(fine_lon, mode_ids, halves, np.ones(2 * orders)).T
    twofold = np.where(mode_ids == 0, 1.0, 2.0)
    inverse = fourier_table(coarse_lon, mode_ids, halves, twofold)
    backward = inverse.reshape(azimuth_count, 2, lon_out // 2, 2 * orders)
    backward = backward.transpose(1, 0, 2, 3).reshape(-1, 2 * orders)

    fine_nodes = colatitudes(fine_lat)
    quadrature = math.pi / fine_lat * np.sin(fine_nodes) * (2.0 * math.pi / fine_lon)
    fine = legendre(fine_nodes, coarse_lat, orders) * quadrature
    coarse = legendre(colatitudes(coarse_lat), coarse_lat, orders)
    owner = np.arange(devices)
    degree = (
        owner % azimuth_count * (coarse_lat // azimuth_count) + owner // azimuth_count * degrees_here
    )
    degree = (degree[None, :] + np.arange(degrees_here)[:, None]).reshape(-1)
    lane = np.arange(LANES)
    lat_fine = lane
    lat_coarse = lane // 32 * lat_out + lane % 16
    fine = fine[:, degree][:, :, lat_fine].transpose(0, 2, 1)
    coarse = coarse[:, degree][:, :, lat_coarse]
    analyse = np.zeros((extra, LANES, 2, 4, devices))
    synthesise = np.zeros((devices, 4, devices, 2, LANES))
    for order in range(devices):
        later, which = devices + order % extra, order // extra
        own = slice(which * devices, (which + 1) * devices)
        analyse[order % extra, :, which, :2] = fine[order].reshape(LANES, 2, devices)
        analyse[order % extra, :, which, 2] = fine[later][:, own]
        synthesise[order, :2, :, 0] = coarse[order].reshape(2, devices, LANES)
        synthesise[order, 2, :, 1] = coarse[later][own]
    analyse = analyse.reshape(extra, LANES, 2 * LANES)
    synthesise = synthesise.reshape(devices, LANES, 2 * LANES)
    for order in range(devices):
        columns = slice(order // extra * LANES, (order // extra + 1) * LANES)
        analyse[order % extra, :, columns] = np.roll(analyse[order % extra, :, columns], order, axis=1)
        synthesise[order] = np.roll(synthesise[order], order, axis=0)

    vmem = pl.BlockSpec(memory_space=pltpu.VMEM)
    hbm = pl.BlockSpec(memory_space=pltpu.HBM)
    dense = count * 3 // 4
    block = pltpu.VMEM((devices * dense, LANES), jnp.float32)

    def exchange(blocks):
        split = blocks.reshape((devices, -1, 2, LANES)) if blocks.ndim == 2 else blocks
        moved = lax.all_to_all(split, BOTH, split_axis=0, concat_axis=0, tiled=True)
        return moved.reshape(blocks.shape)

    def near(*arrays):
        return [pltpu.with_memory_space_constraint(array, pltpu.VMEM) for array in arrays]

    def far(*arrays):
        return [pltpu.with_memory_space_constraint(array, pltpu.HBM) for array in arrays]

    parts = lon_cols // 8
    sent, own_filter = pl.pallas_call(
        scatter_kernel,
        in_specs=[hbm] * 3,
        out_specs=[vmem] * 2,
        out_shape=[
            pltpu.VMEM((devices, lon_cols, channels), jnp.float32),
            pltpu.VMEM((2, degrees_here, channels, channels), jnp.float32),
        ],
        scratch_shapes=[
            pltpu.VMEM((parts, lat_rows, 8, channels), jnp.float32),
            pltpu.SemaphoreType.DMA((parts,)),
            pltpu.SemaphoreType.DMA((2,)),
        ],
        compiler_params=pltpu.CompilerParams(vmem_limit_bytes=8 * MIB),
        name="scatter_channels",
    )(*far(field, filter_real, filter_imag))
    got = exchange(sent)
    coef, sent = pl.pallas_call(
        functools.partial(analysis_kernel, polar_count),
        in_specs=[vmem] * 5,
        out_specs=[vmem] * 2,
        out_shape=[pltpu.VMEM((devices, count, LANES), jnp.float32), block],
        scratch_shapes=[pltpu.VMEM((count * orders, LANES), jnp.float32)],
        compiler_params=pltpu.CompilerParams(vmem_limit_bytes=8 * MIB),
        name="analysis",
    )(*near(got, *split_constant(forward), *split_constant(analyse)))
    got = exchange(sent)
    sent = pl.pallas_call(
        filter_kernel,
        in_specs=[vmem] * 2,
        out_specs=vmem,
        out_shape=block,
        scratch_shapes=[pltpu.VMEM((devices * dense, LANES), jnp.float32)],
        compiler_params=pltpu.CompilerParams(vmem_limit_bytes=8 * MIB),
        name="channel_filter",
    )(*near(got, own_filter))
    got = exchange(sent)
    sent = pl.pallas_call(
        functools.partial(synthesis_kernel, polar_count),
        in_specs=[vmem] * 6,
        out_specs=vmem,
        out_shape=block,
        scratch_shapes=[
            pltpu.VMEM((devices, 8, LANES), jnp.float32),
            pltpu.VMEM((devices, count, LANES), jnp.float32),
            pltpu.VMEM((orders * count, LANES), jnp.float32),
        ],
        compiler_params=pltpu.CompilerParams(vmem_limit_bytes=8 * MIB),
        name="synthesis",
    )(*near(got, coef, *split_constant(backward), *split_constant(synthesise)))
    got = exchange(sent)
    mixed = pl.pallas_call(
        mlp_kernel,
        in_specs=[vmem] * 4,
        out_specs=pl.BlockSpec(memory_space=pl.ANY),
        out_shape=jax.ShapeDtypeStruct((1, lon_out, lat_out, channels), jnp.float32),
        scratch_shapes=[
            pltpu.VMEM((channels // LANES, lat_out * lon_out, LANES), jnp.float32),
            pltpu.VMEM((lon_out, lat_out, channels), jnp.float32),
            pltpu.SemaphoreType.DMA((2,)),
        ],
        compiler_params=pltpu.CompilerParams(vmem_limit_bytes=8 * MIB),
        name="mlp",
    )(*near(got, norm_gain, w_in, w_out))
    return mixed.transpose(0, 2, 1, 3)


def per_device(field, filter_real, filter_imag, norm_gain, w_in, w_out):
    polar_count, azimuth_count = lax.axis_size("polar"), lax.axis_size("azimuth")
    plan = jointly if joint_fits(field, filter_real, polar_count, azimuth_count) else by_axes
    return plan(field, filter_real, filter_imag, norm_gain, w_in, w_out)


def solution(mesh):
    in_specs = (
        P(None, "polar", "azimuth", None),
        P("azimuth", None, None),
        P("azimuth", None, None),
        P(),
        P(),
        P(),
    )
    out_specs = P(None, "polar", "azimuth", None)
    return jax.shard_map(
        per_device, mesh=mesh, in_specs=in_specs, out_specs=out_specs, check_vma=False
    )
```

```python
import functools
import math

import jax
import jax.numpy as jnp
import numpy as np
from jax import lax
from jax.experimental import pallas as pl
from jax.experimental.pallas import tpu as pltpu
from jax.sharding import PartitionSpec as P


def legendre(nodes, degrees, orders):
    cosines, sines = np.cos(nodes)[None, :], np.sin(nodes)[None, :]
    mode = np.arange(orders, dtype=np.float64)[:, None]
    counter = np.arange(1, orders + 1, dtype=np.float64)
    ratios = np.log((2.0 * counter - 1.0) / (2.0 * counter))
    product_log = np.concatenate([[0.0], np.cumsum(ratios)])[:orders, None]
    diagonal = np.exp(
        0.5 * (np.log((2.0 * mode + 1.0) / (4.0 * math.pi)) + product_log) + mode * np.log(sines)
    )
    newest, older = np.zeros_like(diagonal), np.zeros_like(diagonal)
    stacked = []
    for degree in range(degrees):
        lower = np.where(degree > mode, degree * degree - mode * mode, 1.0)
        factor_a = np.sqrt(max(4.0 * degree * degree - 1.0, 0.0) / lower)
        factor_b = np.sqrt(
            np.maximum((degree - 1.0) ** 2 - mode**2, 0.0) / max(4.0 * (degree - 1.0) ** 2 - 1.0, 1.0)
        )
        recurred = factor_a * (cosines * newest - factor_b * older)
        second = np.sqrt(2.0 * mode + 3.0) * cosines * newest
        value = np.where(
            degree == mode,
            diagonal,
            np.where(degree == mode + 1.0, second, np.where(degree > mode + 1.0, recurred, 0.0)),
        )
        stacked.append(value)
        newest, older = value, newest
    return np.stack(stacked, axis=1)


def colatitudes(count):
    return math.pi * (np.arange(count) + 0.5) / count


def fourier_table(points, mode_ids, halves, weights):
    angle = 2.0 * math.pi / points * (np.arange(points)[:, None] * mode_ids[None, :] % points)
    return np.where(
        halves[None, :] == 0, weights[None, :] * np.cos(angle), -weights[None, :] * np.sin(angle)
    )


def by_axes(field, filter_real, filter_imag, norm_gain, w_in, w_out):
    high = lax.Precision.HIGHEST
    samples, lat_rows, lon_cols, channels = field.shape
    polar_count = lax.axis_size("polar")
    azimuth_count = lax.axis_size("azimuth")
    fine_lat = lat_rows * polar_count
    fine_lon = lon_cols * azimuth_count
    coarse_lat = fine_lat // 2
    coarse_lon = fine_lon // 2
    orders = coarse_lon // 2
    order_piece = orders // polar_count
    chan_slice = channels // azimuth_count
    columns_all = np.arange(2 * orders)
    halves = columns_all // order_piece % 2
    mode_ids = columns_all // (2 * order_piece) * order_piece + columns_all % order_piece
    twofold = np.where(mode_ids == 0, 1.0, 2.0)
    forward_table = jnp.asarray(
        fourier_table(fine_lon, mode_ids, halves, np.ones(2 * orders)), jnp.float32
    )
    inverse_table = jnp.asarray(fourier_table(coarse_lon, mode_ids, halves, twofold).T, jnp.float32)
    polar_index = lax.axis_index("polar")
    fine_nodes = colatitudes(fine_lat)
    quadrature = math.pi / fine_lat * np.sin(fine_nodes) * (2.0 * math.pi / fine_lon)
    all_fine = legendre(fine_nodes, coarse_lat, orders) * quadrature
    all_coarse = legendre(colatitudes(coarse_lat), coarse_lat, orders)
    own_orders = lambda table: lax.dynamic_slice_in_dim(
        jnp.asarray(table, jnp.float32), polar_index * order_piece, order_piece, 0
    )
    table_fine = own_orders(all_fine)
    table_coarse = own_orders(all_coarse)
    moved = lax.all_to_all(field, "azimuth", split_axis=3, concat_axis=2, tiled=True)
    spectrum = jnp.einsum("bijc,jk->bick", moved, forward_table, precision=high)
    by_order = lax.all_to_all(spectrum, "polar", split_axis=3, concat_axis=1, tiled=True)
    by_order = by_order.reshape(samples, fine_lat, chan_slice, 2, order_piece)
    coef = jnp.einsum("kli,bicpk->blcpk", table_fine, by_order, precision=high)
    degree_block = lax.all_to_all(coef, "azimuth", split_axis=1, concat_axis=2, tiled=True)
    block_re = degree_block[:, :, :, 0]
    block_im = degree_block[:, :, :, 1]
    out_re = jnp.einsum("lco,blck->blok", filter_real, block_re, precision=high) - jnp.einsum(
        "lco,blck->blok", filter_imag, block_im, precision=high
    )
    out_im = jnp.einsum("lco,blck->blok", filter_real, block_im, precision=high) + jnp.einsum(
        "lco,blck->blok", filter_imag, block_re, precision=high
    )
    mixed_spec = jnp.stack([out_re, out_im], axis=3)
    filtered = lax.all_to_all(mixed_spec, "azimuth", split_axis=2, concat_axis=1, tiled=True)
    both_fields = jnp.concatenate([coef, filtered], axis=2)
    grid_modes = jnp.einsum("kli,blcpk->bicpk", table_coarse, both_fields, precision=high)
    grid_modes = grid_modes.reshape(samples, coarse_lat, 2 * chan_slice, 2 * order_piece)
    row_block = lax.all_to_all(grid_modes, "polar", split_axis=1, concat_axis=3, tiled=True)
    values = jnp.einsum("bick,kj->bijc", row_block, inverse_table, precision=high)
    state_split = (
        jax.nn.gelu(values[..., chan_slice:], approximate=False) + values[..., :chan_slice]
    )
    state = lax.all_to_all(state_split, "azimuth", split_axis=2, concat_axis=3, tiled=True)
    center = jnp.mean(state, axis=-1, keepdims=True)
    spread = jnp.mean((state - center) ** 2, axis=-1, keepdims=True)
    normed = ((state - center) * lax.rsqrt(spread + 1e-05) * norm_gain).astype(jnp.bfloat16)
    flat = normed.reshape(-1, channels)
    hidden = jax.nn.gelu(
        jnp.dot(flat, w_in, preferred_element_type=jnp.float32), approximate=False
    ).astype(jnp.bfloat16)
    update = jnp.dot(hidden, w_out, preferred_element_type=jnp.float32)
    return state + update.reshape(state.shape)


LANES = 128
BOTH = ("polar", "azimuth")
MIB = 1024 * 1024


def split_bf16(table):
    high = table.astype(jnp.bfloat16)
    return high, (table - high.astype(jnp.float32)).astype(jnp.bfloat16)


def split_constant(table):
    table = np.asarray(table, np.float32)
    high = table.astype(jnp.bfloat16)
    return jnp.asarray(high), jnp.asarray((table - high.astype(np.float32)).astype(jnp.bfloat16))


def dot(left, right):
    return jnp.dot(left, right, preferred_element_type=jnp.float32)


def dot3(left, right_high, right_low):
    rows = left.shape[0]
    left_high, left_low = split_bf16(left)
    both = dot(jnp.concatenate([left_high, left_low], axis=0), right_high)
    return both[:rows] + both[rows:] + dot(left_high, right_low)


def swap(blocks, step, before=0, after=0, begin=True, finish=True):
    count = len(blocks)
    axis = len(blocks[0].shape) - 1

    def turn(block, fields, lanes, wanted):
        amount = (fields * step * wanted + lanes) % LANES
        return block if isinstance(amount, int) and amount == 0 else pltpu.roll(block, amount, axis)

    place = lax.broadcasted_iota(jnp.int32, blocks[0].shape, axis) // step
    turned = [turn(blocks[-index % count], -index % count, before, begin) for index in range(count)]
    shift = 1
    while shift < count:
        take = (place & shift) != 0
        turned = [
            jnp.where(take, turned[(index - shift) % count], turned[index]) for index in range(count)
        ]
        shift *= 2
    return [turn(block, -index, after, finish) for index, block in enumerate(turned)]


def own_index(azimuth_count):
    return lax.axis_index("polar") * azimuth_count + lax.axis_index("azimuth")


QUAD = 4
FIELD = LANES // QUAD


def gelu(values):
    return 0.5 * values * (1.0 + lax.erf(values * math.sqrt(0.5)))


def scatter_kernel(field, real, imag, sent, own_filter, buf, sems, filter_sems):
    devices, rows, channels = sent.shape
    copies = []
    for row in range(rows // 8):
        copy = pltpu.make_async_copy(
            field.at[0, :, pl.ds(8 * row, 8), :], buf.at[row], sems.at[row]
        )
        copy.start()
        copies.append(copy)
    degrees = own_filter.shape[1]
    start = lax.axis_index("polar") * degrees
    filter_copies = [
        pltpu.make_async_copy(
            part.at[pl.ds(start, degrees)], own_filter.at[index], filter_sems.at[index]
        )
        for index, part in enumerate((real, imag))
    ]
    for copy in filter_copies:
        copy.start()
    for row, copy in enumerate(copies):
        copy.wait()
        for tile in range(channels // LANES):
            lanes = pl.ds(tile * LANES, LANES)
            blocks = swap([buf[row, lat, :, lanes] for lat in range(devices)], 1, finish=False)
            for device in range(devices):
                sent[device, pl.ds(8 * row, 8), lanes] = blocks[device]
    for copy in filter_copies:
        copy.wait()


def analysis_kernel(
    polar_count, got, four_high, four_low, leg_high, leg_low, coef, sent, rows
):
    devices, lon_cols, width = got.shape
    azimuth_count = devices // polar_count
    modes = four_high.shape[0]
    orders = modes // 2
    four = jnp.concatenate([four_high[...], four_low[...]], axis=0)
    tiles = width // LANES
    own_turn = LANES - own_index(azimuth_count)
    wide = []
    for polar in range(polar_count):
        block = got[pl.ds(polar * azimuth_count, azimuth_count)]
        block_high, block_low = split_bf16(block.reshape(azimuth_count * lon_cols, width))
        both = dot(four, block_high)
        wide.append(both[:modes] + both[modes:] + dot(four[:modes], block_low))
    for tile in range(tiles):
        spectra = [spectrum[:, tile * LANES : (tile + 1) * LANES] for spectrum in wide]
        for quad, spectrum in enumerate(swap(spectra, FIELD, before=own_turn)):
            rows[pl.ds((tile * polar_count + quad) * modes, modes), :] = spectrum
    count = 2 * tiles * polar_count
    extra = orders - devices
    lane = lax.broadcasted_iota(jnp.int32, (count, LANES), 1)
    for order in range(extra):
        own = [
            rows[pl.ds(row, count, stride=orders), :]
            for row in (order, order + extra, devices + order)
        ]
        values = dot3(jnp.concatenate(own, axis=0), leg_high[order], leg_low[order])
        for part in range(2):
            lanes = slice(part * LANES, (part + 1) * LANES)
            index = order + part * extra
            coef[index] = jnp.where(
                ((lane - index) & (LANES - 1)) < LANES // 2,
                values[part * count : (part + 1) * count, lanes],
                values[2 * count :, lanes],
            )
    pack_by_degree(coef, sent)


def pack_by_degree(coef, sent):
    devices, count, _ = coef.shape
    dense, tail = count * 3 // 4, count // 4
    used = LANES * 3 // 4
    for row in range(0, count, 8):
        blocks = swap([coef[order, pl.ds(row, 8), :] for order in range(devices)], 1, begin=False)
        head = min(max(dense - row, 0), 8)
        for device in range(devices):
            start = device * dense
            if head:
                sent[pl.ds(start + row, head), pl.ds(0, used)] = blocks[device][:head, :used]
            if head < 8:
                skip = max(row - dense, 0)
                for part in range(3):
                    moved = pltpu.roll(blocks[device], used - 32 * part, 1)
                    sent[pl.ds(start + tail * part + skip, 8 - head), pl.ds(used, LANES - used)] = moved[
                        head:, used:
                    ]


def filter_kernel(got, own_filter, sent, turned):
    _, degrees, channels, _ = own_filter.shape
    tiles = channels // LANES
    count = 8 * tiles
    dense, tail = count * 3 // 4, count // 4
    devices = sent.shape[0] // dense
    quarter = lax.broadcasted_iota(jnp.int32, (devices, LANES), 1) // 32
    spectra = []
    for half in range(2):
        parts = []
        for own in range(count // 2):
            row = 2 * own + half
            load = lambda start: got[pl.ds(start, devices, stride=dense), :]
            if row < dense:
                parts.append(load(row))
                continue
            folded = [
                pltpu.roll(load(tail * part + row - dense), 32 * (part + 1), 1) for part in range(3)
            ]
            parts.append(
                jnp.where(quarter == 0, folded[0], jnp.where(quarter == 1, folded[1], folded[2]))
            )
        spectra.append(jnp.concatenate(parts, axis=0).T)
    results = [[None] * 4 for _ in range(2)]
    for degree in range(degrees):
        places = [(32 * degree, 32), (64 + 16 * degree, 16)]
        own = jnp.concatenate(
            [spectra[half][start : start + size] for half in range(2) for start, size in places],
            axis=0,
        )
        parts = [split_bf16(own_filter[part, degree]) for part in range(2)]
        both = dot3(own, *(jnp.concatenate(pair, axis=1) for pair in zip(*parts)))
        by_real, by_imag = both[:, :channels], both[:, channels:]
        size = 48
        outs = (by_real[:size] - by_imag[size:], by_real[size:] + by_imag[:size])
        for half in range(2):
            results[half][degree] = outs[half][:32]
            results[half][2 + degree] = outs[half][32:]
    across = []
    for half in range(2):
        padding = jnp.zeros((32, channels), jnp.float32)
        across.append(jnp.concatenate(results[half] + [padding], axis=0).T)
    rows = [
        across[row % 2][row // 2 * devices : (row // 2 + 1) * devices] for row in range(count)
    ]
    for row in range(dense):
        part = row // tail
        folded = pltpu.roll(rows[dense + row % tail], 96 - 32 * part, 1)
        turned[pl.ds(row * devices, devices), :] = jnp.where(quarter < 3, rows[row], folded)
    for device in range(devices):
        sent[pl.ds(device * dense, dense), :] = turned[pl.ds(device, dense, stride=devices), :]


def synthesis_kernel(
    polar_count, got, coef, four_high, four_low, leg_high, leg_low, sent, tails, back, modes_buf
):
    devices, count, _ = coef.shape
    dense, tail = count * 3 // 4, count // 4
    azimuth_count = devices // polar_count
    orders = four_high.shape[1] // 2
    extra = orders - devices
    quarter = lax.broadcasted_iota(jnp.int32, (tail, LANES), 1) // 32
    for device in range(devices):
        folded = [
            pltpu.roll(got[pl.ds(device * dense + tail * part, tail), :], 32 * (part + 1), 1)
            for part in range(3)
        ]
        tails[device, pl.ds(8 - tail, tail), :] = jnp.where(
            quarter == 0, folded[0], jnp.where(quarter == 1, folded[1], folded[2])
        )
        tails[device, pl.ds(0, 8 - tail), :] = got[
            pl.ds(device * dense + count - 8, 8 - tail), :
        ]
    for row in range(0, count, 8):
        if row + 8 < count:
            blocks = [got[pl.ds(device * dense + row, 8), :] for device in range(devices)]
        else:
            blocks = [tails[device] for device in range(devices)]
        blocks = swap(blocks, 1, finish=False)
        for order in range(devices):
            back[order, pl.ds(row, 8), :] = blocks[order]
    keep = (lax.broadcasted_iota(jnp.int32, (count, LANES), 1) & 16) == 0
    for order in range(devices):
        both = jnp.concatenate([coef[order], back[order]], axis=0)
        values = dot3(both, leg_high[order], leg_low[order])
        merged = [
            jnp.where(
                keep,
                values[:count, part * LANES : (part + 1) * LANES],
                values[count:, part * LANES : (part + 1) * LANES],
            )
            for part in range(2)
        ]
        modes_buf[pl.ds(order * count, count), :] = merged[0]
        later = devices + order % extra
        if order < extra:
            modes_buf[pl.ds(later * count, count), :] = merged[1]
        else:
            modes_buf[pl.ds(later * count, count), :] += merged[1]
    four = jnp.concatenate([four_high[...], four_low[...]], axis=0)
    points = four_high.shape[0]
    half = points // 2
    keep = (lax.broadcasted_iota(jnp.int32, (half, LANES), 1) & 16) == 0
    for tile in range(count // 8):
        states = []
        for quad in range(4):
            row = 2 * (4 * tile + quad)
            modes = jnp.concatenate(
                [modes_buf[pl.ds(row + part, orders, stride=count), :] for part in range(2)], axis=0
            )
            modes_high, modes_low = split_bf16(modes)
            both = dot(four, modes_high)
            values = both[:points] + both[points:] + dot(four[:points], modes_low)
            first, second = values[:half], values[half:]
            skip = jnp.where(keep, first, pltpu.roll(second, 16, 1))
            branch = jnp.where(keep, pltpu.roll(first, LANES - 16, 1), second)
            states.append(gelu(branch) + skip)
        for polar, state in enumerate(swap(states, FIELD, after=own_index(azimuth_count))):
            for azimuth in range(azimuth_count):
                device = polar * azimuth_count + azimuth
                sent[pl.ds(device * dense + tail * tile, tail), :] = state[
                    tail * azimuth : tail * (azimuth + 1)
                ]


def mlp_kernel(got, gain, w_in, w_out, mixed, state, result, sems):
    tiles = state.shape[0]
    _, lon_cols, lat_rows, _ = mixed.shape
    part = lon_cols // 2
    devices = got.shape[0] // (tiles * part)
    for tile in range(tiles):
        blocks = swap(
            [
                got[pl.ds((device * tiles + tile) * part, part), :]
                for device in range(devices)
            ],
            1,
            begin=False,
        )
        for device in range(devices):
            state[tile, pl.ds(part * device, part), :] = blocks[device]
    value = jnp.concatenate([state[tile] for tile in range(tiles)], axis=1)
    center = jnp.mean(value, axis=-1, keepdims=True)
    spread = jnp.mean((value - center) ** 2, axis=-1, keepdims=True)
    normed = (value - center) * lax.rsqrt(spread + 1e-05) * gain[...][None, :]
    hidden = gelu(dot(normed.astype(jnp.bfloat16), w_in[...])).astype(jnp.bfloat16)
    size = part * lat_rows
    copies = []
    for top in range(2):
        cells = slice(top * size, (top + 1) * size)
        update = value[cells] + dot(hidden[cells], w_out[...])
        for tile in range(tiles):
            state[tile, cells, :] = update[:, tile * LANES : (tile + 1) * LANES]
            for lon in range(part):
                result[top * part + lon, :, pl.ds(tile * LANES, LANES)] = state[
                    tile, pl.ds(top * size + lon, lat_rows, stride=part), :
                ]
        lons = pl.ds(top * part, part)
        copies.append(pltpu.make_async_copy(result.at[lons], mixed.at[0, lons], sems.at[top]))
        copies[-1].start()
    for copy in copies:
        copy.wait()


def joint_fits(field, filter_real, polar_count, azimuth_count):
    samples, lat_rows, lon_cols, channels = field.shape
    devices = polar_count * azimuth_count
    orders = lon_cols * azimuth_count // 4
    return (
        samples == 1
        and devices == 32
        and polar_count == 4
        and lat_rows == 32
        and lon_cols == 24
        and channels == 3 * LANES
        and filter_real.shape[0] == 2 * polar_count
        and 2 * orders == 3 * devices
    )


def jointly(field, filter_real, filter_imag, norm_gain, w_in, w_out):
    _, lat_rows, lon_cols, channels = field.shape
    polar_count = lax.axis_size("polar")
    azimuth_count = lax.axis_size("azimuth")
    devices = polar_count * azimuth_count
    fine_lat, fine_lon = lat_rows * polar_count, lon_cols * azimuth_count
    coarse_lat, coarse_lon = fine_lat // 2, fine_lon // 2
    orders = coarse_lon // 2
    extra = orders - devices
    count = 2 * channels // devices
    degrees_here = coarse_lat // devices
    lat_out, lon_out = coarse_lat // polar_count, coarse_lon // azimuth_count

    mode_ids = np.tile(np.arange(orders), 2)
    halves = np.repeat(np.arange(2), orders)
    forward = fourier_table(fine_lon, mode_ids, halves, np.ones(2 * orders)).T
    twofold = np.where(mode_ids == 0, 1.0, 2.0)
    inverse = fourier_table(coarse_lon, mode_ids, halves, twofold)
    backward = inverse.reshape(azimuth_count, 2, lon_out // 2, 2 * orders)
    backward = backward.transpose(1, 0, 2, 3).reshape(-1, 2 * orders)

    fine_nodes = colatitudes(fine_lat)
    quadrature = math.pi / fine_lat * np.sin(fine_nodes) * (2.0 * math.pi / fine_lon)
    fine = legendre(fine_nodes, coarse_lat, orders) * quadrature
    coarse = legendre(colatitudes(coarse_lat), coarse_lat, orders)
    owner = np.arange(devices)
    degree = (
        owner % azimuth_count * (coarse_lat // azimuth_count) + owner // azimuth_count * degrees_here
    )
    degree = (degree[None, :] + np.arange(degrees_here)[:, None]).reshape(-1)
    lane = np.arange(LANES)
    lat_fine = lane
    lat_coarse = lane // 32 * lat_out + lane % 16
    fine = fine[:, degree][:, :, lat_fine].transpose(0, 2, 1)
    coarse = coarse[:, degree][:, :, lat_coarse]
    analyse = np.zeros((extra, LANES, 2, 4, devices))
    synthesise = np.zeros((devices, 4, devices, 2, LANES))
    for order in range(devices):
        later, which = devices + order % extra, order // extra
        own = slice(which * devices, (which + 1) * devices)
        analyse[order % extra, :, which, :2] = fine[order].reshape(LANES, 2, devices)
        analyse[order % extra, :, which, 2] = fine[later][:, own]
        synthesise[order, :2, :, 0] = coarse[order].reshape(2, devices, LANES)
        synthesise[order, 2, :, 1] = coarse[later][own]
    analyse = analyse.reshape(extra, LANES, 2 * LANES)
    synthesise = synthesise.reshape(devices, LANES, 2 * LANES)
    for order in range(devices):
        columns = slice(order // extra * LANES, (order // extra + 1) * LANES)
        analyse[order % extra, :, columns] = np.roll(analyse[order % extra, :, columns], order, axis=1)
        synthesise[order] = np.roll(synthesise[order], order, axis=0)

    vmem = pl.BlockSpec(memory_space=pltpu.VMEM)
    hbm = pl.BlockSpec(memory_space=pltpu.HBM)
    dense = count * 3 // 4
    block = pltpu.VMEM((devices * dense, LANES), jnp.float32)

    def exchange(blocks):
        split = blocks.reshape((devices, -1, 2, LANES)) if blocks.ndim == 2 else blocks
        moved = lax.all_to_all(split, BOTH, split_axis=0, concat_axis=0, tiled=True)
        return moved.reshape(blocks.shape)

    def near(*arrays):
        return [pltpu.with_memory_space_constraint(array, pltpu.VMEM) for array in arrays]

    def far(*arrays):
        return [pltpu.with_memory_space_constraint(array, pltpu.HBM) for array in arrays]

    parts = lon_cols // 8
    sent, own_filter = pl.pallas_call(
        scatter_kernel,
        in_specs=[hbm] * 3,
        out_specs=[vmem] * 2,
        out_shape=[
            pltpu.VMEM((devices, lon_cols, channels), jnp.float32),
            pltpu.VMEM((2, degrees_here, channels, channels), jnp.float32),
        ],
        scratch_shapes=[
            pltpu.VMEM((parts, lat_rows, 8, channels), jnp.float32),
            pltpu.SemaphoreType.DMA((parts,)),
            pltpu.SemaphoreType.DMA((2,)),
        ],
        compiler_params=pltpu.CompilerParams(vmem_limit_bytes=8 * MIB),
        name="scatter_channels",
    )(*far(field, filter_real, filter_imag))
    got = exchange(sent)
    coef, sent = pl.pallas_call(
        functools.partial(analysis_kernel, polar_count),
        in_specs=[vmem] * 5,
        out_specs=[vmem] * 2,
        out_shape=[pltpu.VMEM((devices, count, LANES), jnp.float32), block],
        scratch_shapes=[pltpu.VMEM((count * orders, LANES), jnp.float32)],
        compiler_params=pltpu.CompilerParams(vmem_limit_bytes=8 * MIB),
        name="analysis",
    )(*near(got, *split_constant(forward), *split_constant(analyse)))
    got = exchange(sent)
    sent = pl.pallas_call(
        filter_kernel,
        in_specs=[vmem] * 2,
        out_specs=vmem,
        out_shape=block,
        scratch_shapes=[pltpu.VMEM((devices * count, LANES), jnp.float32)],
        compiler_params=pltpu.CompilerParams(vmem_limit_bytes=8 * MIB),
        name="channel_filter",
    )(*near(got, own_filter))
    got = exchange(sent)
    sent = pl.pallas_call(
        functools.partial(synthesis_kernel, polar_count),
        in_specs=[vmem] * 6,
        out_specs=vmem,
        out_shape=block,
        scratch_shapes=[
            pltpu.VMEM((devices, 8, LANES), jnp.float32),
            pltpu.VMEM((devices, count, LANES), jnp.float32),
            pltpu.VMEM((orders * count, LANES), jnp.float32),
        ],
        compiler_params=pltpu.CompilerParams(vmem_limit_bytes=8 * MIB),
        name="synthesis",
    )(*near(got, coef, *split_constant(backward), *split_constant(synthesise)))
    got = exchange(sent)
    mixed = pl.pallas_call(
        mlp_kernel,
        in_specs=[vmem] * 4,
        out_specs=pl.BlockSpec(memory_space=pl.ANY),
        out_shape=jax.ShapeDtypeStruct((1, lon_out, lat_out, channels), jnp.float32),
        scratch_shapes=[
            pltpu.VMEM((channels // LANES, lat_out * lon_out, LANES), jnp.float32),
            pltpu.VMEM((lon_out, lat_out, channels), jnp.float32),
            pltpu.SemaphoreType.DMA((2,)),
        ],
        compiler_params=pltpu.CompilerParams(vmem_limit_bytes=8 * MIB),
        name="mlp",
    )(*near(got, norm_gain, w_in, w_out))
    return mixed.transpose(0, 2, 1, 3)


def per_device(field, filter_real, filter_imag, norm_gain, w_in, w_out):
    polar_count, azimuth_count = lax.axis_size("polar"), lax.axis_size("azimuth")
    plan = jointly if joint_fits(field, filter_real, polar_count, azimuth_count) else by_axes
    return plan(field, filter_real, filter_imag, norm_gain, w_in, w_out)


def solution(mesh):
    in_specs = (
        P(None, "polar", "azimuth", None),
        P("azimuth", None, None),
        P("azimuth", None, None),
        P(),
        P(),
        P(),
    )
    out_specs = P(None, "polar", "azimuth", None)
    return jax.shard_map(
        per_device, mesh=mesh, in_specs=in_specs, out_specs=out_specs, check_vma=False
    )
```

```python
import functools
import math

import jax
import jax.numpy as jnp
import numpy as np
from jax import lax
from jax.experimental import pallas as pl
from jax.experimental.pallas import tpu as pltpu
from jax.sharding import PartitionSpec as P


def legendre(nodes, degrees, orders):
    cosines, sines = np.cos(nodes)[None, :], np.sin(nodes)[None, :]
    mode = np.arange(orders, dtype=np.float64)[:, None]
    counter = np.arange(1, orders + 1, dtype=np.float64)
    ratios = np.log((2.0 * counter - 1.0) / (2.0 * counter))
    product_log = np.concatenate([[0.0], np.cumsum(ratios)])[:orders, None]
    diagonal = np.exp(
        0.5 * (np.log((2.0 * mode + 1.0) / (4.0 * math.pi)) + product_log) + mode * np.log(sines)
    )
    newest, older = np.zeros_like(diagonal), np.zeros_like(diagonal)
    stacked = []
    for degree in range(degrees):
        lower = np.where(degree > mode, degree * degree - mode * mode, 1.0)
        factor_a = np.sqrt(max(4.0 * degree * degree - 1.0, 0.0) / lower)
        factor_b = np.sqrt(
            np.maximum((degree - 1.0) ** 2 - mode**2, 0.0) / max(4.0 * (degree - 1.0) ** 2 - 1.0, 1.0)
        )
        recurred = factor_a * (cosines * newest - factor_b * older)
        second = np.sqrt(2.0 * mode + 3.0) * cosines * newest
        value = np.where(
            degree == mode,
            diagonal,
            np.where(degree == mode + 1.0, second, np.where(degree > mode + 1.0, recurred, 0.0)),
        )
        stacked.append(value)
        newest, older = value, newest
    return np.stack(stacked, axis=1)


def colatitudes(count):
    return math.pi * (np.arange(count) + 0.5) / count


def fourier_table(points, mode_ids, halves, weights):
    angle = 2.0 * math.pi / points * (np.arange(points)[:, None] * mode_ids[None, :] % points)
    return np.where(
        halves[None, :] == 0, weights[None, :] * np.cos(angle), -weights[None, :] * np.sin(angle)
    )


def by_axes(field, filter_real, filter_imag, norm_gain, w_in, w_out):
    high = lax.Precision.HIGHEST
    samples, lat_rows, lon_cols, channels = field.shape
    polar_count = lax.axis_size("polar")
    azimuth_count = lax.axis_size("azimuth")
    fine_lat = lat_rows * polar_count
    fine_lon = lon_cols * azimuth_count
    coarse_lat = fine_lat // 2
    coarse_lon = fine_lon // 2
    orders = coarse_lon // 2
    order_piece = orders // polar_count
    chan_slice = channels // azimuth_count
    columns_all = np.arange(2 * orders)
    halves = columns_all // order_piece % 2
    mode_ids = columns_all // (2 * order_piece) * order_piece + columns_all % order_piece
    twofold = np.where(mode_ids == 0, 1.0, 2.0)
    forward_table = jnp.asarray(
        fourier_table(fine_lon, mode_ids, halves, np.ones(2 * orders)), jnp.float32
    )
    inverse_table = jnp.asarray(fourier_table(coarse_lon, mode_ids, halves, twofold).T, jnp.float32)
    polar_index = lax.axis_index("polar")
    fine_nodes = colatitudes(fine_lat)
    quadrature = math.pi / fine_lat * np.sin(fine_nodes) * (2.0 * math.pi / fine_lon)
    all_fine = legendre(fine_nodes, coarse_lat, orders) * quadrature
    all_coarse = legendre(colatitudes(coarse_lat), coarse_lat, orders)
    own_orders = lambda table: lax.dynamic_slice_in_dim(
        jnp.asarray(table, jnp.float32), polar_index * order_piece, order_piece, 0
    )
    table_fine = own_orders(all_fine)
    table_coarse = own_orders(all_coarse)
    moved = lax.all_to_all(field, "azimuth", split_axis=3, concat_axis=2, tiled=True)
    spectrum = jnp.einsum("bijc,jk->bick", moved, forward_table, precision=high)
    by_order = lax.all_to_all(spectrum, "polar", split_axis=3, concat_axis=1, tiled=True)
    by_order = by_order.reshape(samples, fine_lat, chan_slice, 2, order_piece)
    coef = jnp.einsum("kli,bicpk->blcpk", table_fine, by_order, precision=high)
    degree_block = lax.all_to_all(coef, "azimuth", split_axis=1, concat_axis=2, tiled=True)
    block_re = degree_block[:, :, :, 0]
    block_im = degree_block[:, :, :, 1]
    out_re = jnp.einsum("lco,blck->blok", filter_real, block_re, precision=high) - jnp.einsum(
        "lco,blck->blok", filter_imag, block_im, precision=high
    )
    out_im = jnp.einsum("lco,blck->blok", filter_real, block_im, precision=high) + jnp.einsum(
        "lco,blck->blok", filter_imag, block_re, precision=high
    )
    mixed_spec = jnp.stack([out_re, out_im], axis=3)
    filtered = lax.all_to_all(mixed_spec, "azimuth", split_axis=2, concat_axis=1, tiled=True)
    both_fields = jnp.concatenate([coef, filtered], axis=2)
    grid_modes = jnp.einsum("kli,blcpk->bicpk", table_coarse, both_fields, precision=high)
    grid_modes = grid_modes.reshape(samples, coarse_lat, 2 * chan_slice, 2 * order_piece)
    row_block = lax.all_to_all(grid_modes, "polar", split_axis=1, concat_axis=3, tiled=True)
    values = jnp.einsum("bick,kj->bijc", row_block, inverse_table, precision=high)
    state_split = (
        jax.nn.gelu(values[..., chan_slice:], approximate=False) + values[..., :chan_slice]
    )
    state = lax.all_to_all(state_split, "azimuth", split_axis=2, concat_axis=3, tiled=True)
    center = jnp.mean(state, axis=-1, keepdims=True)
    spread = jnp.mean((state - center) ** 2, axis=-1, keepdims=True)
    normed = ((state - center) * lax.rsqrt(spread + 1e-05) * norm_gain).astype(jnp.bfloat16)
    flat = normed.reshape(-1, channels)
    hidden = jax.nn.gelu(
        jnp.dot(flat, w_in, preferred_element_type=jnp.float32), approximate=False
    ).astype(jnp.bfloat16)
    update = jnp.dot(hidden, w_out, preferred_element_type=jnp.float32)
    return state + update.reshape(state.shape)


LANES = 128
BOTH = ("polar", "azimuth")
MIB = 1024 * 1024


def split_bf16(table):
    high = table.astype(jnp.bfloat16)
    return high, (table - high.astype(jnp.float32)).astype(jnp.bfloat16)


def split_constant(table):
    table = np.asarray(table, np.float32)
    high = table.astype(jnp.bfloat16)
    return jnp.asarray(high), jnp.asarray((table - high.astype(np.float32)).astype(jnp.bfloat16))


def dot(left, right):
    return jnp.dot(left, right, preferred_element_type=jnp.float32)


def dot3(left, right_high, right_low):
    rows = left.shape[0]
    left_high, left_low = split_bf16(left)
    both = dot(jnp.concatenate([left_high, left_low], axis=0), right_high)
    return both[:rows] + both[rows:] + dot(left_high, right_low)


def swap(blocks, step, before=0, after=0, begin=True, finish=True):
    count = len(blocks)
    axis = len(blocks[0].shape) - 1

    def turn(block, fields, lanes, wanted):
        amount = (fields * step * wanted + lanes) % LANES
        return block if isinstance(amount, int) and amount == 0 else pltpu.roll(block, amount, axis)

    place = lax.broadcasted_iota(jnp.int32, blocks[0].shape, axis) // step
    turned = [turn(blocks[-index % count], -index % count, before, begin) for index in range(count)]
    shift = 1
    while shift < count:
        take = (place & shift) != 0
        turned = [
            jnp.where(take, turned[(index - shift) % count], turned[index]) for index in range(count)
        ]
        shift *= 2
    return [turn(block, -index, after, finish) for index, block in enumerate(turned)]


def own_index(azimuth_count):
    return lax.axis_index("polar") * azimuth_count + lax.axis_index("azimuth")


QUAD = 4
FIELD = LANES // QUAD


def gelu(values):
    return 0.5 * values * (1.0 + lax.erf(values * math.sqrt(0.5)))


def scatter_kernel(field, real, imag, sent, own_filter, buf, sems, filter_sems):
    devices, rows, channels = sent.shape
    copies = []
    for row in range(rows // 8):
        copy = pltpu.make_async_copy(
            field.at[0, :, pl.ds(8 * row, 8), :], buf.at[row], sems.at[row]
        )
        copy.start()
        copies.append(copy)
    degrees = own_filter.shape[1]
    start = lax.axis_index("polar") * degrees
    filter_copies = [
        pltpu.make_async_copy(
            part.at[pl.ds(start, degrees)], own_filter.at[index], filter_sems.at[index]
        )
        for index, part in enumerate((real, imag))
    ]
    for copy in filter_copies:
        copy.start()
    for row, copy in enumerate(copies):
        copy.wait()
        for tile in range(channels // LANES):
            lanes = pl.ds(tile * LANES, LANES)
            blocks = swap([buf[row, lat, :, lanes] for lat in range(devices)], 1, finish=False)
            for device in range(devices):
                sent[device, pl.ds(8 * row, 8), lanes] = blocks[device]
    for copy in filter_copies:
        copy.wait()


def analysis_kernel(
    polar_count, got, four_high, four_low, leg_high, leg_low, coef, sent, rows
):
    devices, lon_cols, width = got.shape
    azimuth_count = devices // polar_count
    modes = four_high.shape[0]
    orders = modes // 2
    four = jnp.concatenate([four_high[...], four_low[...]], axis=0)
    tiles = width // LANES
    own_turn = LANES - own_index(azimuth_count)
    block = jnp.concatenate(
        [
            got[pl.ds(polar * azimuth_count, azimuth_count)].reshape(azimuth_count * lon_cols, width)
            for polar in range(polar_count)
        ],
        axis=1,
    )
    block_high, block_low = split_bf16(block)
    both = dot(four, block_high)
    both = both[:modes] + both[modes:] + dot(four[:modes], block_low)
    wide = [both[:, polar * width : (polar + 1) * width] for polar in range(polar_count)]
    for tile in range(tiles):
        spectra = [spectrum[:, tile * LANES : (tile + 1) * LANES] for spectrum in wide]
        for quad, spectrum in enumerate(swap(spectra, FIELD, before=own_turn)):
            rows[pl.ds((tile * polar_count + quad) * modes, modes), :] = spectrum
    count = 2 * tiles * polar_count
    extra = orders - devices
    lane = lax.broadcasted_iota(jnp.int32, (count, LANES), 1)
    for order in range(extra):
        own = [
            rows[pl.ds(row, count, stride=orders), :]
            for row in (order, order + extra, devices + order)
        ]
        values = dot3(jnp.concatenate(own, axis=0), leg_high[order], leg_low[order])
        for part in range(2):
            lanes = slice(part * LANES, (part + 1) * LANES)
            index = order + part * extra
            coef[index] = jnp.where(
                ((lane - index) & (LANES - 1)) < LANES // 2,
                values[part * count : (part + 1) * count, lanes],
                values[2 * count :, lanes],
            )
    pack_by_degree(coef, sent)


def pack_by_degree(coef, sent):
    devices, count, _ = coef.shape
    dense, tail = count * 3 // 4, count // 4
    used = LANES * 3 // 4
    for row in range(0, count, 8):
        blocks = swap([coef[order, pl.ds(row, 8), :] for order in range(devices)], 1, begin=False)
        head = min(max(dense - row, 0), 8)
        for device in range(devices):
            start = device * dense
            if head:
                sent[pl.ds(start + row, head), pl.ds(0, used)] = blocks[device][:head, :used]
            if head < 8:
                skip = max(row - dense, 0)
                for part in range(3):
                    moved = pltpu.roll(blocks[device], used - 32 * part, 1)
                    sent[pl.ds(start + tail * part + skip, 8 - head), pl.ds(used, LANES - used)] = moved[
                        head:, used:
                    ]


def filter_kernel(got, own_filter, sent, turned):
    _, degrees, channels, _ = own_filter.shape
    tiles = channels // LANES
    count = 8 * tiles
    dense, tail = count * 3 // 4, count // 4
    devices = sent.shape[0] // dense
    quarter = lax.broadcasted_iota(jnp.int32, (devices, LANES), 1) // 32
    spectra = []
    for half in range(2):
        parts = []
        for own in range(count // 2):
            row = 2 * own + half
            load = lambda start: got[pl.ds(start, devices, stride=dense), :]
            if row < dense:
                parts.append(load(row))
                continue
            folded = [
                pltpu.roll(load(tail * part + row - dense), 32 * (part + 1), 1) for part in range(3)
            ]
            parts.append(
                jnp.where(quarter == 0, folded[0], jnp.where(quarter == 1, folded[1], folded[2]))
            )
        spectra.append(jnp.concatenate(parts, axis=0).T)
    results = [[None] * 4 for _ in range(2)]
    for degree in range(degrees):
        places = [(32 * degree, 32), (64 + 16 * degree, 16)]
        own = jnp.concatenate(
            [spectra[half][start : start + size] for half in range(2) for start, size in places],
            axis=0,
        )
        parts = [split_bf16(own_filter[part, degree]) for part in range(2)]
        both = dot3(own, *(jnp.concatenate(pair, axis=1) for pair in zip(*parts)))
        by_real, by_imag = both[:, :channels], both[:, channels:]
        size = 48
        outs = (by_real[:size] - by_imag[size:], by_real[size:] + by_imag[:size])
        for half in range(2):
            results[half][degree] = outs[half][:32]
            results[half][2 + degree] = outs[half][32:]
    across = []
    for half in range(2):
        padding = jnp.zeros((32, channels), jnp.float32)
        across.append(jnp.concatenate(results[half] + [padding], axis=0).T)
    rows = [
        across[row % 2][row // 2 * devices : (row // 2 + 1) * devices] for row in range(count)
    ]
    for row in range(dense):
        part = row // tail
        folded = pltpu.roll(rows[dense + row % tail], 96 - 32 * part, 1)
        turned[pl.ds(row * devices, devices), :] = jnp.where(quarter < 3, rows[row], folded)
    for device in range(devices):
        sent[pl.ds(device * dense, dense), :] = turned[pl.ds(device, dense, stride=devices), :]


def synthesis_kernel(
    polar_count, got, coef, four_high, four_low, leg_high, leg_low, sent, tails, back, modes_buf
):
    devices, count, _ = coef.shape
    dense, tail = count * 3 // 4, count // 4
    azimuth_count = devices // polar_count
    orders = four_high.shape[1] // 2
    extra = orders - devices
    quarter = lax.broadcasted_iota(jnp.int32, (tail, LANES), 1) // 32
    for device in range(devices):
        folded = [
            pltpu.roll(got[pl.ds(device * dense + tail * part, tail), :], 32 * (part + 1), 1)
            for part in range(3)
        ]
        tails[device, pl.ds(8 - tail, tail), :] = jnp.where(
            quarter == 0, folded[0], jnp.where(quarter == 1, folded[1], folded[2])
        )
        tails[device, pl.ds(0, 8 - tail), :] = got[
            pl.ds(device * dense + count - 8, 8 - tail), :
        ]
    for row in range(0, count, 8):
        if row + 8 < count:
            blocks = [got[pl.ds(device * dense + row, 8), :] for device in range(devices)]
        else:
            blocks = [tails[device] for device in range(devices)]
        blocks = swap(blocks, 1, finish=False)
        for order in range(devices):
            back[order, pl.ds(row, 8), :] = blocks[order]
    keep = (lax.broadcasted_iota(jnp.int32, (count, LANES), 1) & 16) == 0
    for order in range(devices):
        both = jnp.concatenate([coef[order], back[order]], axis=0)
        values = dot3(both, leg_high[order], leg_low[order])
        merged = [
            jnp.where(
                keep,
                values[:count, part * LANES : (part + 1) * LANES],
                values[count:, part * LANES : (part + 1) * LANES],
            )
            for part in range(2)
        ]
        modes_buf[pl.ds(order * count, count), :] = merged[0]
        later = devices + order % extra
        if order < extra:
            modes_buf[pl.ds(later * count, count), :] = merged[1]
        else:
            modes_buf[pl.ds(later * count, count), :] += merged[1]
    four = jnp.concatenate([four_high[...], four_low[...]], axis=0)
    points = four_high.shape[0]
    half = points // 2
    keep = (lax.broadcasted_iota(jnp.int32, (half, LANES), 1) & 16) == 0
    for tile in range(count // 8):
        modes = jnp.concatenate(
            [
                jnp.concatenate(
                    [
                        modes_buf[pl.ds(2 * (QUAD * tile + quad) + part, orders, stride=count), :]
                        for part in range(2)
                    ],
                    axis=0,
                )
                for quad in range(QUAD)
            ],
            axis=1,
        )
        modes_high, modes_low = split_bf16(modes)
        both = dot(four, modes_high)
        values = both[:points] + both[points:] + dot(four[:points], modes_low)
        states = []
        for quad in range(QUAD):
            lanes = slice(quad * LANES, (quad + 1) * LANES)
            first, second = values[:half, lanes], values[half:, lanes]
            skip = jnp.where(keep, first, pltpu.roll(second, 16, 1))
            branch = jnp.where(keep, pltpu.roll(first, LANES - 16, 1), second)
            states.append(gelu(branch) + skip)
        for polar, state in enumerate(swap(states, FIELD, after=own_index(azimuth_count))):
            for azimuth in range(azimuth_count):
                device = polar * azimuth_count + azimuth
                sent[pl.ds(device * dense + tail * tile, tail), :] = state[
                    tail * azimuth : tail * (azimuth + 1)
                ]


def mlp_kernel(got, gain, w_in, w_out, mixed, state, result, sems):
    tiles = state.shape[0]
    _, lon_cols, lat_rows, _ = mixed.shape
    part = lon_cols // 2
    devices = got.shape[0] // (tiles * part)
    for tile in range(tiles):
        blocks = swap(
            [
                got[pl.ds((device * tiles + tile) * part, part), :]
                for device in range(devices)
            ],
            1,
            begin=False,
        )
        for device in range(devices):
            state[tile, pl.ds(part * device, part), :] = blocks[device]
    value = jnp.concatenate([state[tile] for tile in range(tiles)], axis=1)
    center = jnp.mean(value, axis=-1, keepdims=True)
    spread = jnp.mean((value - center) ** 2, axis=-1, keepdims=True)
    normed = (value - center) * lax.rsqrt(spread + 1e-05) * gain[...][None, :]
    hidden = gelu(dot(normed.astype(jnp.bfloat16), w_in[...])).astype(jnp.bfloat16)
    size = part * lat_rows
    copies = []
    for top in range(2):
        cells = slice(top * size, (top + 1) * size)
        update = value[cells] + dot(hidden[cells], w_out[...])
        for tile in range(tiles):
            state[tile, cells, :] = update[:, tile * LANES : (tile + 1) * LANES]
            for lon in range(part):
                result[top * part + lon, :, pl.ds(tile * LANES, LANES)] = state[
                    tile, pl.ds(top * size + lon, lat_rows, stride=part), :
                ]
        lons = pl.ds(top * part, part)
        copies.append(pltpu.make_async_copy(result.at[lons], mixed.at[0, lons], sems.at[top]))
        copies[-1].start()
    for copy in copies:
        copy.wait()


def joint_fits(field, filter_real, polar_count, azimuth_count):
    samples, lat_rows, lon_cols, channels = field.shape
    devices = polar_count * azimuth_count
    orders = lon_cols * azimuth_count // 4
    return (
        samples == 1
        and devices == 32
        and polar_count == 4
        and lat_rows == 32
        and lon_cols == 24
        and channels == 3 * LANES
        and filter_real.shape[0] == 2 * polar_count
        and 2 * orders == 3 * devices
    )


def jointly(field, filter_real, filter_imag, norm_gain, w_in, w_out):
    _, lat_rows, lon_cols, channels = field.shape
    polar_count = lax.axis_size("polar")
    azimuth_count = lax.axis_size("azimuth")
    devices = polar_count * azimuth_count
    fine_lat, fine_lon = lat_rows * polar_count, lon_cols * azimuth_count
    coarse_lat, coarse_lon = fine_lat // 2, fine_lon // 2
    orders = coarse_lon // 2
    extra = orders - devices
    count = 2 * channels // devices
    degrees_here = coarse_lat // devices
    lat_out, lon_out = coarse_lat // polar_count, coarse_lon // azimuth_count

    mode_ids = np.tile(np.arange(orders), 2)
    halves = np.repeat(np.arange(2), orders)
    forward = fourier_table(fine_lon, mode_ids, halves, np.ones(2 * orders)).T
    twofold = np.where(mode_ids == 0, 1.0, 2.0)
    inverse = fourier_table(coarse_lon, mode_ids, halves, twofold)
    backward = inverse.reshape(azimuth_count, 2, lon_out // 2, 2 * orders)
    backward = backward.transpose(1, 0, 2, 3).reshape(-1, 2 * orders)

    fine_nodes = colatitudes(fine_lat)
    quadrature = math.pi / fine_lat * np.sin(fine_nodes) * (2.0 * math.pi / fine_lon)
    fine = legendre(fine_nodes, coarse_lat, orders) * quadrature
    coarse = legendre(colatitudes(coarse_lat), coarse_lat, orders)
    owner = np.arange(devices)
    degree = (
        owner % azimuth_count * (coarse_lat // azimuth_count) + owner // azimuth_count * degrees_here
    )
    degree = (degree[None, :] + np.arange(degrees_here)[:, None]).reshape(-1)
    lane = np.arange(LANES)
    lat_fine = lane
    lat_coarse = lane // 32 * lat_out + lane % 16
    fine = fine[:, degree][:, :, lat_fine].transpose(0, 2, 1)
    coarse = coarse[:, degree][:, :, lat_coarse]
    analyse = np.zeros((extra, LANES, 2, 4, devices))
    synthesise = np.zeros((devices, 4, devices, 2, LANES))
    for order in range(devices):
        later, which = devices + order % extra, order // extra
        own = slice(which * devices, (which + 1) * devices)
        analyse[order % extra, :, which, :2] = fine[order].reshape(LANES, 2, devices)
        analyse[order % extra, :, which, 2] = fine[later][:, own]
        synthesise[order, :2, :, 0] = coarse[order].reshape(2, devices, LANES)
        synthesise[order, 2, :, 1] = coarse[later][own]
    analyse = analyse.reshape(extra, LANES, 2 * LANES)
    synthesise = synthesise.reshape(devices, LANES, 2 * LANES)
    for order in range(devices):
        columns = slice(order // extra * LANES, (order // extra + 1) * LANES)
        analyse[order % extra, :, columns] = np.roll(analyse[order % extra, :, columns], order, axis=1)
        synthesise[order] = np.roll(synthesise[order], order, axis=0)

    vmem = pl.BlockSpec(memory_space=pltpu.VMEM)
    hbm = pl.BlockSpec(memory_space=pltpu.HBM)
    dense = count * 3 // 4
    block = pltpu.VMEM((devices * dense, LANES), jnp.float32)

    def exchange(blocks):
        split = blocks.reshape((devices, -1, 2, LANES)) if blocks.ndim == 2 else blocks
        moved = lax.all_to_all(split, BOTH, split_axis=0, concat_axis=0, tiled=True)
        return moved.reshape(blocks.shape)

    def near(*arrays):
        return [pltpu.with_memory_space_constraint(array, pltpu.VMEM) for array in arrays]

    def far(*arrays):
        return [pltpu.with_memory_space_constraint(array, pltpu.HBM) for array in arrays]

    parts = lon_cols // 8
    sent, own_filter = pl.pallas_call(
        scatter_kernel,
        in_specs=[hbm] * 3,
        out_specs=[vmem] * 2,
        out_shape=[
            pltpu.VMEM((devices, lon_cols, channels), jnp.float32),
            pltpu.VMEM((2, degrees_here, channels, channels), jnp.float32),
        ],
        scratch_shapes=[
            pltpu.VMEM((parts, lat_rows, 8, channels), jnp.float32),
            pltpu.SemaphoreType.DMA((parts,)),
            pltpu.SemaphoreType.DMA((2,)),
        ],
        compiler_params=pltpu.CompilerParams(vmem_limit_bytes=8 * MIB),
        name="scatter_channels",
    )(*far(field, filter_real, filter_imag))
    got = exchange(sent)
    coef, sent = pl.pallas_call(
        functools.partial(analysis_kernel, polar_count),
        in_specs=[vmem] * 5,
        out_specs=[vmem] * 2,
        out_shape=[pltpu.VMEM((devices, count, LANES), jnp.float32), block],
        scratch_shapes=[pltpu.VMEM((count * orders, LANES), jnp.float32)],
        compiler_params=pltpu.CompilerParams(vmem_limit_bytes=8 * MIB),
        name="analysis",
    )(*near(got, *split_constant(forward), *split_constant(analyse)))
    got = exchange(sent)
    sent = pl.pallas_call(
        filter_kernel,
        in_specs=[vmem] * 2,
        out_specs=vmem,
        out_shape=block,
        scratch_shapes=[pltpu.VMEM((devices * count, LANES), jnp.float32)],
        compiler_params=pltpu.CompilerParams(vmem_limit_bytes=8 * MIB),
        name="channel_filter",
    )(*near(got, own_filter))
    got = exchange(sent)
    sent = pl.pallas_call(
        functools.partial(synthesis_kernel, polar_count),
        in_specs=[vmem] * 6,
        out_specs=vmem,
        out_shape=block,
        scratch_shapes=[
            pltpu.VMEM((devices, 8, LANES), jnp.float32),
            pltpu.VMEM((devices, count, LANES), jnp.float32),
            pltpu.VMEM((orders * count, LANES), jnp.float32),
        ],
        compiler_params=pltpu.CompilerParams(vmem_limit_bytes=8 * MIB),
        name="synthesis",
    )(*near(got, coef, *split_constant(backward), *split_constant(synthesise)))
    got = exchange(sent)
    mixed = pl.pallas_call(
        mlp_kernel,
        in_specs=[vmem] * 4,
        out_specs=pl.BlockSpec(memory_space=pl.ANY),
        out_shape=jax.ShapeDtypeStruct((1, lon_out, lat_out, channels), jnp.float32),
        scratch_shapes=[
            pltpu.VMEM((channels // LANES, lat_out * lon_out, LANES), jnp.float32),
            pltpu.VMEM((lon_out, lat_out, channels), jnp.float32),
            pltpu.SemaphoreType.DMA((2,)),
        ],
        compiler_params=pltpu.CompilerParams(vmem_limit_bytes=8 * MIB),
        name="mlp",
    )(*near(got, norm_gain, w_in, w_out))
    return mixed.transpose(0, 2, 1, 3)


def per_device(field, filter_real, filter_imag, norm_gain, w_in, w_out):
    polar_count, azimuth_count = lax.axis_size("polar"), lax.axis_size("azimuth")
    plan = jointly if joint_fits(field, filter_real, polar_count, azimuth_count) else by_axes
    return plan(field, filter_real, filter_imag, norm_gain, w_in, w_out)


def solution(mesh):
    in_specs = (
        P(None, "polar", "azimuth", None),
        P("azimuth", None, None),
        P("azimuth", None, None),
        P(),
        P(),
        P(),
    )
    out_specs = P(None, "polar", "azimuth", None)
    return jax.shard_map(
        per_device, mesh=mesh, in_specs=in_specs, out_specs=out_specs, check_vma=False
    )
```

```python
import functools
import math

import jax
import jax.numpy as jnp
import numpy as np
from jax import lax
from jax.experimental import pallas as pl
from jax.experimental.pallas import tpu as pltpu
from jax.sharding import PartitionSpec as P


def legendre(nodes, degrees, orders):
    cosines, sines = np.cos(nodes)[None, :], np.sin(nodes)[None, :]
    mode = np.arange(orders, dtype=np.float64)[:, None]
    counter = np.arange(1, orders + 1, dtype=np.float64)
    ratios = np.log((2.0 * counter - 1.0) / (2.0 * counter))
    product_log = np.concatenate([[0.0], np.cumsum(ratios)])[:orders, None]
    diagonal = np.exp(
        0.5 * (np.log((2.0 * mode + 1.0) / (4.0 * math.pi)) + product_log) + mode * np.log(sines)
    )
    newest, older = np.zeros_like(diagonal), np.zeros_like(diagonal)
    stacked = []
    for degree in range(degrees):
        lower = np.where(degree > mode, degree * degree - mode * mode, 1.0)
        factor_a = np.sqrt(max(4.0 * degree * degree - 1.0, 0.0) / lower)
        factor_b = np.sqrt(
            np.maximum((degree - 1.0) ** 2 - mode**2, 0.0) / max(4.0 * (degree - 1.0) ** 2 - 1.0, 1.0)
        )
        recurred = factor_a * (cosines * newest - factor_b * older)
        second = np.sqrt(2.0 * mode + 3.0) * cosines * newest
        value = np.where(
            degree == mode,
            diagonal,
            np.where(degree == mode + 1.0, second, np.where(degree > mode + 1.0, recurred, 0.0)),
        )
        stacked.append(value)
        newest, older = value, newest
    return np.stack(stacked, axis=1)


def colatitudes(count):
    return math.pi * (np.arange(count) + 0.5) / count


def fourier_table(points, mode_ids, halves, weights):
    angle = 2.0 * math.pi / points * (np.arange(points)[:, None] * mode_ids[None, :] % points)
    return np.where(
        halves[None, :] == 0, weights[None, :] * np.cos(angle), -weights[None, :] * np.sin(angle)
    )


def by_axes(field, filter_real, filter_imag, norm_gain, w_in, w_out):
    high = lax.Precision.HIGHEST
    samples, lat_rows, lon_cols, channels = field.shape
    polar_count = lax.axis_size("polar")
    azimuth_count = lax.axis_size("azimuth")
    fine_lat = lat_rows * polar_count
    fine_lon = lon_cols * azimuth_count
    coarse_lat = fine_lat // 2
    coarse_lon = fine_lon // 2
    orders = coarse_lon // 2
    order_piece = orders // polar_count
    chan_slice = channels // azimuth_count
    columns_all = np.arange(2 * orders)
    halves = columns_all // order_piece % 2
    mode_ids = columns_all // (2 * order_piece) * order_piece + columns_all % order_piece
    twofold = np.where(mode_ids == 0, 1.0, 2.0)
    forward_table = jnp.asarray(
        fourier_table(fine_lon, mode_ids, halves, np.ones(2 * orders)), jnp.float32
    )
    inverse_table = jnp.asarray(fourier_table(coarse_lon, mode_ids, halves, twofold).T, jnp.float32)
    polar_index = lax.axis_index("polar")
    fine_nodes = colatitudes(fine_lat)
    quadrature = math.pi / fine_lat * np.sin(fine_nodes) * (2.0 * math.pi / fine_lon)
    all_fine = legendre(fine_nodes, coarse_lat, orders) * quadrature
    all_coarse = legendre(colatitudes(coarse_lat), coarse_lat, orders)
    own_orders = lambda table: lax.dynamic_slice_in_dim(
        jnp.asarray(table, jnp.float32), polar_index * order_piece, order_piece, 0
    )
    table_fine = own_orders(all_fine)
    table_coarse = own_orders(all_coarse)
    moved = lax.all_to_all(field, "azimuth", split_axis=3, concat_axis=2, tiled=True)
    spectrum = jnp.einsum("bijc,jk->bick", moved, forward_table, precision=high)
    by_order = lax.all_to_all(spectrum, "polar", split_axis=3, concat_axis=1, tiled=True)
    by_order = by_order.reshape(samples, fine_lat, chan_slice, 2, order_piece)
    coef = jnp.einsum("kli,bicpk->blcpk", table_fine, by_order, precision=high)
    degree_block = lax.all_to_all(coef, "azimuth", split_axis=1, concat_axis=2, tiled=True)
    block_re = degree_block[:, :, :, 0]
    block_im = degree_block[:, :, :, 1]
    out_re = jnp.einsum("lco,blck->blok", filter_real, block_re, precision=high) - jnp.einsum(
        "lco,blck->blok", filter_imag, block_im, precision=high
    )
    out_im = jnp.einsum("lco,blck->blok", filter_real, block_im, precision=high) + jnp.einsum(
        "lco,blck->blok", filter_imag, block_re, precision=high
    )
    mixed_spec = jnp.stack([out_re, out_im], axis=3)
    filtered = lax.all_to_all(mixed_spec, "azimuth", split_axis=2, concat_axis=1, tiled=True)
    both_fields = jnp.concatenate([coef, filtered], axis=2)
    grid_modes = jnp.einsum("kli,blcpk->bicpk", table_coarse, both_fields, precision=high)
    grid_modes = grid_modes.reshape(samples, coarse_lat, 2 * chan_slice, 2 * order_piece)
    row_block = lax.all_to_all(grid_modes, "polar", split_axis=1, concat_axis=3, tiled=True)
    values = jnp.einsum("bick,kj->bijc", row_block, inverse_table, precision=high)
    state_split = (
        jax.nn.gelu(values[..., chan_slice:], approximate=False) + values[..., :chan_slice]
    )
    state = lax.all_to_all(state_split, "azimuth", split_axis=2, concat_axis=3, tiled=True)
    center = jnp.mean(state, axis=-1, keepdims=True)
    spread = jnp.mean((state - center) ** 2, axis=-1, keepdims=True)
    normed = ((state - center) * lax.rsqrt(spread + 1e-05) * norm_gain).astype(jnp.bfloat16)
    flat = normed.reshape(-1, channels)
    hidden = jax.nn.gelu(
        jnp.dot(flat, w_in, preferred_element_type=jnp.float32), approximate=False
    ).astype(jnp.bfloat16)
    update = jnp.dot(hidden, w_out, preferred_element_type=jnp.float32)
    return state + update.reshape(state.shape)


LANES = 128
BOTH = ("polar", "azimuth")
MIB = 1024 * 1024


def split_bf16(table):
    high = table.astype(jnp.bfloat16)
    return high, (table - high.astype(jnp.float32)).astype(jnp.bfloat16)


def split_constant(table):
    table = np.asarray(table, np.float32)
    high = table.astype(jnp.bfloat16)
    return jnp.asarray(high), jnp.asarray((table - high.astype(np.float32)).astype(jnp.bfloat16))


def dot(left, right):
    return jnp.dot(left, right, preferred_element_type=jnp.float32)


def dot3(left, right_high, right_low):
    rows = left.shape[0]
    left_high, left_low = split_bf16(left)
    both = dot(jnp.concatenate([left_high, left_low], axis=0), right_high)
    return both[:rows] + both[rows:] + dot(left_high, right_low)


def swap(blocks, step, before=0, after=0, begin=True, finish=True):
    count = len(blocks)
    axis = len(blocks[0].shape) - 1

    def turn(block, fields, lanes, wanted):
        amount = (fields * step * wanted + lanes) % LANES
        return block if isinstance(amount, int) and amount == 0 else pltpu.roll(block, amount, axis)

    place = lax.broadcasted_iota(jnp.int32, blocks[0].shape, axis) // step
    turned = [turn(blocks[-index % count], -index % count, before, begin) for index in range(count)]
    shift = 1
    while shift < count:
        take = (place & shift) != 0
        turned = [
            jnp.where(take, turned[(index - shift) % count], turned[index]) for index in range(count)
        ]
        shift *= 2
    return [turn(block, -index, after, finish) for index, block in enumerate(turned)]


def own_index(azimuth_count):
    return lax.axis_index("polar") * azimuth_count + lax.axis_index("azimuth")


QUAD = 4
FIELD = LANES // QUAD


def gelu(values):
    return 0.5 * values * (1.0 + lax.erf(values * math.sqrt(0.5)))


def scatter_kernel(field, real, imag, sent, own_filter, buf, sems, filter_sems):
    devices, rows, channels = sent.shape
    copies = []
    for row in range(rows // 8):
        copy = pltpu.make_async_copy(
            field.at[0, :, pl.ds(8 * row, 8), :], buf.at[row], sems.at[row]
        )
        copy.start()
        copies.append(copy)
    degrees = own_filter.shape[1]
    start = lax.axis_index("polar") * degrees
    size = channels // 2
    filter_copies = [
        pltpu.make_async_copy(
            part.at[pl.ds(start, degrees), pl.ds(piece * size, size)],
            own_filter.at[index, :, pl.ds(piece * size, size)],
            filter_sems.at[index, piece],
        )
        for index, part in enumerate((real, imag))
        for piece in range(2)
    ]
    for copy in filter_copies:
        copy.start()
    for row, copy in enumerate(copies):
        copy.wait()
        for tile in range(channels // LANES):
            lanes = pl.ds(tile * LANES, LANES)
            blocks = swap([buf[row, lat, :, lanes] for lat in range(devices)], 1, finish=False)
            for device in range(devices):
                sent[device, pl.ds(8 * row, 8), lanes] = blocks[device]
    for copy in filter_copies:
        copy.wait()


def analysis_kernel(
    polar_count, got, four_high, four_low, leg_high, leg_low, coef, sent, rows
):
    devices, lon_cols, width = got.shape
    azimuth_count = devices // polar_count
    modes = four_high.shape[0]
    orders = modes // 2
    four = jnp.concatenate([four_high[...], four_low[...]], axis=0)
    tiles = width // LANES
    own_turn = LANES - own_index(azimuth_count)
    block = jnp.concatenate(
        [
            got[pl.ds(polar * azimuth_count, azimuth_count)].reshape(azimuth_count * lon_cols, width)
            for polar in range(polar_count)
        ],
        axis=1,
    )
    block_high, block_low = split_bf16(block)
    both = dot(four, block_high)
    both = both[:modes] + both[modes:] + dot(four[:modes], block_low)
    wide = [both[:, polar * width : (polar + 1) * width] for polar in range(polar_count)]
    for tile in range(tiles):
        spectra = [spectrum[:, tile * LANES : (tile + 1) * LANES] for spectrum in wide]
        for quad, spectrum in enumerate(swap(spectra, FIELD, before=own_turn)):
            rows[pl.ds((tile * polar_count + quad) * modes, modes), :] = spectrum
    count = 2 * tiles * polar_count
    extra = orders - devices
    lane = lax.broadcasted_iota(jnp.int32, (count, LANES), 1)
    for order in range(extra):
        own = [
            rows[pl.ds(row, count, stride=orders), :]
            for row in (order, order + extra, devices + order)
        ]
        values = dot3(jnp.concatenate(own, axis=0), leg_high[order], leg_low[order])
        for part in range(2):
            lanes = slice(part * LANES, (part + 1) * LANES)
            index = order + part * extra
            coef[index] = jnp.where(
                ((lane - index) & (LANES - 1)) < LANES // 2,
                values[part * count : (part + 1) * count, lanes],
                values[2 * count :, lanes],
            )
    pack_by_degree(coef, sent)


def pack_by_degree(coef, sent):
    devices, count, _ = coef.shape
    dense, tail = count * 3 // 4, count // 4
    used = LANES * 3 // 4
    for row in range(0, count, 8):
        blocks = swap([coef[order, pl.ds(row, 8), :] for order in range(devices)], 1, begin=False)
        head = min(max(dense - row, 0), 8)
        for device in range(devices):
            start = device * dense
            if head:
                sent[pl.ds(start + row, head), pl.ds(0, used)] = blocks[device][:head, :used]
            if head < 8:
                skip = max(row - dense, 0)
                for part in range(3):
                    moved = pltpu.roll(blocks[device], used - 32 * part, 1)
                    sent[pl.ds(start + tail * part + skip, 8 - head), pl.ds(used, LANES - used)] = moved[
                        head:, used:
                    ]


def filter_kernel(got, own_filter, sent, turned):
    _, degrees, channels, _ = own_filter.shape
    tiles = channels // LANES
    count = 8 * tiles
    dense, tail = count * 3 // 4, count // 4
    devices = sent.shape[0] // dense
    quarter = lax.broadcasted_iota(jnp.int32, (devices, LANES), 1) // 32
    spectra = []
    for half in range(2):
        parts = []
        for own in range(count // 2):
            row = 2 * own + half
            load = lambda start: got[pl.ds(start, devices, stride=dense), :]
            if row < dense:
                parts.append(load(row))
                continue
            folded = [
                pltpu.roll(load(tail * part + row - dense), 32 * (part + 1), 1) for part in range(3)
            ]
            parts.append(
                jnp.where(quarter == 0, folded[0], jnp.where(quarter == 1, folded[1], folded[2]))
            )
        spectra.append(jnp.concatenate(parts, axis=0).T)
    results = [[None] * 4 for _ in range(2)]
    for degree in range(degrees):
        places = [(32 * degree, 32), (64 + 16 * degree, 16)]
        own = jnp.concatenate(
            [spectra[half][start : start + size] for half in range(2) for start, size in places],
            axis=0,
        )
        parts = [split_bf16(own_filter[part, degree]) for part in range(2)]
        both = dot3(own, *(jnp.concatenate(pair, axis=1) for pair in zip(*parts)))
        by_real, by_imag = both[:, :channels], both[:, channels:]
        size = 48
        outs = (by_real[:size] - by_imag[size:], by_real[size:] + by_imag[:size])
        for half in range(2):
            results[half][degree] = outs[half][:32]
            results[half][2 + degree] = outs[half][32:]
    across = []
    for half in range(2):
        padding = jnp.zeros((32, channels), jnp.float32)
        across.append(jnp.concatenate(results[half] + [padding], axis=0).T)
    rows = [
        across[row % 2][row // 2 * devices : (row // 2 + 1) * devices] for row in range(count)
    ]
    for row in range(dense):
        part = row // tail
        folded = pltpu.roll(rows[dense + row % tail], 96 - 32 * part, 1)
        turned[pl.ds(row * devices, devices), :] = jnp.where(quarter < 3, rows[row], folded)
    for device in range(devices):
        sent[pl.ds(device * dense, dense), :] = turned[pl.ds(device, dense, stride=devices), :]


def synthesis_kernel(
    polar_count, got, coef, four_high, four_low, leg_high, leg_low, sent, tails, back, modes_buf
):
    devices, count, _ = coef.shape
    dense, tail = count * 3 // 4, count // 4
    azimuth_count = devices // polar_count
    orders = four_high.shape[1] // 2
    extra = orders - devices
    quarter = lax.broadcasted_iota(jnp.int32, (tail, LANES), 1) // 32
    for device in range(devices):
        folded = [
            pltpu.roll(got[pl.ds(device * dense + tail * part, tail), :], 32 * (part + 1), 1)
            for part in range(3)
        ]
        tails[device, pl.ds(8 - tail, tail), :] = jnp.where(
            quarter == 0, folded[0], jnp.where(quarter == 1, folded[1], folded[2])
        )
        tails[device, pl.ds(0, 8 - tail), :] = got[
            pl.ds(device * dense + count - 8, 8 - tail), :
        ]
    for row in range(0, count, 8):
        if row + 8 < count:
            blocks = [got[pl.ds(device * dense + row, 8), :] for device in range(devices)]
        else:
            blocks = [tails[device] for device in range(devices)]
        blocks = swap(blocks, 1, finish=False)
        for order in range(devices):
            back[order, pl.ds(row, 8), :] = blocks[order]
    keep = (lax.broadcasted_iota(jnp.int32, (count, LANES), 1) & 16) == 0
    for order in range(devices):
        both = jnp.concatenate([coef[order], back[order]], axis=0)
        values = dot3(both, leg_high[order], leg_low[order])
        merged = [
            jnp.where(
                keep,
                values[:count, part * LANES : (part + 1) * LANES],
                values[count:, part * LANES : (part + 1) * LANES],
            )
            for part in range(2)
        ]
        modes_buf[pl.ds(order * count, count), :] = merged[0]
        later = devices + order % extra
        if order < extra:
            modes_buf[pl.ds(later * count, count), :] = merged[1]
        else:
            modes_buf[pl.ds(later * count, count), :] += merged[1]
    four = jnp.concatenate([four_high[...], four_low[...]], axis=0)
    points = four_high.shape[0]
    half = points // 2
    keep = (lax.broadcasted_iota(jnp.int32, (half, LANES), 1) & 16) == 0
    for tile in range(count // 8):
        modes = jnp.concatenate(
            [
                jnp.concatenate(
                    [
                        modes_buf[pl.ds(2 * (QUAD * tile + quad) + part, orders, stride=count), :]
                        for part in range(2)
                    ],
                    axis=0,
                )
                for quad in range(QUAD)
            ],
            axis=1,
        )
        modes_high, modes_low = split_bf16(modes)
        both = dot(four, modes_high)
        values = both[:points] + both[points:] + dot(four[:points], modes_low)
        states = []
        for quad in range(QUAD):
            lanes = slice(quad * LANES, (quad + 1) * LANES)
            first, second = values[:half, lanes], values[half:, lanes]
            skip = jnp.where(keep, first, pltpu.roll(second, 16, 1))
            branch = jnp.where(keep, pltpu.roll(first, LANES - 16, 1), second)
            states.append(gelu(branch) + skip)
        for polar, state in enumerate(swap(states, FIELD, after=own_index(azimuth_count))):
            for azimuth in range(azimuth_count):
                device = polar * azimuth_count + azimuth
                sent[pl.ds(device * dense + tail * tile, tail), :] = state[
                    tail * azimuth : tail * (azimuth + 1)
                ]


def mlp_kernel(got, gain, w_in, w_out, mixed, state, result, sems):
    tiles = state.shape[0]
    _, lon_cols, lat_rows, _ = mixed.shape
    part = lon_cols // 2
    devices = got.shape[0] // (tiles * part)
    for tile in range(tiles):
        blocks = swap(
            [
                got[pl.ds((device * tiles + tile) * part, part), :]
                for device in range(devices)
            ],
            1,
            begin=False,
        )
        for device in range(devices):
            state[tile, pl.ds(part * device, part), :] = blocks[device]
    value = jnp.concatenate([state[tile] for tile in range(tiles)], axis=1)
    center = jnp.mean(value, axis=-1, keepdims=True)
    spread = jnp.mean((value - center) ** 2, axis=-1, keepdims=True)
    normed = (value - center) * lax.rsqrt(spread + 1e-05) * gain[...][None, :]
    hidden = gelu(dot(normed.astype(jnp.bfloat16), w_in[...])).astype(jnp.bfloat16)
    size = part * lat_rows
    copies = []
    for top in range(2):
        cells = slice(top * size, (top + 1) * size)
        update = value[cells] + dot(hidden[cells], w_out[...])
        for tile in range(tiles):
            state[tile, cells, :] = update[:, tile * LANES : (tile + 1) * LANES]
            for lon in range(part):
                result[top * part + lon, :, pl.ds(tile * LANES, LANES)] = state[
                    tile, pl.ds(top * size + lon, lat_rows, stride=part), :
                ]
        lons = pl.ds(top * part, part)
        copies.append(pltpu.make_async_copy(result.at[lons], mixed.at[0, lons], sems.at[top]))
        copies[-1].start()
    for copy in copies:
        copy.wait()


def joint_fits(field, filter_real, polar_count, azimuth_count):
    samples, lat_rows, lon_cols, channels = field.shape
    devices = polar_count * azimuth_count
    orders = lon_cols * azimuth_count // 4
    return (
        samples == 1
        and devices == 32
        and polar_count == 4
        and lat_rows == 32
        and lon_cols == 24
        and channels == 3 * LANES
        and filter_real.shape[0] == 2 * polar_count
        and 2 * orders == 3 * devices
    )


def jointly(field, filter_real, filter_imag, norm_gain, w_in, w_out):
    _, lat_rows, lon_cols, channels = field.shape
    polar_count = lax.axis_size("polar")
    azimuth_count = lax.axis_size("azimuth")
    devices = polar_count * azimuth_count
    fine_lat, fine_lon = lat_rows * polar_count, lon_cols * azimuth_count
    coarse_lat, coarse_lon = fine_lat // 2, fine_lon // 2
    orders = coarse_lon // 2
    extra = orders - devices
    count = 2 * channels // devices
    degrees_here = coarse_lat // devices
    lat_out, lon_out = coarse_lat // polar_count, coarse_lon // azimuth_count

    mode_ids = np.tile(np.arange(orders), 2)
    halves = np.repeat(np.arange(2), orders)
    forward = fourier_table(fine_lon, mode_ids, halves, np.ones(2 * orders)).T
    twofold = np.where(mode_ids == 0, 1.0, 2.0)
    inverse = fourier_table(coarse_lon, mode_ids, halves, twofold)
    backward = inverse.reshape(azimuth_count, 2, lon_out // 2, 2 * orders)
    backward = backward.transpose(1, 0, 2, 3).reshape(-1, 2 * orders)

    fine_nodes = colatitudes(fine_lat)
    quadrature = math.pi / fine_lat * np.sin(fine_nodes) * (2.0 * math.pi / fine_lon)
    fine = legendre(fine_nodes, coarse_lat, orders) * quadrature
    coarse = legendre(colatitudes(coarse_lat), coarse_lat, orders)
    owner = np.arange(devices)
    degree = (
        owner % azimuth_count * (coarse_lat // azimuth_count) + owner // azimuth_count * degrees_here
    )
    degree = (degree[None, :] + np.arange(degrees_here)[:, None]).reshape(-1)
    lane = np.arange(LANES)
    lat_fine = lane
    lat_coarse = lane // 32 * lat_out + lane % 16
    fine = fine[:, degree][:, :, lat_fine].transpose(0, 2, 1)
    coarse = coarse[:, degree][:, :, lat_coarse]
    analyse = np.zeros((extra, LANES, 2, 4, devices))
    synthesise = np.zeros((devices, 4, devices, 2, LANES))
    for order in range(devices):
        later, which = devices + order % extra, order // extra
        own = slice(which * devices, (which + 1) * devices)
        analyse[order % extra, :, which, :2] = fine[order].reshape(LANES, 2, devices)
        analyse[order % extra, :, which, 2] = fine[later][:, own]
        synthesise[order, :2, :, 0] = coarse[order].reshape(2, devices, LANES)
        synthesise[order, 2, :, 1] = coarse[later][own]
    analyse = analyse.reshape(extra, LANES, 2 * LANES)
    synthesise = synthesise.reshape(devices, LANES, 2 * LANES)
    for order in range(devices):
        columns = slice(order // extra * LANES, (order // extra + 1) * LANES)
        analyse[order % extra, :, columns] = np.roll(analyse[order % extra, :, columns], order, axis=1)
        synthesise[order] = np.roll(synthesise[order], order, axis=0)

    vmem = pl.BlockSpec(memory_space=pltpu.VMEM)
    hbm = pl.BlockSpec(memory_space=pltpu.HBM)
    dense = count * 3 // 4
    block = pltpu.VMEM((devices * dense, LANES), jnp.float32)

    def exchange(blocks):
        split = blocks.reshape((devices, -1, 2, LANES)) if blocks.ndim == 2 else blocks
        moved = lax.all_to_all(split, BOTH, split_axis=0, concat_axis=0, tiled=True)
        return moved.reshape(blocks.shape)

    def near(*arrays):
        return [pltpu.with_memory_space_constraint(array, pltpu.VMEM) for array in arrays]

    def far(*arrays):
        return [pltpu.with_memory_space_constraint(array, pltpu.HBM) for array in arrays]

    parts = lon_cols // 8
    sent, own_filter = pl.pallas_call(
        scatter_kernel,
        in_specs=[hbm] * 3,
        out_specs=[vmem] * 2,
        out_shape=[
            pltpu.VMEM((devices, lon_cols, channels), jnp.float32),
            pltpu.VMEM((2, degrees_here, channels, channels), jnp.float32),
        ],
        scratch_shapes=[
            pltpu.VMEM((parts, lat_rows, 8, channels), jnp.float32),
            pltpu.SemaphoreType.DMA((parts,)),
            pltpu.SemaphoreType.DMA((2, 2)),
        ],
        compiler_params=pltpu.CompilerParams(vmem_limit_bytes=8 * MIB),
        name="scatter_channels",
    )(*far(field, filter_real, filter_imag))
    got = exchange(sent)
    coef, sent = pl.pallas_call(
        functools.partial(analysis_kernel, polar_count),
        in_specs=[vmem] * 5,
        out_specs=[vmem] * 2,
        out_shape=[pltpu.VMEM((devices, count, LANES), jnp.float32), block],
        scratch_shapes=[pltpu.VMEM((count * orders, LANES), jnp.float32)],
        compiler_params=pltpu.CompilerParams(vmem_limit_bytes=8 * MIB),
        name="analysis",
    )(*near(got, *split_constant(forward), *split_constant(analyse)))
    got = exchange(sent)
    sent = pl.pallas_call(
        filter_kernel,
        in_specs=[vmem] * 2,
        out_specs=vmem,
        out_shape=block,
        scratch_shapes=[pltpu.VMEM((devices * count, LANES), jnp.float32)],
        compiler_params=pltpu.CompilerParams(vmem_limit_bytes=8 * MIB),
        name="channel_filter",
    )(*near(got, own_filter))
    got = exchange(sent)
    sent = pl.pallas_call(
        functools.partial(synthesis_kernel, polar_count),
        in_specs=[vmem] * 6,
        out_specs=vmem,
        out_shape=block,
        scratch_shapes=[
            pltpu.VMEM((devices, 8, LANES), jnp.float32),
            pltpu.VMEM((devices, count, LANES), jnp.float32),
            pltpu.VMEM((orders * count, LANES), jnp.float32),
        ],
        compiler_params=pltpu.CompilerParams(vmem_limit_bytes=8 * MIB),
        name="synthesis",
    )(*near(got, coef, *split_constant(backward), *split_constant(synthesise)))
    got = exchange(sent)
    mixed = pl.pallas_call(
        mlp_kernel,
        in_specs=[vmem] * 4,
        out_specs=pl.BlockSpec(memory_space=pl.ANY),
        out_shape=jax.ShapeDtypeStruct((1, lon_out, lat_out, channels), jnp.float32),
        scratch_shapes=[
            pltpu.VMEM((channels // LANES, lat_out * lon_out, LANES), jnp.float32),
            pltpu.VMEM((lon_out, lat_out, channels), jnp.float32),
            pltpu.SemaphoreType.DMA((2,)),
        ],
        compiler_params=pltpu.CompilerParams(vmem_limit_bytes=8 * MIB),
        name="mlp",
    )(*near(got, norm_gain, w_in, w_out))
    return mixed.transpose(0, 2, 1, 3)


def per_device(field, filter_real, filter_imag, norm_gain, w_in, w_out):
    polar_count, azimuth_count = lax.axis_size("polar"), lax.axis_size("azimuth")
    plan = jointly if joint_fits(field, filter_real, polar_count, azimuth_count) else by_axes
    return plan(field, filter_real, filter_imag, norm_gain, w_in, w_out)


def solution(mesh):
    in_specs = (
        P(None, "polar", "azimuth", None),
        P("azimuth", None, None),
        P("azimuth", None, None),
        P(),
        P(),
        P(),
    )
    out_specs = P(None, "polar", "azimuth", None)
    return jax.shard_map(
        per_device, mesh=mesh, in_specs=in_specs, out_specs=out_specs, check_vma=False
    )
```

```python
import functools
import math

import jax
import jax.numpy as jnp
import numpy as np
from jax import lax
from jax.experimental import pallas as pl
from jax.experimental.pallas import tpu as pltpu
from jax.sharding import PartitionSpec as P


def legendre(nodes, degrees, orders):
    cosines, sines = np.cos(nodes)[None, :], np.sin(nodes)[None, :]
    mode = np.arange(orders, dtype=np.float64)[:, None]
    counter = np.arange(1, orders + 1, dtype=np.float64)
    ratios = np.log((2.0 * counter - 1.0) / (2.0 * counter))
    product_log = np.concatenate([[0.0], np.cumsum(ratios)])[:orders, None]
    diagonal = np.exp(
        0.5 * (np.log((2.0 * mode + 1.0) / (4.0 * math.pi)) + product_log) + mode * np.log(sines)
    )
    newest, older = np.zeros_like(diagonal), np.zeros_like(diagonal)
    stacked = []
    for degree in range(degrees):
        lower = np.where(degree > mode, degree * degree - mode * mode, 1.0)
        factor_a = np.sqrt(max(4.0 * degree * degree - 1.0, 0.0) / lower)
        factor_b = np.sqrt(
            np.maximum((degree - 1.0) ** 2 - mode**2, 0.0) / max(4.0 * (degree - 1.0) ** 2 - 1.0, 1.0)
        )
        recurred = factor_a * (cosines * newest - factor_b * older)
        second = np.sqrt(2.0 * mode + 3.0) * cosines * newest
        value = np.where(
            degree == mode,
            diagonal,
            np.where(degree == mode + 1.0, second, np.where(degree > mode + 1.0, recurred, 0.0)),
        )
        stacked.append(value)
        newest, older = value, newest
    return np.stack(stacked, axis=1)


def colatitudes(count):
    return math.pi * (np.arange(count) + 0.5) / count


def fourier_table(points, mode_ids, halves, weights):
    angle = 2.0 * math.pi / points * (np.arange(points)[:, None] * mode_ids[None, :] % points)
    return np.where(
        halves[None, :] == 0, weights[None, :] * np.cos(angle), -weights[None, :] * np.sin(angle)
    )


def by_axes(field, filter_real, filter_imag, norm_gain, w_in, w_out):
    high = lax.Precision.HIGHEST
    samples, lat_rows, lon_cols, channels = field.shape
    polar_count = lax.axis_size("polar")
    azimuth_count = lax.axis_size("azimuth")
    fine_lat = lat_rows * polar_count
    fine_lon = lon_cols * azimuth_count
    coarse_lat = fine_lat // 2
    coarse_lon = fine_lon // 2
    orders = coarse_lon // 2
    order_piece = orders // polar_count
    chan_slice = channels // azimuth_count
    columns_all = np.arange(2 * orders)
    halves = columns_all // order_piece % 2
    mode_ids = columns_all // (2 * order_piece) * order_piece + columns_all % order_piece
    twofold = np.where(mode_ids == 0, 1.0, 2.0)
    forward_table = jnp.asarray(
        fourier_table(fine_lon, mode_ids, halves, np.ones(2 * orders)), jnp.float32
    )
    inverse_table = jnp.asarray(fourier_table(coarse_lon, mode_ids, halves, twofold).T, jnp.float32)
    polar_index = lax.axis_index("polar")
    fine_nodes = colatitudes(fine_lat)
    quadrature = math.pi / fine_lat * np.sin(fine_nodes) * (2.0 * math.pi / fine_lon)
    all_fine = legendre(fine_nodes, coarse_lat, orders) * quadrature
    all_coarse = legendre(colatitudes(coarse_lat), coarse_lat, orders)
    own_orders = lambda table: lax.dynamic_slice_in_dim(
        jnp.asarray(table, jnp.float32), polar_index * order_piece, order_piece, 0
    )
    table_fine = own_orders(all_fine)
    table_coarse = own_orders(all_coarse)
    moved = lax.all_to_all(field, "azimuth", split_axis=3, concat_axis=2, tiled=True)
    spectrum = jnp.einsum("bijc,jk->bick", moved, forward_table, precision=high)
    by_order = lax.all_to_all(spectrum, "polar", split_axis=3, concat_axis=1, tiled=True)
    by_order = by_order.reshape(samples, fine_lat, chan_slice, 2, order_piece)
    coef = jnp.einsum("kli,bicpk->blcpk", table_fine, by_order, precision=high)
    degree_block = lax.all_to_all(coef, "azimuth", split_axis=1, concat_axis=2, tiled=True)
    block_re = degree_block[:, :, :, 0]
    block_im = degree_block[:, :, :, 1]
    out_re = jnp.einsum("lco,blck->blok", filter_real, block_re, precision=high) - jnp.einsum(
        "lco,blck->blok", filter_imag, block_im, precision=high
    )
    out_im = jnp.einsum("lco,blck->blok", filter_real, block_im, precision=high) + jnp.einsum(
        "lco,blck->blok", filter_imag, block_re, precision=high
    )
    mixed_spec = jnp.stack([out_re, out_im], axis=3)
    filtered = lax.all_to_all(mixed_spec, "azimuth", split_axis=2, concat_axis=1, tiled=True)
    both_fields = jnp.concatenate([coef, filtered], axis=2)
    grid_modes = jnp.einsum("kli,blcpk->bicpk", table_coarse, both_fields, precision=high)
    grid_modes = grid_modes.reshape(samples, coarse_lat, 2 * chan_slice, 2 * order_piece)
    row_block = lax.all_to_all(grid_modes, "polar", split_axis=1, concat_axis=3, tiled=True)
    values = jnp.einsum("bick,kj->bijc", row_block, inverse_table, precision=high)
    state_split = (
        jax.nn.gelu(values[..., chan_slice:], approximate=False) + values[..., :chan_slice]
    )
    state = lax.all_to_all(state_split, "azimuth", split_axis=2, concat_axis=3, tiled=True)
    center = jnp.mean(state, axis=-1, keepdims=True)
    spread = jnp.mean((state - center) ** 2, axis=-1, keepdims=True)
    normed = ((state - center) * lax.rsqrt(spread + 1e-05) * norm_gain).astype(jnp.bfloat16)
    flat = normed.reshape(-1, channels)
    hidden = jax.nn.gelu(
        jnp.dot(flat, w_in, preferred_element_type=jnp.float32), approximate=False
    ).astype(jnp.bfloat16)
    update = jnp.dot(hidden, w_out, preferred_element_type=jnp.float32)
    return state + update.reshape(state.shape)


LANES = 128
BOTH = ("polar", "azimuth")
MIB = 1024 * 1024


def split_bf16(table):
    high = table.astype(jnp.bfloat16)
    return high, (table - high.astype(jnp.float32)).astype(jnp.bfloat16)


def split_constant(table):
    table = np.asarray(table, np.float32)
    high = table.astype(jnp.bfloat16)
    return jnp.asarray(high), jnp.asarray((table - high.astype(np.float32)).astype(jnp.bfloat16))


def dot(left, right):
    return jnp.dot(left, right, preferred_element_type=jnp.float32)


def dot3(left, right_high, right_low):
    rows = left.shape[0]
    left_high, left_low = split_bf16(left)
    both = dot(jnp.concatenate([left_high, left_low], axis=0), right_high)
    return both[:rows] + both[rows:] + dot(left_high, right_low)


def swap(blocks, step, before=0, after=0, begin=True, finish=True):
    count = len(blocks)
    axis = len(blocks[0].shape) - 1

    def turn(block, fields, lanes, wanted):
        amount = (fields * step * wanted + lanes) % LANES
        return block if isinstance(amount, int) and amount == 0 else pltpu.roll(block, amount, axis)

    place = lax.broadcasted_iota(jnp.int32, blocks[0].shape, axis) // step
    turned = [turn(blocks[-index % count], -index % count, before, begin) for index in range(count)]
    shift = 1
    while shift < count:
        take = (place & shift) != 0
        turned = [
            jnp.where(take, turned[(index - shift) % count], turned[index]) for index in range(count)
        ]
        shift *= 2
    return [turn(block, -index, after, finish) for index, block in enumerate(turned)]


def own_index(azimuth_count):
    return lax.axis_index("polar") * azimuth_count + lax.axis_index("azimuth")


QUAD = 4
FIELD = LANES // QUAD


def gelu(values):
    return 0.5 * values * (1.0 + lax.erf(values * math.sqrt(0.5)))


def scatter_kernel(field, real, imag, sent, own_filter, buf, sems, filter_sems):
    devices, rows, channels = sent.shape
    copies = []
    for row in range(rows // 8):
        copy = pltpu.make_async_copy(
            field.at[0, :, pl.ds(8 * row, 8), :], buf.at[row], sems.at[row]
        )
        copy.start()
        copies.append(copy)
    degrees = own_filter.shape[1]
    start = lax.axis_index("polar") * degrees
    size = channels // 2
    filter_copies = [
        pltpu.make_async_copy(
            part.at[pl.ds(start, degrees), pl.ds(piece * size, size)],
            own_filter.at[index, :, pl.ds(piece * size, size)],
            filter_sems.at[index, piece],
        )
        for index, part in enumerate((real, imag))
        for piece in range(2)
    ]
    for copy in filter_copies:
        copy.start()
    for row, copy in enumerate(copies):
        copy.wait()
        for tile in range(channels // LANES):
            lanes = pl.ds(tile * LANES, LANES)
            blocks = swap([buf[row, lat, :, lanes] for lat in range(devices)], 1, finish=False)
            for device in range(devices):
                sent[device, pl.ds(8 * row, 8), lanes] = blocks[device]
    for copy in filter_copies:
        copy.wait()


def analysis_kernel(
    polar_count, got, four_high, four_low, leg_high, leg_low, coef, sent, rows
):
    devices, lon_cols, width = got.shape
    azimuth_count = devices // polar_count
    modes = four_high.shape[0]
    orders = modes // 2
    four = jnp.concatenate([four_high[...], four_low[...]], axis=0)
    tiles = width // LANES
    own_turn = LANES - own_index(azimuth_count)
    block = jnp.concatenate(
        [
            got[pl.ds(polar * azimuth_count, azimuth_count)].reshape(azimuth_count * lon_cols, width)
            for polar in range(polar_count)
        ],
        axis=1,
    )
    block_high, block_low = split_bf16(block)
    both = dot(four, block_high)
    both = both[:modes] + both[modes:] + dot(four[:modes], block_low)
    wide = [both[:, polar * width : (polar + 1) * width] for polar in range(polar_count)]
    for tile in range(tiles):
        spectra = [spectrum[:, tile * LANES : (tile + 1) * LANES] for spectrum in wide]
        for quad, spectrum in enumerate(swap(spectra, FIELD, before=own_turn)):
            rows[pl.ds((tile * polar_count + quad) * modes, modes), :] = spectrum
    count = 2 * tiles * polar_count
    extra = orders - devices
    lane = lax.broadcasted_iota(jnp.int32, (count, LANES), 1)
    for order in range(extra):
        own = [
            rows[pl.ds(row, count, stride=orders), :]
            for row in (order, order + extra, devices + order)
        ]
        values = dot3(jnp.concatenate(own, axis=0), leg_high[order], leg_low[order])
        for part in range(2):
            lanes = slice(part * LANES, (part + 1) * LANES)
            index = order + part * extra
            coef[index] = jnp.where(
                ((lane - index) & (LANES - 1)) < LANES // 2,
                values[part * count : (part + 1) * count, lanes],
                values[2 * count :, lanes],
            )
    pack_by_degree(coef, sent)


def pack_by_degree(coef, sent):
    devices, count, _ = coef.shape
    dense, tail = count * 3 // 4, count // 4
    used = LANES * 3 // 4
    for row in range(0, count, 8):
        blocks = swap([coef[order, pl.ds(row, 8), :] for order in range(devices)], 1, begin=False)
        head = min(max(dense - row, 0), 8)
        for device in range(devices):
            start = device * dense
            if head:
                sent[pl.ds(start + row, head), pl.ds(0, used)] = blocks[device][:head, :used]
            if head < 8:
                skip = max(row - dense, 0)
                for part in range(3):
                    moved = pltpu.roll(blocks[device], used - 32 * part, 1)
                    sent[pl.ds(start + tail * part + skip, 8 - head), pl.ds(used, LANES - used)] = moved[
                        head:, used:
                    ]


def filter_kernel(got, own_filter, sent, turned):
    _, degrees, channels, _ = own_filter.shape
    tiles = channels // LANES
    count = 8 * tiles
    dense, tail = count * 3 // 4, count // 4
    devices = sent.shape[0] // dense
    quarter = lax.broadcasted_iota(jnp.int32, (devices, LANES), 1) // 32
    spectra = []
    for half in range(2):
        parts = []
        for own in range(count // 2):
            row = 2 * own + half
            load = lambda start: got[pl.ds(start, devices, stride=dense), :]
            if row < dense:
                parts.append(load(row))
                continue
            folded = [
                pltpu.roll(load(tail * part + row - dense), 32 * (part + 1), 1) for part in range(3)
            ]
            parts.append(
                jnp.where(quarter == 0, folded[0], jnp.where(quarter == 1, folded[1], folded[2]))
            )
        spectra.append(jnp.concatenate(parts, axis=0).T)
    results = [[None] * 4 for _ in range(2)]
    for degree in range(degrees):
        places = [(32 * degree, 32), (64 + 16 * degree, 16)]
        own = jnp.concatenate(
            [spectra[half][start : start + size] for half in range(2) for start, size in places],
            axis=0,
        )
        parts = [split_bf16(own_filter[part, degree]) for part in range(2)]
        both = dot3(own, *(jnp.concatenate(pair, axis=1) for pair in zip(*parts)))
        by_real, by_imag = both[:, :channels], both[:, channels:]
        size = 48
        outs = (by_real[:size] - by_imag[size:], by_real[size:] + by_imag[:size])
        for half in range(2):
            results[half][degree] = outs[half][:32]
            results[half][2 + degree] = outs[half][32:]
    across = []
    for half in range(2):
        padding = jnp.zeros((32, channels), jnp.float32)
        across.append(jnp.concatenate(results[half] + [padding], axis=0).T)
    rows = [
        across[row % 2][row // 2 * devices : (row // 2 + 1) * devices] for row in range(count)
    ]
    for row in range(dense):
        part = row // tail
        folded = pltpu.roll(rows[dense + row % tail], 96 - 32 * part, 1)
        turned[pl.ds(row * devices, devices), :] = jnp.where(quarter < 3, rows[row], folded)
    for device in range(devices):
        sent[pl.ds(device * dense, dense), :] = turned[pl.ds(device, dense, stride=devices), :]


def synthesis_kernel(
    polar_count, got, coef, four_high, four_low, leg_high, leg_low, sent, tails, back, modes_buf
):
    devices, count, _ = coef.shape
    dense, tail = count * 3 // 4, count // 4
    azimuth_count = devices // polar_count
    orders = four_high.shape[1] // 2
    extra = orders - devices
    quarter = lax.broadcasted_iota(jnp.int32, (tail, LANES), 1) // 32
    for device in range(devices):
        folded = [
            pltpu.roll(got[pl.ds(device * dense + tail * part, tail), :], 32 * (part + 1), 1)
            for part in range(3)
        ]
        tails[device, pl.ds(8 - tail, tail), :] = jnp.where(
            quarter == 0, folded[0], jnp.where(quarter == 1, folded[1], folded[2])
        )
        tails[device, pl.ds(0, 8 - tail), :] = got[
            pl.ds(device * dense + count - 8, 8 - tail), :
        ]
    for row in range(0, count, 8):
        if row + 8 < count:
            blocks = [got[pl.ds(device * dense + row, 8), :] for device in range(devices)]
        else:
            blocks = [tails[device] for device in range(devices)]
        blocks = swap(blocks, 1, finish=False)
        for order in range(devices):
            back[order, pl.ds(row, 8), :] = blocks[order]
    keep = (lax.broadcasted_iota(jnp.int32, (count, LANES), 1) & 16) == 0
    for order in range(devices):
        both = jnp.concatenate([coef[order], back[order]], axis=0)
        values = dot3(both, leg_high[order], leg_low[order])
        merged = [
            jnp.where(
                keep,
                values[:count, part * LANES : (part + 1) * LANES],
                values[count:, part * LANES : (part + 1) * LANES],
            )
            for part in range(2)
        ]
        modes_buf[pl.ds(order * count, count), :] = merged[0]
        later = devices + order % extra
        if order < extra:
            modes_buf[pl.ds(later * count, count), :] = merged[1]
        else:
            modes_buf[pl.ds(later * count, count), :] += merged[1]
    four = jnp.concatenate([four_high[...], four_low[...]], axis=0)
    points = four_high.shape[0]
    half = points // 2
    keep = (lax.broadcasted_iota(jnp.int32, (half, LANES), 1) & 16) == 0
    for tile in range(count // 8):
        modes = jnp.concatenate(
            [
                jnp.concatenate(
                    [
                        modes_buf[pl.ds(2 * (QUAD * tile + quad) + part, orders, stride=count), :]
                        for part in range(2)
                    ],
                    axis=0,
                )
                for quad in range(QUAD)
            ],
            axis=1,
        )
        modes_high, modes_low = split_bf16(modes)
        both = dot(four, modes_high)
        values = both[:points] + both[points:] + dot(four[:points], modes_low)
        states = []
        for quad in range(QUAD):
            lanes = slice(quad * LANES, (quad + 1) * LANES)
            first, second = values[:half, lanes], values[half:, lanes]
            skip = jnp.where(keep, first, pltpu.roll(second, 16, 1))
            branch = jnp.where(keep, pltpu.roll(first, LANES - 16, 1), second)
            states.append(gelu(branch) + skip)
        for polar, state in enumerate(swap(states, FIELD, after=own_index(azimuth_count))):
            for azimuth in range(azimuth_count):
                device = polar * azimuth_count + azimuth
                sent[pl.ds(device * dense + tail * tile, tail), :] = state[
                    tail * azimuth : tail * (azimuth + 1)
                ]


def mlp_kernel(got, gain, w_in, w_out, mixed, state, result, sems):
    tiles = state.shape[0]
    _, lon_cols, lat_rows, _ = mixed.shape
    part = lon_cols // 2
    devices = got.shape[0] // (tiles * part)
    for tile in range(tiles):
        blocks = swap(
            [
                got[pl.ds((device * tiles + tile) * part, part), :]
                for device in range(devices)
            ],
            1,
            begin=False,
        )
        for device in range(devices):
            state[tile, pl.ds(part * device, part), :] = blocks[device]
    value = jnp.concatenate([state[tile] for tile in range(tiles)], axis=1)
    center = jnp.mean(value, axis=-1, keepdims=True)
    spread = jnp.mean((value - center) ** 2, axis=-1, keepdims=True)
    normed = (value - center) * lax.rsqrt(spread + 1e-05) * gain[...][None, :]
    hidden = gelu(dot(normed.astype(jnp.bfloat16), w_in[...])).astype(jnp.bfloat16)
    copies = []
    for tile in range(tiles):
        lanes = pl.ds(tile * LANES, LANES)
        state[tile] = value[:, tile * LANES : (tile + 1) * LANES] + dot(hidden, w_out[:, lanes])
        for lon in range(lon_cols):
            first = lon // part * part * lat_rows + lon % part
            result[lon, :, lanes] = state[tile, pl.ds(first, lat_rows, stride=part), :]
        copies.append(
            pltpu.make_async_copy(result.at[:, :, lanes], mixed.at[0, :, :, lanes], sems.at[tile])
        )
        copies[-1].start()
    for copy in copies:
        copy.wait()


def joint_fits(field, filter_real, polar_count, azimuth_count):
    samples, lat_rows, lon_cols, channels = field.shape
    devices = polar_count * azimuth_count
    orders = lon_cols * azimuth_count // 4
    return (
        samples == 1
        and devices == 32
        and polar_count == 4
        and lat_rows == 32
        and lon_cols == 24
        and channels == 3 * LANES
        and filter_real.shape[0] == 2 * polar_count
        and 2 * orders == 3 * devices
    )


def jointly(field, filter_real, filter_imag, norm_gain, w_in, w_out):
    _, lat_rows, lon_cols, channels = field.shape
    polar_count = lax.axis_size("polar")
    azimuth_count = lax.axis_size("azimuth")
    devices = polar_count * azimuth_count
    fine_lat, fine_lon = lat_rows * polar_count, lon_cols * azimuth_count
    coarse_lat, coarse_lon = fine_lat // 2, fine_lon // 2
    orders = coarse_lon // 2
    extra = orders - devices
    count = 2 * channels // devices
    degrees_here = coarse_lat // devices
    lat_out, lon_out = coarse_lat // polar_count, coarse_lon // azimuth_count

    mode_ids = np.tile(np.arange(orders), 2)
    halves = np.repeat(np.arange(2), orders)
    forward = fourier_table(fine_lon, mode_ids, halves, np.ones(2 * orders)).T
    twofold = np.where(mode_ids == 0, 1.0, 2.0)
    inverse = fourier_table(coarse_lon, mode_ids, halves, twofold)
    backward = inverse.reshape(azimuth_count, 2, lon_out // 2, 2 * orders)
    backward = backward.transpose(1, 0, 2, 3).reshape(-1, 2 * orders)

    fine_nodes = colatitudes(fine_lat)
    quadrature = math.pi / fine_lat * np.sin(fine_nodes) * (2.0 * math.pi / fine_lon)
    fine = legendre(fine_nodes, coarse_lat, orders) * quadrature
    coarse = legendre(colatitudes(coarse_lat), coarse_lat, orders)
    owner = np.arange(devices)
    degree = (
        owner % azimuth_count * (coarse_lat // azimuth_count) + owner // azimuth_count * degrees_here
    )
    degree = (degree[None, :] + np.arange(degrees_here)[:, None]).reshape(-1)
    lane = np.arange(LANES)
    lat_fine = lane
    lat_coarse = lane // 32 * lat_out + lane % 16
    fine = fine[:, degree][:, :, lat_fine].transpose(0, 2, 1)
    coarse = coarse[:, degree][:, :, lat_coarse]
    analyse = np.zeros((extra, LANES, 2, 4, devices))
    synthesise = np.zeros((devices, 4, devices, 2, LANES))
    for order in range(devices):
        later, which = devices + order % extra, order // extra
        own = slice(which * devices, (which + 1) * devices)
        analyse[order % extra, :, which, :2] = fine[order].reshape(LANES, 2, devices)
        analyse[order % extra, :, which, 2] = fine[later][:, own]
        synthesise[order, :2, :, 0] = coarse[order].reshape(2, devices, LANES)
        synthesise[order, 2, :, 1] = coarse[later][own]
    analyse = analyse.reshape(extra, LANES, 2 * LANES)
    synthesise = synthesise.reshape(devices, LANES, 2 * LANES)
    for order in range(devices):
        columns = slice(order // extra * LANES, (order // extra + 1) * LANES)
        analyse[order % extra, :, columns] = np.roll(analyse[order % extra, :, columns], order, axis=1)
        synthesise[order] = np.roll(synthesise[order], order, axis=0)

    vmem = pl.BlockSpec(memory_space=pltpu.VMEM)
    hbm = pl.BlockSpec(memory_space=pltpu.HBM)
    dense = count * 3 // 4
    block = pltpu.VMEM((devices * dense, LANES), jnp.float32)

    def exchange(blocks):
        split = blocks.reshape((devices, -1, 2, LANES)) if blocks.ndim == 2 else blocks
        moved = lax.all_to_all(split, BOTH, split_axis=0, concat_axis=0, tiled=True)
        return moved.reshape(blocks.shape)

    def near(*arrays):
        return [pltpu.with_memory_space_constraint(array, pltpu.VMEM) for array in arrays]

    def far(*arrays):
        return [pltpu.with_memory_space_constraint(array, pltpu.HBM) for array in arrays]

    parts = lon_cols // 8
    sent, own_filter = pl.pallas_call(
        scatter_kernel,
        in_specs=[hbm] * 3,
        out_specs=[vmem] * 2,
        out_shape=[
            pltpu.VMEM((devices, lon_cols, channels), jnp.float32),
            pltpu.VMEM((2, degrees_here, channels, channels), jnp.float32),
        ],
        scratch_shapes=[
            pltpu.VMEM((parts, lat_rows, 8, channels), jnp.float32),
            pltpu.SemaphoreType.DMA((parts,)),
            pltpu.SemaphoreType.DMA((2, 2)),
        ],
        compiler_params=pltpu.CompilerParams(vmem_limit_bytes=8 * MIB),
        name="scatter_channels",
    )(*far(field, filter_real, filter_imag))
    got = exchange(sent)
    coef, sent = pl.pallas_call(
        functools.partial(analysis_kernel, polar_count),
        in_specs=[vmem] * 5,
        out_specs=[vmem] * 2,
        out_shape=[pltpu.VMEM((devices, count, LANES), jnp.float32), block],
        scratch_shapes=[pltpu.VMEM((count * orders, LANES), jnp.float32)],
        compiler_params=pltpu.CompilerParams(vmem_limit_bytes=8 * MIB),
        name="analysis",
    )(*near(got, *split_constant(forward), *split_constant(analyse)))
    got = exchange(sent)
    sent = pl.pallas_call(
        filter_kernel,
        in_specs=[vmem] * 2,
        out_specs=vmem,
        out_shape=block,
        scratch_shapes=[pltpu.VMEM((devices * count, LANES), jnp.float32)],
        compiler_params=pltpu.CompilerParams(vmem_limit_bytes=8 * MIB),
        name="channel_filter",
    )(*near(got, own_filter))
    got = exchange(sent)
    sent = pl.pallas_call(
        functools.partial(synthesis_kernel, polar_count),
        in_specs=[vmem] * 6,
        out_specs=vmem,
        out_shape=block,
        scratch_shapes=[
            pltpu.VMEM((devices, 8, LANES), jnp.float32),
            pltpu.VMEM((devices, count, LANES), jnp.float32),
            pltpu.VMEM((orders * count, LANES), jnp.float32),
        ],
        compiler_params=pltpu.CompilerParams(vmem_limit_bytes=8 * MIB),
        name="synthesis",
    )(*near(got, coef, *split_constant(backward), *split_constant(synthesise)))
    got = exchange(sent)
    mixed = pl.pallas_call(
        mlp_kernel,
        in_specs=[vmem] * 4,
        out_specs=pl.BlockSpec(memory_space=pl.ANY),
        out_shape=jax.ShapeDtypeStruct((1, lon_out, lat_out, channels), jnp.float32),
        scratch_shapes=[
            pltpu.VMEM((channels // LANES, lat_out * lon_out, LANES), jnp.float32),
            pltpu.VMEM((lon_out, lat_out, channels), jnp.float32),
            pltpu.SemaphoreType.DMA((channels // LANES,)),
        ],
        compiler_params=pltpu.CompilerParams(vmem_limit_bytes=8 * MIB),
        name="mlp",
    )(*near(got, norm_gain, w_in, w_out))
    return mixed.transpose(0, 2, 1, 3)


def per_device(field, filter_real, filter_imag, norm_gain, w_in, w_out):
    polar_count, azimuth_count = lax.axis_size("polar"), lax.axis_size("azimuth")
    plan = jointly if joint_fits(field, filter_real, polar_count, azimuth_count) else by_axes
    return plan(field, filter_real, filter_imag, norm_gain, w_in, w_out)


def solution(mesh):
    in_specs = (
        P(None, "polar", "azimuth", None),
        P("azimuth", None, None),
        P("azimuth", None, None),
        P(),
        P(),
        P(),
    )
    out_specs = P(None, "polar", "azimuth", None)
    return jax.shard_map(
        per_device, mesh=mesh, in_specs=in_specs, out_specs=out_specs, check_vma=False
    )
```
